128 devices in a mesh: gx: 16 (over y, x), gy: 8 (over z, core).
Axes of the slice: x: 4, y: 4, z: 4, core: 2. Of those that a mesh axis runs over, the one named last changes fastest.
Arguments:
- orbitals: float32 [32, 128, 128, 128], P(None, 'gx', 'gy'), may hold values from -50 to 50
- potential: float32 [128, 128, 128], P('gx', 'gy'), may hold values from -1 to 1
Outputs:
- orthonormal: float32 [32, 128, 128, 128], P(None, 'gx', 'gy')
The draws below stay inside these ranges and needn't reach their ends.
All inputs are finite; a program needn't handle non-finite values.
Results may differ from the reference program's by a relative error of at most 0.00022.
Values sent between devices are 32-bit elements; how exact they have to be, the bound alone decides.
No kernel may reach another device: no remote copies, remote signals or barrier semaphores. Data moves between devices by JAX's collectives and lax.ppermute only.
A program may use at most 256 MiB of HBM per device.

```python
import math
import jax
import jax.numpy as jnp
from jax import lax

NORB = 32
DEG = 4
CX = 8
CY = 16
CZ = 128
NX = 128
NY = 128


def draw_orbitals(key, part):
    key = jax.random.fold_in(key, 11)
    key_scale = jax.random.fold_in(key, 0)
    key_base = jax.random.fold_in(key, 1)
    key_envelope = jax.random.fold_in(key, 3)
    shape = (NORB, NX, NY, CZ)
    scales = jnp.exp(jax.random.uniform(key_scale, (NORB, 1, 1, 1), jnp.float32) * math.log(4.0))
    amplitudes = jnp.exp(jax.random.uniform(key_envelope, (NORB, NX // CX, NY // CY), jnp.float32, -1.0, 1.0))
    envelope = jnp.repeat(jnp.repeat(amplitudes, CX, axis=1), CY, axis=2)[..., None]
    values = scales * envelope * jax.random.normal(key_base, shape, jnp.float32)
    return jnp.clip(values, -50.0, 50.0)


def block_scale(key, extent, cuts, least, high):
    loudness = 1.0
    for axis_at, shards_of in cuts:
        draws = jax.random.uniform(jax.random.fold_in(jax.random.fold_in(key, 6), axis_at), (shards_of,), jnp.float32, least / len(cuts), high / len(cuts))
        loudness = loudness * jnp.repeat(jnp.exp(draws), extent[axis_at] // shards_of).reshape((-1,) + (1,) * (len(extent) - 1 - axis_at))
    return loudness


def setup_inputs(seed: int = 0) -> dict:
    key_list = jax.random.split(jax.random.key(seed), 3)
    return {
        "orbitals": draw_orbitals(jax.random.fold_in(key_list[2], 71), 0),
        "potential": jnp.clip(jax.random.uniform(key_list[1], (NX, NY, CZ), jnp.float32, -1.0, 1.0) * block_scale(key_list[1], (NX, NY, CZ), ((0, 16), (1, 8)), -0.4, 0.0), -1.0, 1.0),
    }


center_c = 5.0
half_w = 4.0

def difference(field, axis):
    near = jnp.roll(field, 1, axis) + jnp.roll(field, -1, axis)
    far = jnp.roll(field, 2, axis) + jnp.roll(field, -2, axis)
    return -2.5 * field + 4.0 / 3.0 * near - 1.0 / 12.0 * far

def hamiltonian(field, potential):
    laplace = difference(field, 0) + difference(field, 1) + difference(field, 2)
    return -0.5 * laplace + potential * field

def filter_one(field, potential):
    prev = field
    current = 1.0 / half_w * (hamiltonian(field, potential) - center_c * field)
    for step in range(1, DEG):
        fresh = 2.0 / half_w * (hamiltonian(current, potential) - center_c * current) - prev
        prev = current
        current = fresh
    return current

def reference(orbitals, potential):
    filtered = lax.map(lambda field: filter_one(field, potential), orbitals)
    flat = filtered.reshape(NORB, -1)
    total = jnp.float32(flat.shape[1])
    gram = jnp.dot(flat.astype(jnp.float32), flat.T.astype(jnp.float32), precision=lax.Precision.HIGHEST, preferred_element_type=jnp.float32) / total
    lower = jnp.linalg.cholesky(gram)
    solved = lax.linalg.triangular_solve(lower, flat, left_side=True, lower=True)
    return solved.reshape(orbitals.shape)
```

```python
import functools

import jax
import jax.numpy as jnp
from jax import lax
from jax.experimental import pallas as pl
from jax.experimental.pallas import tpu as pltpu
from jax.sharding import PartitionSpec as P

DEG = 4
HALO = 2 * DEG
CENTER = 5.0
HALF_W = 4.0
NEAR = (2.0 / HALF_W) * -0.5 * (4.0 / 3.0)
FAR = (2.0 / HALF_W) * 0.5 / 12.0
DIAG_SCALE = 2.0 / HALF_W
DIAG_SHIFT = (2.0 / HALF_W) * (3 * 0.5 * 2.5 - CENTER)

SIZES = (11, 9, 7, 5)
AXES = ("gx", "gy")


def shift_perm(axis, step):
    count = lax.axis_size(axis)
    return [(i, (i + step) % count) for i in range(count)]


def both_ways(low_part, high_part, axis):
    return (
        lax.ppermute(high_part, axis, shift_perm(axis, 1)),
        lax.ppermute(low_part, axis, shift_perm(axis, -1)),
    )


def apply_plane(center, minus1, plus1, minus2, plus2, diag):
    up_y = jnp.roll(center, -2, 0)
    up_z = jnp.roll(center, -2, 1)
    near = jnp.roll(center + up_y, 1, 0) + jnp.roll(center + up_z, 1, 1) + (minus1 + plus1)
    far = (jnp.roll(center, 2, 0) + up_y) + (jnp.roll(center, 2, 1) + up_z) + (minus2 + plus2)
    return diag * center + NEAR * near + FAR * far


def filter_kernel(count, lo_ref, mid_ref, hi_ref, yl_ref, yh_ref, diag_ref, out_ref, ext_ref, t1_ref, t2_ref, t3_ref):
    cx = mid_ref.shape[1]
    cy = mid_ref.shape[2]
    total = cx + 2 * HALO

    def one(orbital, _):
        ext_ref[0:HALO, HALO : HALO + cy, :] = lo_ref[orbital]
        ext_ref[HALO : HALO + cx, HALO : HALO + cy, :] = mid_ref[orbital]
        ext_ref[HALO + cx : total, HALO : HALO + cy, :] = hi_ref[orbital]
        ext_ref[2 : total - 2, 0:HALO, :] = yl_ref[orbital]
        ext_ref[2 : total - 2, HALO + cy :, :] = yh_ref[orbital]
        chain = (ext_ref, t1_ref, t2_ref, t3_ref)
        for step in range(DEG):
            source = chain[step]
            start, stop = 2 * (step + 1), total - 2 * (step + 1)
            window = [source[start - 2 + k] for k in range(4)]
            for x in range(start, stop):
                window.append(source[x + 2])
                applied = apply_plane(window[2], window[1], window[3], window[0], window[4], diag_ref[x])
                window.pop(0)
                fresh = 0.5 * applied if step == 0 else applied - chain[step - 1][x]
                if step < DEG - 1:
                    chain[step + 1][x] = fresh
                else:
                    out_ref[orbital, x - HALO] = fresh[HALO : HALO + cy]
        return 0

    lax.fori_loop(0, count, one, 0)


def run_filter(lo, mid, hi, yl, yh, diag, count):
    _, cx, cy, cz = mid.shape
    ext = (cx + 2 * HALO, cy + 2 * HALO, cz)
    return pl.pallas_call(
        functools.partial(filter_kernel, count),
        out_shape=jax.ShapeDtypeStruct((count, cx, cy, cz), jnp.float32),
        in_specs=[pl.BlockSpec(memory_space=pltpu.VMEM)] * 6,
        out_specs=pl.BlockSpec(memory_space=pltpu.VMEM),
        scratch_shapes=[pltpu.VMEM(ext, jnp.float32)] * 4,
        compiler_params=pltpu.CompilerParams(vmem_limit_bytes=24 * 2**20),
        cost_estimate=pl.CostEstimate(
            flops=count * 2_000_000, bytes_accessed=count * 2_000_000, transcendentals=0
        ),
        name="filter_chunk",
    )(lo, mid, hi, yl, yh, diag)


def gram_kernel(offset, *refs):
    chunks, out_ref = refs[:-1], refs[-1]
    own = chunks[-1]
    count, cx, cy, cz = own.shape
    rows = []
    for index, ref in enumerate(chunks):
        for at in range(ref.shape[0]):
            rows.append((ref, at))
    out_ref[...] = jnp.zeros_like(out_ref)
    block = 4
    for a0 in range(0, count, block):
        a_list = list(range(a0, min(a0 + block, count)))
        last = offset + a_list[-1]
        for j0 in range(0, last + 1, block):
            j_list = list(range(j0, min(j0 + block, last + 1)))

            def add(x, accs, a_list=a_list, j_list=j_list):
                left = [own[a, x] for a in a_list]
                right = [rows[j][0][rows[j][1], x] for j in j_list]
                new = []
                at = 0
                for l in left:
                    for r in right:
                        prod = l * r
                        new.append(accs[at] + (prod[:8] + prod[8:]))
                        at += 1
                return tuple(new)

            zero = jnp.zeros((8, cz), jnp.float32)
            accs = lax.fori_loop(0, cx, add, (zero,) * (len(a_list) * len(j_list)), unroll=True)
            at = 0
            for a in a_list:
                for j in j_list:
                    out_ref[a, j : j + 1, :] = jnp.sum(accs[at], axis=0, keepdims=True)
                    at += 1


def run_gram(chunks, offset, norb):
    count, cx, cy, cz = chunks[-1].shape
    return pl.pallas_call(
        functools.partial(gram_kernel, offset),
        out_shape=jax.ShapeDtypeStruct((count, norb, cz), jnp.float32),
        in_specs=[pl.BlockSpec(memory_space=pltpu.VMEM)] * len(chunks),
        out_specs=pl.BlockSpec(memory_space=pltpu.VMEM),
        compiler_params=pltpu.CompilerParams(vmem_limit_bytes=24 * 2**20),
        cost_estimate=pl.CostEstimate(
            flops=count * 500_000, bytes_accessed=count * 500_000, transcendentals=0
        ),
        name="gram_rows",
    )(*chunks)


def pack_kernel(scale, *refs):
    parts, out_ref = refs[:-1], refs[-1]
    rows = []
    for ref in parts:
        for at in range(ref.shape[0]):
            rows.append((ref, at))
    ones = jnp.ones((8, 128), jnp.float32)
    packed = []
    for r in range(8):
        block = jnp.concatenate([rows[8 * q + r][0][rows[8 * q + r][1]] for q in range(4)], axis=0)
        sums = lax.dot_general(
            ones, block, (((1,), (1,)), ((), ())),
            precision=lax.Precision.HIGHEST, preferred_element_type=jnp.float32,
        )
        packed.append(sums[0:1])
    whole = jnp.concatenate(packed, axis=0) * scale
    out_ref[...] = jnp.broadcast_to(whole[None], out_ref.shape)


def run_pack(parts, scale, devices):
    return pl.pallas_call(
        functools.partial(pack_kernel, scale),
        out_shape=jax.ShapeDtypeStruct((devices, 8, 128), jnp.float32),
        in_specs=[pl.BlockSpec(memory_space=pltpu.VMEM)] * len(parts),
        out_specs=pl.BlockSpec(memory_space=pltpu.VMEM),
        compiler_params=pltpu.CompilerParams(vmem_limit_bytes=16 * 2**20),
        name="pack_gram",
    )(*parts)


def inverse_factor(gram):
    norb = gram.shape[0]
    lane = lax.broadcasted_iota(jnp.int32, gram.shape, 1)
    row = lax.broadcasted_iota(jnp.int32, gram.shape, 0)
    work = jnp.where(lane < norb, gram, jnp.where(lane == row + norb, 1.0, 0.0))
    pivots = jnp.ones((norb, 1), jnp.float32)
    row1 = lax.broadcasted_iota(jnp.int32, (norb, 1), 0)
    for k in range(norb):
        pivot_row = work[k : k + 1, :]
        pivot = pivot_row[:, k : k + 1]
        pivots = jnp.where(row1 == k, pivot, pivots)
        if k + 1 < norb:
            scaled = pivot_row / pivot
            factor = jnp.where(row1 > k, work[:, k : k + 1], 0.0)
            work = work - factor * scaled
    return jnp.roll(work, -norb, 1) / jnp.sqrt(pivots)


def solve_kernel(counts, recv_ref, *refs):
    norb = sum(counts)
    chunks, out_ref, table_ref = refs[: len(counts)], refs[-2], refs[-1]

    @pl.when(pl.program_id(0) == 0)
    def _():
        packed = jnp.sum(recv_ref[...], axis=0)
        rows = jnp.concatenate([packed] + [jnp.roll(packed, -norb * q, 1) for q in range(1, 4)], axis=0)
        square = jnp.concatenate([rows] + [jnp.zeros((128 - norb, 128), jnp.float32)], axis=0)
        flipped = square.T[:norb]
        lane = lax.broadcasted_iota(jnp.int32, rows.shape, 1)
        row = lax.broadcasted_iota(jnp.int32, rows.shape, 0)
        inverse = inverse_factor(jnp.where(row >= lane, rows, flipped))
        square = jnp.concatenate([inverse] + [jnp.zeros((128 - norb, 128), jnp.float32)], axis=0)
        columns = square.T[:norb]
        for i in range(norb):
            table_ref[i] = jnp.broadcast_to(columns[:, i : i + 1], (norb, 128))

    x = pl.program_id(0)
    where = []
    for ref, count in zip(chunks, counts):
        for at in range(count):
            where.append((ref, at))
    block = 8
    for i0 in range(0, norb, block):
        accs = [None] * block
        for j in range(i0 + block):
            value = where[j][0][where[j][1], x]
            for a in range(block):
                i = i0 + a
                if j > i:
                    continue
                term = table_ref[i, j : j + 1, :] * value
                accs[a] = term if accs[a] is None else accs[a] + term
        for a in range(block):
            out_ref[i0 + a, 0] = accs[a]


def run_solve(received, chunks):
    counts = tuple(c.shape[0] for c in chunks)
    norb = sum(counts)
    _, cx, cy, cz = chunks[0].shape
    whole = pl.BlockSpec(memory_space=pltpu.VMEM)
    return pl.pallas_call(
        functools.partial(solve_kernel, counts),
        grid=(cx,),
        out_shape=jax.ShapeDtypeStruct((norb, cx, cy, cz), jnp.float32),
        in_specs=[whole] * (1 + len(chunks)),
        out_specs=pl.BlockSpec((norb, 1, cy, cz), lambda x: (0, x, 0, 0)),
        scratch_shapes=[pltpu.VMEM((norb, norb, 128), jnp.float32)],
        compiler_params=pltpu.CompilerParams(vmem_limit_bytes=24 * 2**20),
        name="orthonormalize",
    )(received, *chunks)


def body(orbitals, potential):
    norb, cx, cy, cz = orbitals.shape
    devices = lax.axis_size("gx") * lax.axis_size("gy")
    mids, los, his, yls, yhs = [], [], [], [], []
    offset = 0
    for index, count in enumerate(SIZES):
        mid = orbitals[offset : offset + count]
        if index == 0:
            mid = jnp.concatenate([mid, potential[None]], axis=0)
        if index >= 2:
            mid, los[index - 2] = lax.optimization_barrier((mid, los[index - 2]))
        lo, hi = both_ways(mid, mid, "gx")
        mids.append(mid)
        los.append(lo)
        his.append(hi)
        offset += count
    for lo, mid, hi in zip(los, mids, his):
        low = jnp.concatenate([lo[:, 2:, :HALO], mid[:, :, :HALO], hi[:, :-2, :HALO]], axis=1)
        high = jnp.concatenate([lo[:, 2:, cy - HALO :], mid[:, :, cy - HALO :], hi[:, :-2, cy - HALO :]], axis=1)
        yl, yh = both_ways(low, high, "gy")
        yls.append(yl)
        yhs.append(yh)
    at = SIZES[0]
    inner = jnp.concatenate([los[0][at], mids[0][at], his[0][at]], axis=0)
    pad = ((2, 2), (0, 0), (0, 0))
    pot_ext = jnp.concatenate([jnp.pad(yls[0][at], pad), inner, jnp.pad(yhs[0][at], pad)], axis=1)
    diag = DIAG_SCALE * pot_ext + DIAG_SHIFT
    chunks, grams = [], []
    offset = 0
    for index, count in enumerate(SIZES):
        chunks.append(run_filter(los[index], mids[index], his[index], yls[index], yhs[index], diag, count))
        grams.append(run_gram(chunks, offset, norb))
        offset += count
    scale = 1.0 / float(devices * cx * cy * cz)
    packed = run_pack(grams, scale, devices)
    received = lax.all_to_all(packed, AXES, 0, 0, tiled=True)
    return run_solve(received, chunks)


def solution(mesh):
    placed = (P(None, "gx", "gy", None), P("gx", "gy", None))
    return jax.shard_map(
        body, mesh=mesh, in_specs=placed, out_specs=P(None, "gx", "gy", None), check_vma=False
    )
```

```python
import functools

import jax
import jax.numpy as jnp
from jax import lax
from jax.experimental import pallas as pl
from jax.experimental.pallas import tpu as pltpu
from jax.sharding import PartitionSpec as P

DEG = 4
HALO = 2 * DEG
CENTER = 5.0
HALF_W = 4.0
NEAR = (2.0 / HALF_W) * -0.5 * (4.0 / 3.0)
FAR = (2.0 / HALF_W) * 0.5 / 12.0
DIAG_SCALE = 2.0 / HALF_W
DIAG_SHIFT = (2.0 / HALF_W) * (3 * 0.5 * 2.5 - CENTER)

GROUP = 8
AXES = ("gx", "gy")


def shift_perm(axis, step):
    count = lax.axis_size(axis)
    return [(i, (i + step) % count) for i in range(count)]


def both_ways(low_part, high_part, axis):
    return (
        lax.ppermute(high_part, axis, shift_perm(axis, 1)),
        lax.ppermute(low_part, axis, shift_perm(axis, -1)),
    )


def reach(plane, cx, left):
    outside = max(HALO - plane, plane - (HALO + cx - 1), 0)
    return left - 2 * ((outside + 1) // 2)


def halo_planes(cx, corners_only=False):
    planes = []
    for plane in range(2, cx + 2 * HALO - 2):
        if corners_only and HALO <= plane < HALO + cx:
            continue
        planes.append((plane, reach(plane, cx, HALO)))
    return planes


def split_plane(plane, cx):
    if plane < HALO:
        return 0, plane
    if plane < HALO + cx:
        return 1, plane - HALO
    return 2, plane - HALO - cx


def prep_kernel(groups, pot_ref, orb_ref, out_ref):
    x = pl.program_id(0)
    cx = pl.num_programs(0)
    cy, cz = orb_ref.shape[2:]
    for g in range(groups):
        tiles = jnp.swapaxes(orb_ref[GROUP * g : GROUP * (g + 1), 0], 0, 1)
        out_ref[pl.ds(g * cx * cy + x * cy, cy)] = tiles
    if pot_ref is not None:
        per = cy // 8
        out_ref[pl.ds(groups * cx * cy + x * per, per)] = pot_ref[0].reshape(per, 8, cz)


def prep(orbitals, at, groups, potential=None):
    norb, cx, cy, cz = orbitals.shape
    tiles = groups * cx * cy + (0 if potential is None else cx * cy // 8)
    count = groups * GROUP
    orb_spec = pl.BlockSpec((count, 1, cy, cz), lambda x: (at // count, x, 0, 0))
    if potential is None:
        kernel, specs, operands = functools.partial(prep_kernel, groups, None), [orb_spec], (orbitals,)
    else:
        kernel = functools.partial(prep_kernel, groups)
        specs = [pl.BlockSpec((1, cy, cz), lambda x: (x, 0, 0)), orb_spec]
        operands = (potential, orbitals)
    return pl.pallas_call(
        kernel,
        grid=(cx,),
        out_shape=jax.ShapeDtypeStruct((tiles, 8, cz), jnp.float32),
        in_specs=specs,
        out_specs=pl.BlockSpec((tiles, 8, cz), lambda x: (0, 0, 0)),
        compiler_params=pltpu.CompilerParams(vmem_limit_bytes=8 * 2**20),
        cost_estimate=pl.CostEstimate(flops=0, bytes_accessed=count * 2**17, transcendentals=0),
        name="tiles_of_orbitals",
    )(*operands)


def sides_kernel(groups, cx, cy, with_pot, others, lo_ref, mid_ref, hi_ref, *refs):
    low_ref, high_ref = refs[-2:]
    sources = (lo_ref, mid_ref, hi_ref)
    at = 0
    for g in range(groups):
        for plane, rows in halo_planes(cx, corners_only=not with_pot):
            which, x = split_plane(plane, cx)
            base = g * cx * cy + x * cy
            low_ref[at : at + rows] = sources[which][base : base + rows]
            high_ref[at : at + rows] = sources[which][base + cy - rows : base + cy]
            at += rows
    if with_pot:
        per = cy // 8
        for plane, _ in halo_planes(cx):
            which, x = split_plane(plane, cx)
            base = groups * cx * cy + x * per
            low_ref[at] = sources[which][base]
            high_ref[at] = sources[which][base + per - 1]
            at += 1
        for g in range(others):
            for x in range(cx):
                base = g * cx * cy + x * cy
                low_ref[at : at + HALO] = refs[0][base : base + HALO]
                high_ref[at : at + HALO] = refs[0][base + cy - HALO : base + cy]
                at += HALO


def pack_sides(lo, mid, hi, groups, cx, cy, other=None, others=0):
    with_pot = other is not None
    tiles = groups * sum(rows for _, rows in halo_planes(cx, corners_only=not with_pot))
    if with_pot:
        tiles += len(halo_planes(cx)) + others * cx * HALO
    shape = jax.ShapeDtypeStruct((tiles,) + mid.shape[1:], jnp.float32)
    operands = (lo, mid, hi) + ((other,) if with_pot else ())
    return pl.pallas_call(
        functools.partial(sides_kernel, groups, cx, cy, with_pot, others),
        out_shape=(shape, shape),
        in_specs=[pl.BlockSpec(memory_space=pltpu.VMEM)] * len(operands),
        out_specs=(pl.BlockSpec(memory_space=pltpu.VMEM),) * 2,
        compiler_params=pltpu.CompilerParams(vmem_limit_bytes=16 * 2**20),
        cost_estimate=pl.CostEstimate(flops=0, bytes_accessed=2_000_000, transcendentals=0),
        name="pack_sides",
    )(*operands)


def z_circulant(cz):
    row = lax.broadcasted_iota(jnp.int32, (cz, cz), 0)
    col = lax.broadcasted_iota(jnp.int32, (cz, cz), 1)
    gap = jnp.where(row >= col, row - col, row - col + cz)
    near = (gap == 1) | (gap == cz - 1)
    far = (gap == 2) | (gap == cz - 2)
    return jnp.where(near, -16.0, jnp.where(far, 1.0, 0.0)).astype(jnp.bfloat16)


def z_part(center, matrix):
    flat = center.reshape(-1, center.shape[-1])
    high = flat.astype(jnp.bfloat16)
    rest = flat - high.astype(jnp.float32)
    middle = rest.astype(jnp.bfloat16)
    low = (rest - middle.astype(jnp.float32)).astype(jnp.bfloat16)

    def times(part):
        return jnp.dot(part, matrix, preferred_element_type=jnp.float32)

    return (times(high) + (times(middle) + times(low))).reshape(center.shape)


def four_steps(cx, cy, chain, diag_ref, out_ref):
    total = cx + 2 * HALO
    matrix = z_circulant(out_ref.shape[-1])
    for step in range(DEG):
        source = chain[step]
        left = HALO - 2 * (step + 1)
        for plane in range(total):
            rows = reach(plane, cx, left)
            if rows < 0:
                continue
            first, count = HALO - rows, cy + 2 * rows
            here = slice(first, first + count)
            column = source[plane, first - 2 : first + count + 2]
            center = column[2:-2]
            near = (column[1:-3] + column[3:-1]) + (source[plane - 1, here] + source[plane + 1, here])
            far = (column[:-4] + column[4:]) + (source[plane - 2, here] + source[plane + 2, here])
            applied = diag_ref[plane, here][:, None, :] * center + FAR * ((z_part(center, matrix) + far) - 16.0 * near)
            fresh = 0.5 * applied if step == 0 else applied - chain[step - 1][plane, here]
            if step < DEG - 1:
                chain[step + 1][plane, here] = fresh
            else:
                out_ref[:, plane - HALO] = jnp.swapaxes(fresh, 0, 1)


def fill_blocks(cx, cy, base, sources, ext_ref):
    for x in range(cx):
        for which in range(3):
            ext_ref[which * cx + x, HALO : HALO + cy] = sources[which][pl.ds(base + x * cy, cy)]


def filter_first_kernel(groups, cx, cy, lo_ref, mid_ref, hi_ref, yl_ref, yh_ref, out_ref, diag_ref, ext_ref, *steps):
    group = pl.program_id(0)
    sources = (lo_ref, mid_ref, hi_ref)
    planes = halo_planes(cx)
    side = sum(rows for _, rows in planes)

    @pl.when(group == 0)
    def _():
        per = cy // 8
        cz = out_ref.shape[-1]
        for x in range(cx):
            for which in range(3):
                base = groups * cx * cy + x * per
                block = sources[which][base : base + per].reshape(cy, cz)
                diag_ref[which * cx + x, HALO : HALO + cy] = DIAG_SCALE * block + DIAG_SHIFT
        at = groups * side
        for plane, _ in planes:
            diag_ref[plane, 0:HALO] = DIAG_SCALE * yl_ref[at] + DIAG_SHIFT
            diag_ref[plane, HALO + cy :] = DIAG_SCALE * yh_ref[at] + DIAG_SHIFT
            at += 1

    fill_blocks(cx, cy, group * cx * cy, sources, ext_ref)
    at = 0
    for plane, rows in planes:
        ext_ref[plane, HALO - rows : HALO] = yl_ref[pl.ds(group * side + at, rows)]
        ext_ref[plane, HALO + cy : HALO + cy + rows] = yh_ref[pl.ds(group * side + at, rows)]
        at += rows
    four_steps(cx, cy, (ext_ref,) + steps, diag_ref, out_ref)


def filter_second_kernel(start, cx, cy, lo_ref, mid_ref, hi_ref, yl_ref, yh_ref, cl_ref, ch_ref, diag_ref, out_ref, ext_ref, *steps):
    group = pl.program_id(0)
    fill_blocks(cx, cy, group * cx * cy, (lo_ref, mid_ref, hi_ref), ext_ref)
    for x in range(cx):
        base = start + group * cx * HALO + x * HALO
        ext_ref[HALO + x, 0:HALO] = yl_ref[pl.ds(base, HALO)]
        ext_ref[HALO + x, HALO + cy :] = yh_ref[pl.ds(base, HALO)]
    planes = halo_planes(cx, corners_only=True)
    side = sum(rows for _, rows in planes)
    at = 0
    for plane, rows in planes:
        ext_ref[plane, HALO - rows : HALO] = cl_ref[pl.ds(group * side + at, rows)]
        ext_ref[plane, HALO + cy : HALO + cy + rows] = ch_ref[pl.ds(group * side + at, rows)]
        at += rows
    four_steps(cx, cy, (ext_ref,) + steps, diag_ref, out_ref)


def run_filter(kernel, operands, groups, cx, cy, cz, with_diag):
    ext = (cx + 2 * HALO, cy + 2 * HALO, GROUP, cz)
    out_shape = [jax.ShapeDtypeStruct((groups * GROUP, cx, cy, cz), jnp.float32)]
    out_specs = [pl.BlockSpec((GROUP, cx, cy, cz), lambda g: (g, 0, 0, 0))]
    if with_diag:
        wide = (cx + 2 * HALO, cy + 2 * HALO, cz)
        out_shape.append(jax.ShapeDtypeStruct(wide, jnp.float32))
        out_specs.append(pl.BlockSpec(wide, lambda g: (0, 0, 0)))
    return pl.pallas_call(
        kernel,
        grid=(groups,),
        out_shape=out_shape,
        in_specs=[pl.BlockSpec(memory_space=pltpu.VMEM)] * len(operands),
        out_specs=out_specs,
        scratch_shapes=[pltpu.VMEM(ext, jnp.float32)] * 4,
        compiler_params=pltpu.CompilerParams(vmem_limit_bytes=32 * 2**20),
        cost_estimate=pl.CostEstimate(
            flops=groups * 16_000_000, bytes_accessed=groups * 16_000_000, transcendentals=0
        ),
        name="filter_orbitals",
    )(*operands)


def gram_kernel(offset, *refs):
    chunks, out_ref = refs[:-1], refs[-1]
    own = chunks[-1]
    count, cx, cy, cz = own.shape
    rows = []
    for index, ref in enumerate(chunks):
        for at in range(ref.shape[0]):
            rows.append((ref, at))
    out_ref[...] = jnp.zeros_like(out_ref)
    block = 4
    for a0 in range(0, count, block):
        a_list = list(range(a0, min(a0 + block, count)))
        last = offset + a_list[-1]
        for j0 in range(0, last + 1, block):
            j_list = list(range(j0, min(j0 + block, last + 1)))

            def add(x, accs, a_list=a_list, j_list=j_list):
                left = [own[a, x] for a in a_list]
                right = [rows[j][0][rows[j][1], x] for j in j_list]
                new = []
                at = 0
                for l in left:
                    for r in right:
                        prod = l * r
                        new.append(accs[at] + (prod[:8] + prod[8:]))
                        at += 1
                return tuple(new)

            zero = jnp.zeros((8, cz), jnp.float32)
            accs = lax.fori_loop(0, cx, add, (zero,) * (len(a_list) * len(j_list)), unroll=True)
            at = 0
            for a in a_list:
                for j in j_list:
                    out_ref[a, j : j + 1, :] = jnp.sum(accs[at], axis=0, keepdims=True)
                    at += 1


def run_gram(chunks, offset, norb):
    count, cx, cy, cz = chunks[-1].shape
    return pl.pallas_call(
        functools.partial(gram_kernel, offset),
        out_shape=jax.ShapeDtypeStruct((count, norb, cz), jnp.float32),
        in_specs=[pl.BlockSpec(memory_space=pltpu.VMEM)] * len(chunks),
        out_specs=pl.BlockSpec(memory_space=pltpu.VMEM),
        compiler_params=pltpu.CompilerParams(vmem_limit_bytes=24 * 2**20),
        cost_estimate=pl.CostEstimate(
            flops=count * 500_000, bytes_accessed=count * 500_000, transcendentals=0
        ),
        name="gram_rows",
    )(*chunks)


def pack_kernel(scale, *refs):
    parts, out_ref = refs[:-1], refs[-1]
    rows = []
    for ref in parts:
        for at in range(ref.shape[0]):
            rows.append((ref, at))
    ones = jnp.ones((8, 128), jnp.float32)
    packed = []
    for r in range(8):
        block = jnp.concatenate([rows[8 * q + r][0][rows[8 * q + r][1]] for q in range(4)], axis=0)
        sums = lax.dot_general(
            ones, block, (((1,), (1,)), ((), ())),
            precision=lax.Precision.HIGHEST, preferred_element_type=jnp.float32,
        )
        packed.append(sums[0:1])
    whole = jnp.concatenate(packed, axis=0) * scale
    out_ref[...] = jnp.broadcast_to(whole[None], out_ref.shape)


def run_pack(parts, scale, devices):
    return pl.pallas_call(
        functools.partial(pack_kernel, scale),
        out_shape=jax.ShapeDtypeStruct((devices, 8, 128), jnp.float32),
        in_specs=[pl.BlockSpec(memory_space=pltpu.VMEM)] * len(parts),
        out_specs=pl.BlockSpec(memory_space=pltpu.VMEM),
        compiler_params=pltpu.CompilerParams(vmem_limit_bytes=16 * 2**20),
        name="pack_gram",
    )(*parts)


def inverse_factor(gram):
    norb = gram.shape[0]
    lane = lax.broadcasted_iota(jnp.int32, gram.shape, 1)
    row = lax.broadcasted_iota(jnp.int32, gram.shape, 0)
    work = jnp.where(lane < norb, gram, jnp.where(lane == row + norb, 1.0, 0.0))
    pivots = jnp.ones((norb, 1), jnp.float32)
    row1 = lax.broadcasted_iota(jnp.int32, (norb, 1), 0)
    for k in range(norb):
        pivot_row = work[k : k + 1, :]
        pivot = pivot_row[:, k : k + 1]
        pivots = jnp.where(row1 == k, pivot, pivots)
        if k + 1 < norb:
            scaled = pivot_row / pivot
            factor = jnp.where(row1 > k, work[:, k : k + 1], 0.0)
            work = work - factor * scaled
    return jnp.roll(work, -norb, 1) / jnp.sqrt(pivots)


def solve_kernel(counts, recv_ref, *refs):
    norb = sum(counts)
    chunks, out_ref, table_ref = refs[: len(counts)], refs[-2], refs[-1]

    @pl.when(pl.program_id(0) == 0)
    def _():
        packed = jnp.sum(recv_ref[...], axis=0)
        rows = jnp.concatenate([packed] + [jnp.roll(packed, -norb * q, 1) for q in range(1, 4)], axis=0)
        square = jnp.concatenate([rows] + [jnp.zeros((128 - norb, 128), jnp.float32)], axis=0)
        flipped = square.T[:norb]
        lane = lax.broadcasted_iota(jnp.int32, rows.shape, 1)
        row = lax.broadcasted_iota(jnp.int32, rows.shape, 0)
        inverse = inverse_factor(jnp.where(row >= lane, rows, flipped))
        square = jnp.concatenate([inverse] + [jnp.zeros((128 - norb, 128), jnp.float32)], axis=0)
        columns = square.T[:norb]
        for i in range(norb):
            table_ref[i] = jnp.broadcast_to(columns[:, i : i + 1], (norb, 128))

    x = pl.program_id(0)
    where = []
    for ref, count in zip(chunks, counts):
        for at in range(count):
            where.append((ref, at))
    block = 8
    for i0 in range(0, norb, block):
        accs = [None] * block
        for j in range(i0 + block):
            value = where[j][0][where[j][1], x]
            for a in range(block):
                i = i0 + a
                if j > i:
                    continue
                term = table_ref[i, j : j + 1, :] * value
                accs[a] = term if accs[a] is None else accs[a] + term
        for a in range(block):
            out_ref[i0 + a, 0] = accs[a]


def run_solve(received, chunks):
    counts = tuple(c.shape[0] for c in chunks)
    norb = sum(counts)
    _, cx, cy, cz = chunks[0].shape
    whole = pl.BlockSpec(memory_space=pltpu.VMEM)
    return pl.pallas_call(
        functools.partial(solve_kernel, counts),
        grid=(cx,),
        out_shape=jax.ShapeDtypeStruct((norb, cx, cy, cz), jnp.float32),
        in_specs=[whole] * (1 + len(chunks)),
        out_specs=pl.BlockSpec((norb, 1, cy, cz), lambda x: (0, x, 0, 0)),
        scratch_shapes=[pltpu.VMEM((norb, norb, 128), jnp.float32)],
        compiler_params=pltpu.CompilerParams(vmem_limit_bytes=24 * 2**20),
        name="orthonormalize",
    )(received, *chunks)


def body(orbitals, potential):
    norb, cx, cy, cz = orbitals.shape
    devices = lax.axis_size("gx") * lax.axis_size("gy")
    groups = norb // GROUP // 2
    half = groups * GROUP
    mid_a = prep(orbitals, 0, groups, potential)
    lo_a, hi_a = both_ways(mid_a, mid_a, "gx")
    mid_b = prep(orbitals, half, groups)
    lo_b, hi_b = both_ways(mid_b, mid_b, "gx")
    low, high = pack_sides(lo_a, mid_a, hi_a, groups, cx, cy, mid_b, groups)
    yl_a, yh_a = both_ways(low, high, "gy")
    low, high = pack_sides(lo_b, mid_b, hi_b, groups, cx, cy)
    yl_b, yh_b = both_ways(low, high, "gy")
    filtered_a, diag = run_filter(
        functools.partial(filter_first_kernel, groups, cx, cy),
        (lo_a, mid_a, hi_a, yl_a, yh_a), groups, cx, cy, cz, True,
    )
    gram_a = run_gram([filtered_a], 0, norb)
    planes = halo_planes(cx)
    start = groups * sum(rows for _, rows in planes) + len(planes)
    (filtered_b,) = run_filter(
        functools.partial(filter_second_kernel, start, cx, cy),
        (lo_b, mid_b, hi_b, yl_a, yh_a, yl_b, yh_b, diag), groups, cx, cy, cz, False,
    )
    gram_b = run_gram([filtered_a, filtered_b], half, norb)
    scale = 1.0 / float(devices * cx * cy * cz)
    packed = run_pack([gram_a, gram_b], scale, devices)
    received = lax.all_to_all(packed, AXES, 0, 0, tiled=True)
    return run_solve(received, [filtered_a, filtered_b])


def solution(mesh):
    placed = (P(None, "gx", "gy", None), P("gx", "gy", None))
    return jax.shard_map(
        body, mesh=mesh, in_specs=placed, out_specs=P(None, "gx", "gy", None), check_vma=False
    )
```

```python
import functools
import math

import jax
import jax.numpy as jnp
from jax import lax
from jax.experimental import pallas as pl
from jax.experimental.pallas import tpu as pltpu
from jax.sharding import PartitionSpec as P

DEG = 4
HALO = 2 * DEG
CENTER = 5.0
HALF_W = 4.0
NEAR = (2.0 / HALF_W) * -0.5 * (4.0 / 3.0)
FAR = (2.0 / HALF_W) * 0.5 / 12.0
DIAG_SCALE = 2.0 / HALF_W
DIAG_SHIFT = (2.0 / HALF_W) * (3 * 0.5 * 2.5 - CENTER)

GROUP = 8
PREP_VMEM = 59 * 2**20
CHUNKS = (2, 2)
UNITS = ((0, 0, 1), (0, 1, 1), (1, 0, 1), (1, 1, 1))
AFTER = {2: 1}
RIDES = {}
FILTER_COST = 100
GY = ("gz", "core")
CORES = 2


def axis_count(axis):
    return math.prod(lax.axis_size(a) for a in ((axis,) if isinstance(axis, str) else axis))


def shift_perm(axis, step):
    count = axis_count(axis)
    return [(i, (i + step) % count) for i in range(count)]


def both_ways(low_part, high_part, axis):
    return (
        lax.ppermute(high_part, axis, shift_perm(axis, 1)),
        lax.ppermute(low_part, axis, shift_perm(axis, -1)),
    )


def reach(plane, cx, left):
    outside = max(HALO - plane, plane - (HALO + cx - 1), 0)
    return left - 2 * ((outside + 1) // 2)


def halo_planes(cx, late=False):
    planes = []
    for plane in range(2, cx + 2 * HALO - 2):
        if late and HALO <= plane < HALO + cx:
            continue
        planes.append((plane, reach(plane, cx, HALO)))
    return planes


def split_plane(plane, cx):
    if plane < HALO:
        return 0, plane
    if plane < HALO + cx:
        return 1, plane - HALO
    return 2, plane - HALO - cx


def tile_block(out_ref, at, block):
    out_ref[at : at + block.shape[1]] = jnp.swapaxes(block, 0, 1)


def first_tiles_kernel(groups, pot_ref, orb_ref, out_ref, pot_here, here, pot_sem, sems):
    cx, cy, cz = pot_ref.shape
    pot_copy = pltpu.make_async_copy(pot_ref, pot_here, pot_sem)
    pot_copy.start()
    copies = []
    for g in range(groups):
        part = pl.ds(GROUP * g, GROUP)
        copies.append(pltpu.make_async_copy(orb_ref.at[part], here.at[part], sems.at[g]))
        copies[-1].start()
    for g in range(groups):
        copies[g].wait()
        for x in range(cx):
            tile_block(out_ref, g * cx * cy + x * cy, here[GROUP * g : GROUP * (g + 1), x])
    pot_copy.wait()
    out_ref[groups * cx * cy :] = pot_here[...].reshape(cx * cy // 8, 8, cz)


def first_tiles(orbitals, potential):
    _, cx, cy, cz = orbitals.shape
    groups = CHUNKS[0]
    tiles = groups * cx * cy + cx * cy // 8
    return pl.pallas_call(
        functools.partial(first_tiles_kernel, groups),
        out_shape=jax.ShapeDtypeStruct((tiles, 8, cz), jnp.float32),
        in_specs=[pl.BlockSpec(memory_space=pltpu.HBM)] * 2,
        out_specs=pl.BlockSpec(memory_space=pltpu.VMEM),
        scratch_shapes=[
            pltpu.VMEM((cx, cy, cz), jnp.float32),
            pltpu.VMEM((groups * GROUP, cx, cy, cz), jnp.float32),
            pltpu.SemaphoreType.DMA,
            pltpu.SemaphoreType.DMA((groups,)),
        ],
        compiler_params=pltpu.CompilerParams(vmem_limit_bytes=PREP_VMEM),
        name="first_tiles",
    )(potential, orbitals)


def tiles_kernel(chunks, pot_ref, orb_ref, *out_refs):
    cx, cy, cz = pot_ref.shape
    group = 0
    for out_ref, groups in zip(out_refs, chunks):
        for g in range(groups):
            for x in range(cx):
                tile_block(out_ref, g * cx * cy + x * cy, orb_ref[GROUP * group : GROUP * (group + 1), x])
            group += 1
    out_refs[0][chunks[0] * cx * cy :] = pot_ref[...].reshape(cx * cy // 8, 8, cz)


def all_tiles(orbitals, potential):
    _, cx, cy, cz = orbitals.shape
    tiles = [groups * cx * cy for groups in CHUNKS]
    tiles[0] += cx * cy // 8
    return pl.pallas_call(
        functools.partial(tiles_kernel, CHUNKS),
        out_shape=[jax.ShapeDtypeStruct((t, 8, cz), jnp.float32) for t in tiles],
        in_specs=[pl.BlockSpec(memory_space=pltpu.VMEM)] * 2,
        out_specs=[pl.BlockSpec(memory_space=pltpu.VMEM)] * len(tiles),
        compiler_params=pltpu.CompilerParams(vmem_limit_bytes=16 * 2**20),
        name="all_tiles",
    )(potential, orbitals)


def sides_kernel(unit, chunk_groups, rider, cx, cy, *refs):
    low_ref, high_ref = refs[-2:]
    start, groups, first, late = unit
    at = 0
    for g in range(start, start + groups):
        for plane, rows in halo_planes(cx, late):
            which, x = split_plane(plane, cx)
            base = g * cx * cy + x * cy
            low_ref[at : at + rows] = refs[which][base : base + rows]
            high_ref[at : at + rows] = refs[which][base + cy - rows : base + cy]
            at += rows
    if first:
        per = cy // 8
        for plane, _ in halo_planes(cx):
            which, x = split_plane(plane, cx)
            base = chunk_groups * cx * cy + x * per
            low_ref[at] = refs[which][base]
            high_ref[at] = refs[which][base + per - 1]
            at += 1
    if rider is not None:
        for g in range(rider[0], rider[0] + rider[1]):
            for x in range(cx):
                base = g * cx * cy + x * cy
                low_ref[at : at + HALO] = refs[3][base : base + HALO]
                high_ref[at : at + HALO] = refs[3][base + cy - HALO : base + cy]
                at += HALO


def unit_tiles(cx, unit):
    _, groups, first, late = unit
    return groups * sum(rows for _, rows in halo_planes(cx, late)) + (len(halo_planes(cx)) if first else 0)


def pack_sides(blocks, unit, chunk_groups, cx, cy, rider, rider_mid):
    tiles = unit_tiles(cx, unit) + (0 if rider is None else rider[1] * cx * HALO)
    shape = jax.ShapeDtypeStruct((tiles,) + blocks[0].shape[1:], jnp.float32)
    operands = blocks + (() if rider is None else (rider_mid,))
    return pl.pallas_call(
        functools.partial(sides_kernel, unit, chunk_groups, rider, cx, cy),
        out_shape=(shape, shape),
        in_specs=[pl.BlockSpec(memory_space=pltpu.VMEM)] * len(operands),
        out_specs=(pl.BlockSpec(memory_space=pltpu.VMEM),) * 2,
        compiler_params=pltpu.CompilerParams(vmem_limit_bytes=16 * 2**20),
        cost_estimate=pl.CostEstimate(flops=0, bytes_accessed=1_000_000, transcendentals=0),
        name="pack_sides",
    )(*operands)


def z_circulant(cz):
    row = lax.broadcasted_iota(jnp.int32, (cz, cz), 0)
    col = lax.broadcasted_iota(jnp.int32, (cz, cz), 1)
    gap = jnp.where(row >= col, row - col, row - col + cz)
    near = (gap == 1) | (gap == cz - 1)
    far = (gap == 2) | (gap == cz - 2)
    return jnp.where(near, -16.0, jnp.where(far, 1.0, 0.0)).astype(jnp.bfloat16)


def z_part(center, matrix):
    flat = center.reshape(-1, center.shape[-1])
    high = flat.astype(jnp.bfloat16)
    rest = flat - high.astype(jnp.float32)
    middle = rest.astype(jnp.bfloat16)
    low = (rest - middle.astype(jnp.float32)).astype(jnp.bfloat16)

    def times(part):
        return jnp.dot(part, matrix, preferred_element_type=jnp.float32)

    return (times(high) + (times(middle) + times(low))).reshape(center.shape)


def four_steps(cx, cy, chain, diag_ref, out_ref):
    total = cx + 2 * HALO
    matrix = z_circulant(out_ref.shape[-1])
    for step in range(DEG):
        source = chain[step]
        left = HALO - 2 * (step + 1)
        for plane in range(total):
            rows = reach(plane, cx, left)
            if rows < 0:
                continue
            first, count = HALO - rows, cy + 2 * rows
            here = slice(first, first + count)
            column = source[plane, first - 2 : first + count + 2]
            center = column[2:-2]
            near = (column[1:-3] + column[3:-1]) + (source[plane - 1, here] + source[plane + 1, here])
            far = (column[:-4] + column[4:]) + (source[plane - 2, here] + source[plane + 2, here])
            applied = diag_ref[plane, here][:, None, :] * center + FAR * ((z_part(center, matrix) + far) - 16.0 * near)
            fresh = 0.5 * applied if step == 0 else applied - chain[step - 1][plane, here]
            if step < DEG - 1:
                chain[step + 1][plane, here] = fresh
            else:
                out_ref[:, plane - HALO] = jnp.swapaxes(fresh, 0, 1)


def fill_blocks(cx, cy, base, sources, ext_ref):
    for x in range(cx):
        for which in range(3):
            ext_ref[which * cx + x, HALO : HALO + cy] = sources[which][pl.ds(base + x * cy, cy)]


def filter_kernel(unit, chunk_groups, own_at, cx, cy, lo_ref, mid_ref, hi_ref, yl_ref, yh_ref, *refs):
    start, groups, first, late = unit
    group = pl.program_id(0)
    sources = (lo_ref, mid_ref, hi_ref)
    planes = halo_planes(cx, late)
    side = sum(rows for _, rows in planes)
    if first:
        out_ref, diag_ref = refs[:2]

        @pl.when(group == 0)
        def _():
            per = cy // 8
            cz = out_ref.shape[-1]
            for x in range(cx):
                for which in range(3):
                    base = chunk_groups * cx * cy + x * per
                    block = sources[which][base : base + per].reshape(cy, cz)
                    diag_ref[which * cx + x, HALO : HALO + cy] = DIAG_SCALE * block + DIAG_SHIFT
            at = groups * side
            for plane, _ in planes:
                diag_ref[plane, 0:HALO] = DIAG_SCALE * yl_ref[at] + DIAG_SHIFT
                diag_ref[plane, HALO + cy :] = DIAG_SCALE * yh_ref[at] + DIAG_SHIFT
                at += 1
    else:
        diag_ref, out_ref = refs[-6:-4]
    chain = refs[-4:]
    if late:
        for x in range(cx):
            base = own_at + group * cx * HALO + x * HALO
            chain[0][HALO + x, 0:HALO] = refs[0][pl.ds(base, HALO)]
            chain[0][HALO + x, HALO + cy :] = refs[1][pl.ds(base, HALO)]
    for x in range(cx):
        for which in range(3):
            tiles = sources[which][pl.ds((start + group) * cx * cy + x * cy, cy)]
            chain[0][which * cx + x, HALO : HALO + cy] = tiles
    at = 0
    for plane, rows in planes:
        chain[0][plane, HALO - rows : HALO] = yl_ref[pl.ds(group * side + at, rows)]
        chain[0][plane, HALO + cy : HALO + cy + rows] = yh_ref[pl.ds(group * side + at, rows)]
        at += rows
    four_steps(cx, cy, chain, diag_ref, out_ref)


def run_filter(blocks, sides, unit, chunk_groups, own, own_at, cx, cy, cz, diag):
    _, groups, first, late = unit
    ext = (cx + 2 * HALO, cy + 2 * HALO, GROUP, cz)
    out_shape = [jax.ShapeDtypeStruct((groups * GROUP, cx, cy, cz), jnp.float32)]
    out_specs = [pl.BlockSpec((GROUP, cx, cy, cz), lambda g: (g, 0, 0, 0))]
    operands = blocks + sides + (own if late else ())
    if first:
        wide = (cx + 2 * HALO, cy + 2 * HALO, cz)
        out_shape.append(jax.ShapeDtypeStruct(wide, jnp.float32))
        out_specs.append(pl.BlockSpec(wide, lambda g: (0, 0, 0)))
    else:
        operands = operands + (diag,)
    got = pl.pallas_call(
        functools.partial(filter_kernel, unit, chunk_groups, own_at, cx, cy),
        grid=(groups,),
        out_shape=out_shape,
        in_specs=[pl.BlockSpec(memory_space=pltpu.VMEM)] * len(operands),
        out_specs=out_specs,
        scratch_shapes=[pltpu.VMEM(ext, jnp.float32)] * 4,
        compiler_params=pltpu.CompilerParams(vmem_limit_bytes=32 * 2**20),
        cost_estimate=pl.CostEstimate(flops=0, bytes_accessed=groups * FILTER_COST, transcendentals=0),
        name="filter_orbitals",
    )(*operands)
    return got if first else (got[0], diag)


def gram_kernel(offset, scale, counts, *refs):
    chunks, earlier, out_ref, rows_ref = refs[: len(counts)], refs[len(counts) : -2], refs[-2], refs[-1]
    own = chunks[-1]
    count, cx, cy, cz = own.shape
    norb = rows_ref.shape[1]
    rows = []
    for ref, size in zip(chunks, counts):
        for at in range(size):
            rows.append((ref, at))
    rows_ref[...] = jnp.zeros_like(rows_ref)
    block = 4
    for a0 in range(0, count, block):
        a_list = list(range(a0, min(a0 + block, count)))
        last = offset + a_list[-1]
        for j0 in range(0, last + 1, block):
            j_list = list(range(j0, min(j0 + block, last + 1)))
            accs = [None] * (len(a_list) * len(j_list))
            for x in range(cx):
                left = [own[a, x] for a in a_list]
                right = [rows[j][0][rows[j][1], x] for j in j_list]
                at = 0
                for l in left:
                    for r in right:
                        prod = l * r
                        prod = prod[:8] + prod[8:]
                        accs[at] = prod if accs[at] is None else accs[at] + prod
                        at += 1
            at = 0
            for a in a_list:
                for j in j_list:
                    rows_ref[a, j : j + 1, :] = jnp.sum(accs[at], axis=0, keepdims=True)
                    at += 1
    sums = lax.dot_general(
        jnp.ones((8, cz), jnp.float32), rows_ref[...].reshape(count * norb, cz), (((1,), (1,)), ((), ())),
        precision=lax.Precision.HIGHEST, preferred_element_type=jnp.float32,
    )
    lane = lax.broadcasted_iota(jnp.int32, (8, 128), 1)
    row = lax.broadcasted_iota(jnp.int32, (8, 128), 0)
    per = 128 // norb
    packed = jnp.zeros((8, 128), jnp.float32)
    for a in range(count):
        here, slot = a // per, (offset + a) // 8
        value = pltpu.roll(sums[:, 128 * here : 128 * (here + 1)], (norb * (slot - a % per)) % 128, 1)
        mask = (row == (offset + a) % 8) & (lane >= norb * slot) & (lane < norb * (slot + 1))
        packed = packed + jnp.where(mask, value, 0.0)
    packed = packed * scale
    for ref in earlier:
        packed = packed + ref[...]
    out_ref[...] = packed


def run_gram(chunks, earlier, offset, norb, scale):
    count, cx, cy, cz = chunks[-1].shape
    counts = tuple(c.shape[0] for c in chunks)
    operands = tuple(chunks) + tuple(earlier)
    return pl.pallas_call(
        functools.partial(gram_kernel, offset, scale, counts),
        out_shape=jax.ShapeDtypeStruct((8, 128), jnp.float32),
        in_specs=[pl.BlockSpec(memory_space=pltpu.VMEM)] * len(operands),
        out_specs=pl.BlockSpec(memory_space=pltpu.VMEM),
        scratch_shapes=[pltpu.VMEM((count, norb, cz), jnp.float32)],
        compiler_params=pltpu.CompilerParams(vmem_limit_bytes=24 * 2**20),
        cost_estimate=pl.CostEstimate(flops=0, bytes_accessed=100, transcendentals=0),
        name="gram_rows",
    )(*operands)


def factor_table(gram, table_ref):
    norb = gram.shape[0]
    columns = [jnp.broadcast_to(gram[:, j : j + 1], (norb, 128)) for j in range(norb)]
    row = lax.broadcasted_iota(jnp.int32, (norb, 128), 0)
    for k in range(norb):
        scale = 1.0 / jnp.sqrt(columns[k][k : k + 1])
        column = columns[k] * scale
        table_ref[k] = jnp.where(row == k, scale, column)
        for j in range(k + 1, norb):
            top = 8 * (j // 8)
            fresh = columns[j][top:] - column[top:] * column[j : j + 1]
            columns[j] = fresh if top == 0 else jnp.concatenate([jnp.zeros((top, 128), jnp.float32), fresh], axis=0)


def solve_kernel(counts, recv_ref, *refs):
    norb = sum(counts)
    chunks, (out_ref, here_ref, table_ref, sems) = refs[: len(counts)], refs[len(counts) :]
    packed = jnp.sum(recv_ref[...], axis=0)
    rows = jnp.concatenate([packed] + [jnp.roll(packed, -norb * q, 1) for q in range(1, 4)], axis=0)
    factor_table(rows, table_ref)
    where = []
    for ref, count in zip(chunks, counts):
        for at in range(count):
            where.append((ref, at))
    block = 8
    cx = here_ref.shape[1]

    def copy_out(x):
        return pltpu.make_async_copy(here_ref.at[:, x], out_ref.at[:, x], sems.at[x])

    def layer(x, _):
        for i0 in range(0, norb, block):
            accs = [where[i0 + a][0][where[i0 + a][1], x] for a in range(block)]
            for j in range(i0):
                value = here_ref[j, x]
                for a in range(block):
                    accs[a] = accs[a] - table_ref[j, i0 + a : i0 + a + 1, :] * value
            for a in range(block):
                value = accs[a] * table_ref[i0 + a, i0 + a : i0 + a + 1, :]
                here_ref[i0 + a, x] = value
                for c in range(a + 1, block):
                    accs[c] = accs[c] - table_ref[i0 + a, i0 + c : i0 + c + 1, :] * value
        copy_out(x).start()
        return 0

    lax.fori_loop(0, cx, layer, 0)
    for x in range(cx):
        copy_out(x).wait()


def run_solve(received, chunks):
    counts = tuple(c.shape[0] for c in chunks)
    norb = sum(counts)
    _, cx, cy, cz = chunks[0].shape
    return pl.pallas_call(
        functools.partial(solve_kernel, counts),
        out_shape=jax.ShapeDtypeStruct((norb, cx, cy, cz), jnp.float32),
        in_specs=[pl.BlockSpec(memory_space=pltpu.VMEM)] * (1 + len(chunks)),
        out_specs=pl.BlockSpec(memory_space=pl.ANY),
        scratch_shapes=[
            pltpu.VMEM((norb, cx, cy, cz), jnp.float32),
            pltpu.VMEM((norb, norb, 128), jnp.float32),
            pltpu.SemaphoreType.DMA((cx,)),
        ],
        compiler_params=pltpu.CompilerParams(vmem_limit_bytes=24 * 2**20),
        name="orthonormalize",
    )(received, *chunks)


def body(orbitals, potential):
    norb, cx, cy, cz = orbitals.shape
    chips = axis_count(("gx", "gz"))
    scale = 1.0 / float(chips * CORES * cx * cy * cz)
    blocks = []
    first = first_tiles(orbitals, potential)
    for index, mid in enumerate(all_tiles(orbitals, potential)):
        lo, hi = both_ways(*((first, first) if index == 0 else (mid, mid)), "gx")
        blocks.append((lo, mid, hi))
    diag = None
    filtered, grams, all_sides = [], [], []
    for index, (chunk, start, groups) in enumerate(UNITS):
        unit = (start, groups, index == 0, index in RIDES)
        if index in AFTER:
            lo, mid, hi = blocks[chunk]
            lo, hi, filtered[AFTER[index]] = lax.optimization_barrier((lo, hi, filtered[AFTER[index]]))
            blocks[chunk] = lo, mid, hi
        rider, rider_mid = None, None
        for later, carrier in RIDES.items():
            if carrier == index:
                rider, rider_mid = UNITS[later][1:], blocks[UNITS[later][0]][1]
        low, high = pack_sides(blocks[chunk], unit, CHUNKS[chunk], cx, cy, rider, rider_mid)
        all_sides.append(both_ways(low, high, GY))
        own, own_at = None, 0
        if index in RIDES:
            carrier = RIDES[index]
            own = all_sides[carrier]
            own_at = unit_tiles(cx, UNITS[carrier][1:] + (carrier == 0, carrier in RIDES))
        out, diag = run_filter(blocks[chunk], all_sides[index], unit, CHUNKS[chunk], own, own_at, cx, cy, cz, diag)
        offset = GROUP * sum(g for _, _, g in UNITS[:index])
        filtered.append(out)
        last = index + 1 == len(UNITS)
        grams.append(run_gram(filtered, grams if last else (), offset, norb, scale))
    local = grams[-1]
    other = lax.ppermute(local, "core", [(core, 1 - core) for core in range(CORES)])
    chip = jnp.broadcast_to((local + other)[None], (chips,) + local.shape)
    received = lax.all_to_all(chip, ("gx", "gz"), 0, 0, tiled=True)
    return run_solve(received, filtered)


def solution(mesh):
    count = mesh.shape["gx"], mesh.shape["gy"] // CORES, CORES
    split = jax.sharding.Mesh(mesh.devices.reshape(count), ("gx",) + GY)
    placed = (P(None, "gx", GY, None), P("gx", GY, None))
    return jax.shard_map(
        body, mesh=split, in_specs=placed, out_specs=P(None, "gx", GY, None), check_vma=False
    )
```

```python
import functools
import math

import jax
import jax.numpy as jnp
from jax import lax
from jax.experimental import pallas as pl
from jax.experimental.pallas import tpu as pltpu
from jax.sharding import PartitionSpec as P

DEG = 4
HALO = 2 * DEG
CENTER = 5.0
HALF_W = 4.0
NEAR = (2.0 / HALF_W) * -0.5 * (4.0 / 3.0)
FAR = (2.0 / HALF_W) * 0.5 / 12.0
DIAG_SCALE = 2.0 / HALF_W
DIAG_SHIFT = (2.0 / HALF_W) * (3 * 0.5 * 2.5 - CENTER)

GROUP = 8
PREP_VMEM = 59 * 2**20
CHUNKS = (1, 2, 1)
UNITS = ((0, 0, 1), (1, 0, 1), (1, 1, 1), (2, 0, 1))
AFTER = {1: 0, 3: 1}
RIDES = {}
FILTER_COST = 100
GY = ("gz", "core")
CORES = 2


def axis_count(axis):
    return math.prod(lax.axis_size(a) for a in ((axis,) if isinstance(axis, str) else axis))


def shift_perm(axis, step):
    count = axis_count(axis)
    return [(i, (i + step) % count) for i in range(count)]


def both_ways(low_part, high_part, axis):
    return (
        lax.ppermute(high_part, axis, shift_perm(axis, 1)),
        lax.ppermute(low_part, axis, shift_perm(axis, -1)),
    )


def reach(plane, cx, left):
    outside = max(HALO - plane, plane - (HALO + cx - 1), 0)
    return left - 2 * ((outside + 1) // 2)


def halo_planes(cx, late=False):
    planes = []
    for plane in range(2, cx + 2 * HALO - 2):
        if late and HALO <= plane < HALO + cx:
            continue
        planes.append((plane, reach(plane, cx, HALO)))
    return planes


def diag_planes(cx):
    return range(4, cx + 2 * HALO - 4)


def split_plane(plane, cx):
    if plane < HALO:
        return 0, plane
    if plane < HALO + cx:
        return 1, plane - HALO
    return 2, plane - HALO - cx


def tile_block(out_ref, at, block):
    out_ref[at : at + block.shape[1]] = jnp.swapaxes(block, 0, 1)


def first_tiles_kernel(groups, pot_ref, orb_ref, out_ref, pot_here, here, pot_sem, sems):
    cx, cy, cz = pot_ref.shape
    pot_copy = pltpu.make_async_copy(pot_ref, pot_here, pot_sem)
    pot_copy.start()
    copies = []
    for g in range(groups):
        part = pl.ds(GROUP * g, GROUP)
        copies.append(pltpu.make_async_copy(orb_ref.at[part], here.at[part], sems.at[g]))
        copies[-1].start()
    for g in range(groups):
        copies[g].wait()
        for x in range(cx):
            tile_block(out_ref, g * cx * cy + x * cy, here[GROUP * g : GROUP * (g + 1), x])
    pot_copy.wait()
    out_ref[groups * cx * cy :] = pot_here[...].reshape(cx * cy // 8, 8, cz)


def first_tiles(orbitals, potential):
    _, cx, cy, cz = orbitals.shape
    groups = CHUNKS[0]
    tiles = groups * cx * cy + cx * cy // 8
    return pl.pallas_call(
        functools.partial(first_tiles_kernel, groups),
        out_shape=jax.ShapeDtypeStruct((tiles, 8, cz), jnp.float32),
        in_specs=[pl.BlockSpec(memory_space=pltpu.HBM)] * 2,
        out_specs=pl.BlockSpec(memory_space=pltpu.VMEM),
        scratch_shapes=[
            pltpu.VMEM((cx, cy, cz), jnp.float32),
            pltpu.VMEM((groups * GROUP, cx, cy, cz), jnp.float32),
            pltpu.SemaphoreType.DMA,
            pltpu.SemaphoreType.DMA((groups,)),
        ],
        compiler_params=pltpu.CompilerParams(vmem_limit_bytes=PREP_VMEM),
        name="first_tiles",
    )(potential, orbitals)


def tiles_kernel(chunks, pot_ref, orb_ref, *out_refs):
    cx, cy, cz = pot_ref.shape
    group = 0
    for out_ref, groups in zip(out_refs, chunks):
        for g in range(groups):
            for x in range(cx):
                tile_block(out_ref, g * cx * cy + x * cy, orb_ref[GROUP * group : GROUP * (group + 1), x])
            group += 1
    out_refs[0][chunks[0] * cx * cy :] = pot_ref[...].reshape(cx * cy // 8, 8, cz)


def all_tiles(orbitals, potential):
    _, cx, cy, cz = orbitals.shape
    tiles = [groups * cx * cy for groups in CHUNKS]
    tiles[0] += cx * cy // 8
    return pl.pallas_call(
        functools.partial(tiles_kernel, CHUNKS),
        out_shape=[jax.ShapeDtypeStruct((t, 8, cz), jnp.float32) for t in tiles],
        in_specs=[pl.BlockSpec(memory_space=pltpu.VMEM)] * 2,
        out_specs=[pl.BlockSpec(memory_space=pltpu.VMEM)] * len(tiles),
        compiler_params=pltpu.CompilerParams(vmem_limit_bytes=16 * 2**20),
        name="all_tiles",
    )(potential, orbitals)


def sides_kernel(unit, chunk_groups, rider, cx, cy, *refs):
    low_ref, high_ref = refs[-2:]
    start, groups, first, late = unit
    at = 0
    for g in range(start, start + groups):
        for plane, rows in halo_planes(cx, late):
            which, x = split_plane(plane, cx)
            base = g * cx * cy + x * cy
            low_ref[at : at + rows] = refs[which][base : base + rows]
            high_ref[at : at + rows] = refs[which][base + cy - rows : base + cy]
            at += rows
    if first:
        per = cy // 8
        for plane in diag_planes(cx):
            which, x = split_plane(plane, cx)
            base = chunk_groups * cx * cy + x * per
            low_ref[at] = refs[which][base]
            high_ref[at] = refs[which][base + per - 1]
            at += 1
    if rider is not None:
        for g in range(rider[0], rider[0] + rider[1]):
            for x in range(cx):
                base = g * cx * cy + x * cy
                low_ref[at : at + HALO] = refs[3][base : base + HALO]
                high_ref[at : at + HALO] = refs[3][base + cy - HALO : base + cy]
                at += HALO


def unit_tiles(cx, unit):
    _, groups, first, late = unit
    return groups * sum(rows for _, rows in halo_planes(cx, late)) + (len(diag_planes(cx)) if first else 0)


def pack_sides(blocks, unit, chunk_groups, cx, cy, rider, rider_mid):
    tiles = unit_tiles(cx, unit) + (0 if rider is None else rider[1] * cx * HALO)
    shape = jax.ShapeDtypeStruct((tiles,) + blocks[0].shape[1:], jnp.float32)
    operands = blocks + (() if rider is None else (rider_mid,))
    return pl.pallas_call(
        functools.partial(sides_kernel, unit, chunk_groups, rider, cx, cy),
        out_shape=(shape, shape),
        in_specs=[pl.BlockSpec(memory_space=pltpu.VMEM)] * len(operands),
        out_specs=(pl.BlockSpec(memory_space=pltpu.VMEM),) * 2,
        compiler_params=pltpu.CompilerParams(vmem_limit_bytes=16 * 2**20),
        cost_estimate=pl.CostEstimate(flops=0, bytes_accessed=1_000_000, transcendentals=0),
        name="pack_sides",
    )(*operands)


def z_circulant(cz):
    row = lax.broadcasted_iota(jnp.int32, (cz, cz), 0)
    col = lax.broadcasted_iota(jnp.int32, (cz, cz), 1)
    gap = jnp.where(row >= col, row - col, row - col + cz)
    near = (gap == 1) | (gap == cz - 1)
    far = (gap == 2) | (gap == cz - 2)
    return jnp.where(near, -16.0, jnp.where(far, 1.0, 0.0)).astype(jnp.bfloat16)


def z_part(center, matrix):
    flat = center.reshape(-1, center.shape[-1])
    high = flat.astype(jnp.bfloat16)
    rest = flat - high.astype(jnp.float32)
    middle = rest.astype(jnp.bfloat16)
    low = (rest - middle.astype(jnp.float32)).astype(jnp.bfloat16)

    def times(part):
        return jnp.dot(part, matrix, preferred_element_type=jnp.float32)

    return (times(high) + (times(middle) + times(low))).reshape(center.shape)


def four_steps(cx, cy, chain, diag_ref, out_ref):
    total = cx + 2 * HALO
    matrix = z_circulant(out_ref.shape[-1])
    for step in range(DEG):
        source = chain[step]
        left = HALO - 2 * (step + 1)
        for plane in range(total):
            rows = reach(plane, cx, left)
            if rows < 0:
                continue
            first, count = HALO - rows, cy + 2 * rows
            here = slice(first, first + count)
            column = source[plane, first - 2 : first + count + 2]
            center = column[2:-2]
            near = (column[1:-3] + column[3:-1]) + (source[plane - 1, here] + source[plane + 1, here])
            far = (column[:-4] + column[4:]) + (source[plane - 2, here] + source[plane + 2, here])
            applied = diag_ref[plane, here][:, None, :] * center + FAR * ((z_part(center, matrix) + far) - 16.0 * near)
            fresh = 0.5 * applied if step == 0 else applied - chain[step - 1][plane, here]
            if step < DEG - 1:
                chain[step + 1][plane, here] = fresh
            else:
                out_ref[:, plane - HALO] = jnp.swapaxes(fresh, 0, 1)


def fill_blocks(cx, cy, base, sources, ext_ref):
    for x in range(cx):
        for which in range(3):
            ext_ref[which * cx + x, HALO : HALO + cy] = sources[which][pl.ds(base + x * cy, cy)]


def filter_kernel(unit, chunk_groups, own_at, cx, cy, lo_ref, mid_ref, hi_ref, yl_ref, yh_ref, *refs):
    start, groups, first, late = unit
    group = pl.program_id(0)
    sources = (lo_ref, mid_ref, hi_ref)
    planes = halo_planes(cx, late)
    side = sum(rows for _, rows in planes)
    if first:
        out_ref, diag_ref = refs[:2]

        @pl.when(group == 0)
        def _():
            per = cy // 8
            cz = out_ref.shape[-1]
            for x in range(cx):
                for which in range(3):
                    base = chunk_groups * cx * cy + x * per
                    block = sources[which][base : base + per].reshape(cy, cz)
                    diag_ref[which * cx + x, HALO : HALO + cy] = DIAG_SCALE * block + DIAG_SHIFT
            at = groups * side
            for plane in diag_planes(cx):
                diag_ref[plane, 0:HALO] = DIAG_SCALE * yl_ref[at] + DIAG_SHIFT
                diag_ref[plane, HALO + cy :] = DIAG_SCALE * yh_ref[at] + DIAG_SHIFT
                at += 1
    else:
        diag_ref, out_ref = refs[-6:-4]
    chain = refs[-4:]
    if late:
        for x in range(cx):
            base = own_at + group * cx * HALO + x * HALO
            chain[0][HALO + x, 0:HALO] = refs[0][pl.ds(base, HALO)]
            chain[0][HALO + x, HALO + cy :] = refs[1][pl.ds(base, HALO)]
    for x in range(cx):
        for which in range(3):
            tiles = sources[which][pl.ds((start + group) * cx * cy + x * cy, cy)]
            chain[0][which * cx + x, HALO : HALO + cy] = tiles
    at = 0
    for plane, rows in planes:
        chain[0][plane, HALO - rows : HALO] = yl_ref[pl.ds(group * side + at, rows)]
        chain[0][plane, HALO + cy : HALO + cy + rows] = yh_ref[pl.ds(group * side + at, rows)]
        at += rows
    four_steps(cx, cy, chain, diag_ref, out_ref)


def run_filter(blocks, sides, unit, chunk_groups, own, own_at, cx, cy, cz, diag):
    _, groups, first, late = unit
    ext = (cx + 2 * HALO, cy + 2 * HALO, GROUP, cz)
    out_shape = [jax.ShapeDtypeStruct((groups * GROUP, cx, cy, cz), jnp.float32)]
    out_specs = [pl.BlockSpec((GROUP, cx, cy, cz), lambda g: (g, 0, 0, 0))]
    operands = blocks + sides + (own if late else ())
    if first:
        wide = (cx + 2 * HALO, cy + 2 * HALO, cz)
        out_shape.append(jax.ShapeDtypeStruct(wide, jnp.float32))
        out_specs.append(pl.BlockSpec(wide, lambda g: (0, 0, 0)))
    else:
        operands = operands + (diag,)
    got = pl.pallas_call(
        functools.partial(filter_kernel, unit, chunk_groups, own_at, cx, cy),
        grid=(groups,),
        out_shape=out_shape,
        in_specs=[pl.BlockSpec(memory_space=pltpu.VMEM)] * len(operands),
        out_specs=out_specs,
        scratch_shapes=[pltpu.VMEM(ext, jnp.float32)] * 4,
        compiler_params=pltpu.CompilerParams(vmem_limit_bytes=32 * 2**20),
        cost_estimate=pl.CostEstimate(flops=0, bytes_accessed=groups * FILTER_COST, transcendentals=0),
        name="filter_orbitals",
    )(*operands)
    return got if first else (got[0], diag)


def gram_kernel(offset, scale, counts, *refs):
    chunks, earlier, out_ref, rows_ref = refs[: len(counts)], refs[len(counts) : -2], refs[-2], refs[-1]
    own = chunks[-1]
    count, cx, cy, cz = own.shape
    norb = rows_ref.shape[1]
    rows = []
    for ref, size in zip(chunks, counts):
        for at in range(size):
            rows.append((ref, at))
    rows_ref[...] = jnp.zeros_like(rows_ref)
    block = 4
    for a0 in range(0, count, block):
        a_list = list(range(a0, min(a0 + block, count)))
        last = offset + a_list[-1]
        for j0 in range(0, last + 1, block):
            j_list = list(range(j0, min(j0 + block, last + 1)))
            accs = [None] * (len(a_list) * len(j_list))
            for x in range(cx):
                left = [own[a, x] for a in a_list]
                right = [rows[j][0][rows[j][1], x] for j in j_list]
                at = 0
                for l in left:
                    for r in right:
                        prod = l * r
                        prod = prod[:8] + prod[8:]
                        accs[at] = prod if accs[at] is None else accs[at] + prod
                        at += 1
            at = 0
            for a in a_list:
                for j in j_list:
                    rows_ref[a, j : j + 1, :] = jnp.sum(accs[at], axis=0, keepdims=True)
                    at += 1
    sums = lax.dot_general(
        jnp.ones((8, cz), jnp.float32), rows_ref[...].reshape(count * norb, cz), (((1,), (1,)), ((), ())),
        precision=lax.Precision.HIGHEST, preferred_element_type=jnp.float32,
    )
    lane = lax.broadcasted_iota(jnp.int32, (8, 128), 1)
    row = lax.broadcasted_iota(jnp.int32, (8, 128), 0)
    per = 128 // norb
    packed = jnp.zeros((8, 128), jnp.float32)
    for a in range(count):
        here, slot = a // per, (offset + a) // 8
        value = pltpu.roll(sums[:, 128 * here : 128 * (here + 1)], (norb * (slot - a % per)) % 128, 1)
        mask = (row == (offset + a) % 8) & (lane >= norb * slot) & (lane < norb * (slot + 1))
        packed = packed + jnp.where(mask, value, 0.0)
    packed = packed * scale
    for ref in earlier:
        packed = packed + ref[...]
    out_ref[...] = packed


def run_gram(chunks, earlier, offset, norb, scale):
    count, cx, cy, cz = chunks[-1].shape
    counts = tuple(c.shape[0] for c in chunks)
    operands = tuple(chunks) + tuple(earlier)
    return pl.pallas_call(
        functools.partial(gram_kernel, offset, scale, counts),
        out_shape=jax.ShapeDtypeStruct((8, 128), jnp.float32),
        in_specs=[pl.BlockSpec(memory_space=pltpu.VMEM)] * len(operands),
        out_specs=pl.BlockSpec(memory_space=pltpu.VMEM),
        scratch_shapes=[pltpu.VMEM((count, norb, cz), jnp.float32)],
        compiler_params=pltpu.CompilerParams(vmem_limit_bytes=24 * 2**20),
        cost_estimate=pl.CostEstimate(flops=0, bytes_accessed=100, transcendentals=0),
        name="gram_rows",
    )(*operands)


def factor_table(gram, table_ref):
    norb = gram.shape[0]
    columns = [jnp.broadcast_to(gram[:, j : j + 1], (norb, 128)) for j in range(norb)]
    row = lax.broadcasted_iota(jnp.int32, (norb, 128), 0)
    for k in range(norb):
        scale = 1.0 / jnp.sqrt(columns[k][k : k + 1])
        column = columns[k] * scale
        table_ref[k] = jnp.where(row == k, scale, column)
        for j in range(k + 1, norb):
            top = 8 * (j // 8)
            fresh = columns[j][top:] - column[top:] * column[j : j + 1]
            columns[j] = fresh if top == 0 else jnp.concatenate([jnp.zeros((top, 128), jnp.float32), fresh], axis=0)


def solve_kernel(counts, recv_ref, *refs):
    norb = sum(counts)
    chunks, (out_ref, here_ref, table_ref, sems) = refs[: len(counts)], refs[len(counts) :]
    packed = jnp.sum(recv_ref[...], axis=0)
    rows = jnp.concatenate([packed] + [jnp.roll(packed, -norb * q, 1) for q in range(1, 4)], axis=0)
    factor_table(rows, table_ref)
    where = []
    for ref, count in zip(chunks, counts):
        for at in range(count):
            where.append((ref, at))
    block = 8
    cx = here_ref.shape[1]

    def copy_out(x):
        return pltpu.make_async_copy(here_ref.at[:, x], out_ref.at[:, x], sems.at[x])

    def layer(x, _):
        for i0 in range(0, norb, block):
            accs = [where[i0 + a][0][where[i0 + a][1], x] for a in range(block)]
            for j in range(i0):
                value = here_ref[j, x]
                for a in range(block):
                    accs[a] = accs[a] - table_ref[j, i0 + a : i0 + a + 1, :] * value
            for a in range(block):
                value = accs[a] * table_ref[i0 + a, i0 + a : i0 + a + 1, :]
                here_ref[i0 + a, x] = value
                for c in range(a + 1, block):
                    accs[c] = accs[c] - table_ref[i0 + a, i0 + c : i0 + c + 1, :] * value
        copy_out(x).start()
        return 0

    lax.fori_loop(0, cx, layer, 0)
    for x in range(cx):
        copy_out(x).wait()


def run_solve(received, chunks):
    counts = tuple(c.shape[0] for c in chunks)
    norb = sum(counts)
    _, cx, cy, cz = chunks[0].shape
    return pl.pallas_call(
        functools.partial(solve_kernel, counts),
        out_shape=jax.ShapeDtypeStruct((norb, cx, cy, cz), jnp.float32),
        in_specs=[pl.BlockSpec(memory_space=pltpu.VMEM)] * (1 + len(chunks)),
        out_specs=pl.BlockSpec(memory_space=pl.ANY),
        scratch_shapes=[
            pltpu.VMEM((norb, cx, cy, cz), jnp.float32),
            pltpu.VMEM((norb, norb, 128), jnp.float32),
            pltpu.SemaphoreType.DMA((cx,)),
        ],
        compiler_params=pltpu.CompilerParams(vmem_limit_bytes=24 * 2**20),
        name="orthonormalize",
    )(received, *chunks)


def body(orbitals, potential):
    norb, cx, cy, cz = orbitals.shape
    chips = axis_count(("gx", "gz"))
    scale = 1.0 / float(chips * CORES * cx * cy * cz)
    blocks = []
    first = first_tiles(orbitals, potential)
    for index, mid in enumerate(all_tiles(orbitals, potential)):
        lo, hi = both_ways(*((first, first) if index == 0 else (mid, mid)), "gx")
        blocks.append((lo, mid, hi))
    diag = None
    filtered, grams, all_sides = [], [], []
    for index, (chunk, start, groups) in enumerate(UNITS):
        unit = (start, groups, index == 0, index in RIDES)
        if index in AFTER:
            lo, mid, hi = blocks[chunk]
            before = AFTER[index]
            tied = (lo, hi, filtered[before]) + ((grams[before],) if before == 0 else ())
            lo, hi, filtered[before], *rest = lax.optimization_barrier(tied)
            grams[before : before + len(rest)] = rest
            blocks[chunk] = lo, mid, hi
        rider, rider_mid = None, None
        for later, carrier in RIDES.items():
            if carrier == index:
                rider, rider_mid = UNITS[later][1:], blocks[UNITS[later][0]][1]
        low, high = pack_sides(blocks[chunk], unit, CHUNKS[chunk], cx, cy, rider, rider_mid)
        all_sides.append(both_ways(low, high, GY))
        own, own_at = None, 0
        if index in RIDES:
            carrier = RIDES[index]
            own = all_sides[carrier]
            own_at = unit_tiles(cx, UNITS[carrier][1:] + (carrier == 0, carrier in RIDES))
        out, diag = run_filter(blocks[chunk], all_sides[index], unit, CHUNKS[chunk], own, own_at, cx, cy, cz, diag)
        offset = GROUP * sum(g for _, _, g in UNITS[:index])
        filtered.append(out)
        last = index + 1 == len(UNITS)
        grams.append(run_gram(filtered, grams if last else (), offset, norb, scale))
    local = grams[-1]
    other = lax.ppermute(local, "core", [(core, 1 - core) for core in range(CORES)])
    chip = jnp.broadcast_to((local + other)[None], (chips,) + local.shape)
    received = lax.all_to_all(chip, ("gx", "gz"), 0, 0, tiled=True)
    return run_solve(received, filtered)


def solution(mesh):
    count = mesh.shape["gx"], mesh.shape["gy"] // CORES, CORES
    split = jax.sharding.Mesh(mesh.devices.reshape(count), ("gx",) + GY)
    placed = (P(None, "gx", GY, None), P("gx", GY, None))
    return jax.shard_map(
        body, mesh=split, in_specs=placed, out_specs=P(None, "gx", GY, None), check_vma=False
    )
```

```python
import functools
import math

import jax
import jax.numpy as jnp
from jax import lax
from jax.experimental import pallas as pl
from jax.experimental.pallas import tpu as pltpu
from jax.sharding import PartitionSpec as P

DEG = 4
HALO = 2 * DEG
CENTER = 5.0
HALF_W = 4.0
NEAR = (2.0 / HALF_W) * -0.5 * (4.0 / 3.0)
FAR = (2.0 / HALF_W) * 0.5 / 12.0
DIAG_SCALE = 2.0 / HALF_W
DIAG_SHIFT = (2.0 / HALF_W) * (3 * 0.5 * 2.5 - CENTER)

GROUP = 8
PREP_VMEM = 59 * 2**20
CHUNKS = (1, 2, 1)
UNITS = ((0, 0, 1), (1, 0, 1), (1, 1, 1), (2, 0, 1))
AFTER = {1: 0, 3: 1}
RIDES = {}
ALONE = {1: 0}
FILTER_COST = 100
GY = ("gz", "core")
CORES = 2


def axis_count(axis):
    return math.prod(lax.axis_size(a) for a in ((axis,) if isinstance(axis, str) else axis))


def shift_perm(axis, step):
    count = axis_count(axis)
    return [(i, (i + step) % count) for i in range(count)]


def both_ways(low_part, high_part, axis):
    return (
        lax.ppermute(high_part, axis, shift_perm(axis, 1)),
        lax.ppermute(low_part, axis, shift_perm(axis, -1)),
    )


def reach(plane, cx, left):
    outside = max(HALO - plane, plane - (HALO + cx - 1), 0)
    return left - 2 * ((outside + 1) // 2)


def halo_planes(cx, late=False):
    planes = []
    for plane in range(2, cx + 2 * HALO - 2):
        if late and HALO <= plane < HALO + cx:
            continue
        planes.append((plane, reach(plane, cx, HALO)))
    return planes


def diag_planes(cx):
    return range(4, cx + 2 * HALO - 4)


def split_plane(plane, cx):
    if plane < HALO:
        return 0, plane
    if plane < HALO + cx:
        return 1, plane - HALO
    return 2, plane - HALO - cx


def tile_block(out_ref, at, block):
    out_ref[at : at + block.shape[1]] = jnp.swapaxes(block, 0, 1)


def first_tiles_kernel(groups, pieces, pot_ref, orb_ref, out_ref, pot_here, here, tiles, in_sems, out_sems):
    cx, cy, cz = pot_ref.shape
    pot_copy = pltpu.make_async_copy(pot_ref, pot_here, in_sems.at[groups * pieces])
    pot_copy.start()
    deep = cx // pieces
    parts = [(g, p) for g in range(groups) for p in range(pieces)]
    loads, stores = [], []
    for index, (g, p) in enumerate(parts):
        part = (pl.ds(GROUP * g, GROUP), pl.ds(deep * p, deep))
        loads.append(pltpu.make_async_copy(orb_ref.at[part], here.at[part], in_sems.at[index]))
        loads[-1].start()

    def store(index, start, size):
        rows = pl.ds(start, size)
        stores.append(pltpu.make_async_copy(tiles.at[rows], out_ref.at[rows], out_sems.at[index]))
        stores[-1].start()

    pot_copy.wait()
    tiles[groups * cx * cy :] = pot_here[...].reshape(cx * cy // 8, 8, cz)
    store(groups * pieces, groups * cx * cy, cx * cy // 8)
    for index, (g, p) in enumerate(parts):
        loads[index].wait()
        for x in range(deep * p, deep * (p + 1)):
            tile_block(tiles, g * cx * cy + x * cy, here[GROUP * g : GROUP * (g + 1), x])
        store(index, g * cx * cy + deep * p * cy, deep * cy)
    for copy in stores:
        copy.wait()


def first_tiles(orbitals, potential):
    _, cx, cy, cz = orbitals.shape
    groups, pieces = CHUNKS[0], 2
    tiles = (groups * cx * cy + cx * cy // 8, 8, cz)
    return pl.pallas_call(
        functools.partial(first_tiles_kernel, groups, pieces),
        out_shape=jax.ShapeDtypeStruct(tiles, jnp.float32),
        in_specs=[pl.BlockSpec(memory_space=pltpu.HBM)] * 2,
        out_specs=pl.BlockSpec(memory_space=pltpu.HBM),
        scratch_shapes=[
            pltpu.VMEM((cx, cy, cz), jnp.float32),
            pltpu.VMEM((groups * GROUP, cx, cy, cz), jnp.float32),
            pltpu.VMEM(tiles, jnp.float32),
            pltpu.SemaphoreType.DMA((groups * pieces + 1,)),
            pltpu.SemaphoreType.DMA((groups * pieces + 1,)),
        ],
        compiler_params=pltpu.CompilerParams(vmem_limit_bytes=PREP_VMEM),
        name="first_tiles",
    )(potential, orbitals)


def tiles_kernel(chunks, pot_ref, orb_ref, *out_refs):
    cx, cy, cz = pot_ref.shape
    group = 0
    for out_ref, groups in zip(out_refs, chunks):
        for g in range(groups):
            for x in range(cx):
                tile_block(out_ref, g * cx * cy + x * cy, orb_ref[GROUP * group : GROUP * (group + 1), x])
            group += 1
    out_refs[0][chunks[0] * cx * cy :] = pot_ref[...].reshape(cx * cy // 8, 8, cz)


def all_tiles(orbitals, potential):
    _, cx, cy, cz = orbitals.shape
    tiles = [groups * cx * cy for groups in CHUNKS]
    tiles[0] += cx * cy // 8
    return pl.pallas_call(
        functools.partial(tiles_kernel, CHUNKS),
        out_shape=[jax.ShapeDtypeStruct((t, 8, cz), jnp.float32) for t in tiles],
        in_specs=[pl.BlockSpec(memory_space=pltpu.VMEM)] * 2,
        out_specs=[pl.BlockSpec(memory_space=pltpu.VMEM)] * len(tiles),
        compiler_params=pltpu.CompilerParams(vmem_limit_bytes=16 * 2**20),
        name="all_tiles",
    )(potential, orbitals)


def sides_kernel(unit, chunk_groups, rider, cx, cy, *refs):
    low_ref, high_ref = refs[-2:]
    start, groups, first, late = unit
    at = 0
    for g in range(start, start + groups):
        for plane, rows in halo_planes(cx, late):
            which, x = split_plane(plane, cx)
            base = g * cx * cy + x * cy
            low_ref[at : at + rows] = refs[which][base : base + rows]
            high_ref[at : at + rows] = refs[which][base + cy - rows : base + cy]
            at += rows
    if first:
        per = cy // 8
        for plane in diag_planes(cx):
            which, x = split_plane(plane, cx)
            base = chunk_groups * cx * cy + x * per
            low_ref[at] = refs[which][base]
            high_ref[at] = refs[which][base + per - 1]
            at += 1
    if rider is not None:
        for g in range(rider[0], rider[0] + rider[1]):
            for x in range(cx):
                base = g * cx * cy + x * cy
                low_ref[at : at + HALO] = refs[3][base : base + HALO]
                high_ref[at : at + HALO] = refs[3][base + cy - HALO : base + cy]
                at += HALO


def unit_tiles(cx, unit):
    _, groups, first, late = unit
    return groups * sum(rows for _, rows in halo_planes(cx, late)) + (len(diag_planes(cx)) if first else 0)


def pack_sides(blocks, unit, chunk_groups, cx, cy, rider, rider_mid):
    tiles = unit_tiles(cx, unit) + (0 if rider is None else rider[1] * cx * HALO)
    shape = jax.ShapeDtypeStruct((tiles,) + blocks[0].shape[1:], jnp.float32)
    operands = blocks + (() if rider is None else (rider_mid,))
    return pl.pallas_call(
        functools.partial(sides_kernel, unit, chunk_groups, rider, cx, cy),
        out_shape=(shape, shape),
        in_specs=[pl.BlockSpec(memory_space=pltpu.VMEM)] * len(operands),
        out_specs=(pl.BlockSpec(memory_space=pltpu.VMEM),) * 2,
        compiler_params=pltpu.CompilerParams(vmem_limit_bytes=16 * 2**20),
        cost_estimate=pl.CostEstimate(flops=0, bytes_accessed=1_000_000, transcendentals=0),
        name="pack_sides",
    )(*operands)


def z_circulant(cz):
    row = lax.broadcasted_iota(jnp.int32, (cz, cz), 0)
    col = lax.broadcasted_iota(jnp.int32, (cz, cz), 1)
    gap = jnp.where(row >= col, row - col, row - col + cz)
    near = (gap == 1) | (gap == cz - 1)
    far = (gap == 2) | (gap == cz - 2)
    return jnp.where(near, -16.0, jnp.where(far, 1.0, 0.0)).astype(jnp.bfloat16)


def z_part(center, matrix):
    flat = center.reshape(-1, center.shape[-1])
    high = flat.astype(jnp.bfloat16)
    rest = flat - high.astype(jnp.float32)
    middle = rest.astype(jnp.bfloat16)
    low = (rest - middle.astype(jnp.float32)).astype(jnp.bfloat16)

    def times(part):
        return jnp.dot(part, matrix, preferred_element_type=jnp.float32)

    return (times(high) + (times(middle) + times(low))).reshape(center.shape)


def four_steps(cx, cy, chain, diag_ref, out_ref):
    total = cx + 2 * HALO
    matrix = z_circulant(out_ref.shape[-1])
    for step in range(DEG):
        source = chain[step]
        left = HALO - 2 * (step + 1)
        for plane in range(total):
            rows = reach(plane, cx, left)
            if rows < 0:
                continue
            first, count = HALO - rows, cy + 2 * rows
            here = slice(first, first + count)
            column = source[plane, first - 2 : first + count + 2]
            center = column[2:-2]
            near = (column[1:-3] + column[3:-1]) + (source[plane - 1, here] + source[plane + 1, here])
            far = (column[:-4] + column[4:]) + (source[plane - 2, here] + source[plane + 2, here])
            applied = diag_ref[plane, here][:, None, :] * center + FAR * ((z_part(center, matrix) + far) - 16.0 * near)
            fresh = 0.5 * applied if step == 0 else applied - chain[step - 1][plane, here]
            if step < DEG - 1:
                chain[step + 1][plane, here] = fresh
            else:
                out_ref[:, plane - HALO] = jnp.swapaxes(fresh, 0, 1)


def fill_blocks(cx, cy, base, sources, ext_ref):
    for x in range(cx):
        for which in range(3):
            ext_ref[which * cx + x, HALO : HALO + cy] = sources[which][pl.ds(base + x * cy, cy)]


def filter_kernel(unit, chunk_groups, own_at, cx, cy, lo_ref, mid_ref, hi_ref, yl_ref, yh_ref, *refs):
    start, groups, first, late = unit
    group = pl.program_id(0)
    sources = (lo_ref, mid_ref, hi_ref)
    planes = halo_planes(cx, late)
    side = sum(rows for _, rows in planes)
    if first:
        out_ref, diag_ref = refs[:2]

        @pl.when(group == 0)
        def _():
            per = cy // 8
            cz = out_ref.shape[-1]
            for x in range(cx):
                for which in range(3):
                    base = chunk_groups * cx * cy + x * per
                    block = sources[which][base : base + per].reshape(cy, cz)
                    diag_ref[which * cx + x, HALO : HALO + cy] = DIAG_SCALE * block + DIAG_SHIFT
            at = groups * side
            for plane in diag_planes(cx):
                diag_ref[plane, 0:HALO] = DIAG_SCALE * yl_ref[at] + DIAG_SHIFT
                diag_ref[plane, HALO + cy :] = DIAG_SCALE * yh_ref[at] + DIAG_SHIFT
                at += 1
    else:
        diag_ref, out_ref = refs[-6:-4]
    chain = refs[-4:]
    if late:
        for x in range(cx):
            base = own_at + group * cx * HALO + x * HALO
            chain[0][HALO + x, 0:HALO] = refs[0][pl.ds(base, HALO)]
            chain[0][HALO + x, HALO + cy :] = refs[1][pl.ds(base, HALO)]
    for x in range(cx):
        for which in range(3):
            tiles = sources[which][pl.ds((start + group) * cx * cy + x * cy, cy)]
            chain[0][which * cx + x, HALO : HALO + cy] = tiles
    at = 0
    for plane, rows in planes:
        chain[0][plane, HALO - rows : HALO] = yl_ref[pl.ds(group * side + at, rows)]
        chain[0][plane, HALO + cy : HALO + cy + rows] = yh_ref[pl.ds(group * side + at, rows)]
        at += rows
    four_steps(cx, cy, chain, diag_ref, out_ref)


def run_filter(blocks, sides, unit, chunk_groups, own, own_at, cx, cy, cz, diag):
    _, groups, first, late = unit
    ext = (cx + 2 * HALO, cy + 2 * HALO, GROUP, cz)
    out_shape = [jax.ShapeDtypeStruct((groups * GROUP, cx, cy, cz), jnp.float32)]
    out_specs = [pl.BlockSpec((GROUP, cx, cy, cz), lambda g: (g, 0, 0, 0))]
    operands = blocks + sides + (own if late else ())
    if first:
        wide = (cx + 2 * HALO, cy + 2 * HALO, cz)
        out_shape.append(jax.ShapeDtypeStruct(wide, jnp.float32))
        out_specs.append(pl.BlockSpec(wide, lambda g: (0, 0, 0)))
    else:
        operands = operands + (diag,)
    got = pl.pallas_call(
        functools.partial(filter_kernel, unit, chunk_groups, own_at, cx, cy),
        grid=(groups,),
        out_shape=out_shape,
        in_specs=[pl.BlockSpec(memory_space=pltpu.VMEM)] * len(operands),
        out_specs=out_specs,
        scratch_shapes=[pltpu.VMEM(ext, jnp.float32)] * 4,
        compiler_params=pltpu.CompilerParams(vmem_limit_bytes=32 * 2**20),
        cost_estimate=pl.CostEstimate(flops=0, bytes_accessed=groups * FILTER_COST, transcendentals=0),
        name="filter_orbitals",
    )(*operands)
    return got if first else (got[0], diag)


def gram_kernel(offset, scale, counts, *refs):
    chunks, earlier, out_ref, rows_ref = refs[: len(counts)], refs[len(counts) : -2], refs[-2], refs[-1]
    own = chunks[-1]
    count, cx, cy, cz = own.shape
    norb = rows_ref.shape[1]
    rows = []
    for ref, size in zip(chunks, counts):
        for at in range(size):
            rows.append((ref, at))
    rows_ref[...] = jnp.zeros_like(rows_ref)
    block = 4
    for a0 in range(0, count, block):
        a_list = list(range(a0, min(a0 + block, count)))
        last = offset + a_list[-1]
        for j0 in range(0, last + 1, block):
            j_list = list(range(j0, min(j0 + block, last + 1)))
            accs = [None] * (len(a_list) * len(j_list))
            for x in range(cx):
                left = [own[a, x] for a in a_list]
                right = [rows[j][0][rows[j][1], x] for j in j_list]
                at = 0
                for l in left:
                    for r in right:
                        prod = l * r
                        prod = prod[:8] + prod[8:]
                        accs[at] = prod if accs[at] is None else accs[at] + prod
                        at += 1
            at = 0
            for a in a_list:
                for j in j_list:
                    rows_ref[a, j : j + 1, :] = jnp.sum(accs[at], axis=0, keepdims=True)
                    at += 1
    sums = lax.dot_general(
        jnp.ones((8, cz), jnp.float32), rows_ref[...].reshape(count * norb, cz), (((1,), (1,)), ((), ())),
        precision=lax.Precision.HIGHEST, preferred_element_type=jnp.float32,
    )
    lane = lax.broadcasted_iota(jnp.int32, (8, 128), 1)
    row = lax.broadcasted_iota(jnp.int32, (8, 128), 0)
    per = 128 // norb
    packed = jnp.zeros((8, 128), jnp.float32)
    for a in range(count):
        here, slot = a // per, (offset + a) // 8
        value = pltpu.roll(sums[:, 128 * here : 128 * (here + 1)], (norb * (slot - a % per)) % 128, 1)
        mask = (row == (offset + a) % 8) & (lane >= norb * slot) & (lane < norb * (slot + 1))
        packed = packed + jnp.where(mask, value, 0.0)
    packed = packed * scale
    for ref in earlier:
        packed = packed + ref[...]
    out_ref[...] = packed


def run_gram(chunks, earlier, offset, norb, scale):
    count, cx, cy, cz = chunks[-1].shape
    counts = tuple(c.shape[0] for c in chunks)
    operands = tuple(chunks) + tuple(earlier)
    return pl.pallas_call(
        functools.partial(gram_kernel, offset, scale, counts),
        out_shape=jax.ShapeDtypeStruct((8, 128), jnp.float32),
        in_specs=[pl.BlockSpec(memory_space=pltpu.VMEM)] * len(operands),
        out_specs=pl.BlockSpec(memory_space=pltpu.VMEM),
        scratch_shapes=[pltpu.VMEM((count, norb, cz), jnp.float32)],
        compiler_params=pltpu.CompilerParams(vmem_limit_bytes=24 * 2**20),
        cost_estimate=pl.CostEstimate(flops=0, bytes_accessed=100, transcendentals=0),
        name="gram_rows",
    )(*operands)


def factor_table(gram, table_ref):
    norb = gram.shape[0]
    columns = [jnp.broadcast_to(gram[:, j : j + 1], (norb, 128)) for j in range(norb)]
    row = lax.broadcasted_iota(jnp.int32, (norb, 128), 0)
    for k in range(norb):
        scale = 1.0 / jnp.sqrt(columns[k][k : k + 1])
        column = columns[k] * scale
        table_ref[k] = jnp.where(row == k, scale, column)
        for j in range(k + 1, norb):
            top = 8 * (j // 8)
            fresh = columns[j][top:] - column[top:] * column[j : j + 1]
            columns[j] = fresh if top == 0 else jnp.concatenate([jnp.zeros((top, 128), jnp.float32), fresh], axis=0)


def solve_kernel(counts, recv_ref, *refs):
    norb = sum(counts)
    chunks, (out_ref, here_ref, table_ref, sems) = refs[: len(counts)], refs[len(counts) :]
    packed = jnp.sum(recv_ref[...], axis=0)
    rows = jnp.concatenate([packed] + [jnp.roll(packed, -norb * q, 1) for q in range(1, 4)], axis=0)
    factor_table(rows, table_ref)
    where = []
    for ref, count in zip(chunks, counts):
        for at in range(count):
            where.append((ref, at))
    block = 8
    cx = here_ref.shape[1]

    def copy_out(x):
        return pltpu.make_async_copy(here_ref.at[:, x], out_ref.at[:, x], sems.at[x])

    def layer(x, _):
        for i0 in range(0, norb, block):
            accs = [where[i0 + a][0][where[i0 + a][1], x] for a in range(block)]
            for j in range(i0):
                value = here_ref[j, x]
                for a in range(block):
                    accs[a] = accs[a] - table_ref[j, i0 + a : i0 + a + 1, :] * value
            for a in range(block):
                value = accs[a] * table_ref[i0 + a, i0 + a : i0 + a + 1, :]
                here_ref[i0 + a, x] = value
                for c in range(a + 1, block):
                    accs[c] = accs[c] - table_ref[i0 + a, i0 + c : i0 + c + 1, :] * value
        copy_out(x).start()
        return 0

    lax.fori_loop(0, cx, layer, 0)
    for x in range(cx):
        copy_out(x).wait()


def run_solve(received, chunks):
    counts = tuple(c.shape[0] for c in chunks)
    norb = sum(counts)
    _, cx, cy, cz = chunks[0].shape
    return pl.pallas_call(
        functools.partial(solve_kernel, counts),
        out_shape=jax.ShapeDtypeStruct((norb, cx, cy, cz), jnp.float32),
        in_specs=[pl.BlockSpec(memory_space=pltpu.VMEM)] * (1 + len(chunks)),
        out_specs=pl.BlockSpec(memory_space=pl.ANY),
        scratch_shapes=[
            pltpu.VMEM((norb, cx, cy, cz), jnp.float32),
            pltpu.VMEM((norb, norb, 128), jnp.float32),
            pltpu.SemaphoreType.DMA((cx,)),
        ],
        compiler_params=pltpu.CompilerParams(vmem_limit_bytes=24 * 2**20),
        name="orthonormalize",
    )(received, *chunks)


def body(orbitals, potential):
    norb, cx, cy, cz = orbitals.shape
    chips = axis_count(("gx", "gz"))
    scale = 1.0 / float(chips * CORES * cx * cy * cz)
    blocks = []
    first = first_tiles(orbitals, potential)
    for index, mid in enumerate(all_tiles(orbitals, potential)):
        lo, hi = both_ways(*((first, first) if index == 0 else (mid, mid)), "gx")
        blocks.append((lo, mid, hi))
    diag = None
    filtered, grams, all_sides, alone = [], [], [], {}
    for index, (chunk, start, groups) in enumerate(UNITS):
        unit = (start, groups, index == 0, index in RIDES or index in ALONE)
        if index in AFTER:
            lo, mid, hi = blocks[chunk]
            before = AFTER[index]
            tied = (lo, hi, filtered[before]) + ((grams[before],) if before == 0 else ())
            lo, hi, filtered[before], *rest = lax.optimization_barrier(tied)
            grams[before : before + len(rest)] = rest
            blocks[chunk] = lo, mid, hi
        rider, rider_mid = None, None
        for later, carrier in RIDES.items():
            if carrier == index:
                rider, rider_mid = UNITS[later][1:], blocks[UNITS[later][0]][1]
        low, high = pack_sides(blocks[chunk], unit, CHUNKS[chunk], cx, cy, rider, rider_mid)
        all_sides.append(both_ways(low, high, GY))
        own, own_at = None, 0
        if index in RIDES:
            carrier = RIDES[index]
            own = all_sides[carrier]
            own_at = unit_tiles(cx, UNITS[carrier][1:] + (carrier == 0, carrier in RIDES))
        if index in ALONE:
            own = alone[index]
        for later, by in ALONE.items():
            if by == index:
                part = blocks[UNITS[later][0]][1][UNITS[later][1] * cx * cy :][: cx * cy]
                part = part.reshape((cx, cy) + part.shape[1:])
                rows = [p.reshape((cx * HALO,) + p.shape[2:]) for p in (part[:, :HALO], part[:, cy - HALO :])]
                tied = lax.optimization_barrier(all_sides[index] + both_ways(*rows, GY))
                all_sides[index], alone[later] = tied[:2], tied[2:]
        out, diag = run_filter(blocks[chunk], all_sides[index], unit, CHUNKS[chunk], own, own_at, cx, cy, cz, diag)
        offset = GROUP * sum(g for _, _, g in UNITS[:index])
        filtered.append(out)
        last = index + 1 == len(UNITS)
        grams.append(run_gram(filtered, grams if last else (), offset, norb, scale))
    local = grams[-1]
    other = lax.ppermute(local, "core", [(core, 1 - core) for core in range(CORES)])
    chip = jnp.broadcast_to((local + other)[None], (chips,) + local.shape)
    received = lax.all_to_all(chip, ("gx", "gz"), 0, 0, tiled=True)
    return run_solve(received, filtered)


def solution(mesh):
    count = mesh.shape["gx"], mesh.shape["gy"] // CORES, CORES
    split = jax.sharding.Mesh(mesh.devices.reshape(count), ("gx",) + GY)
    placed = (P(None, "gx", GY, None), P("gx", GY, None))
    return jax.shard_map(
        body, mesh=split, in_specs=placed, out_specs=P(None, "gx", GY, None), check_vma=False
    )
```

```python
import functools
import math

import jax
import jax.numpy as jnp
from jax import lax
from jax.experimental import pallas as pl
from jax.experimental.pallas import tpu as pltpu
from jax.sharding import PartitionSpec as P

DEG = 4
HALO = 2 * DEG
CENTER = 5.0
HALF_W = 4.0
NEAR = (2.0 / HALF_W) * -0.5 * (4.0 / 3.0)
FAR = (2.0 / HALF_W) * 0.5 / 12.0
DIAG_SCALE = 2.0 / HALF_W
DIAG_SHIFT = (2.0 / HALF_W) * (3 * 0.5 * 2.5 - CENTER)

GROUP = 8
PREP_VMEM = 59 * 2**20
CHUNKS = (1, 2, 1)
UNITS = ((0, 0, 1), (1, 0, 1), (1, 1, 1), (2, 0, 1))
AFTER = {1: 0, 3: 1}
RIDES = {}
ALONE = (1,)
FILTER_COST = 100
GY = ("gz", "core")
CORES = 2


def axis_count(axis):
    return math.prod(lax.axis_size(a) for a in ((axis,) if isinstance(axis, str) else axis))


def shift_perm(axis, step):
    count = axis_count(axis)
    return [(i, (i + step) % count) for i in range(count)]


def both_ways(low_part, high_part, axis):
    return (
        lax.ppermute(high_part, axis, shift_perm(axis, 1)),
        lax.ppermute(low_part, axis, shift_perm(axis, -1)),
    )


def reach(plane, cx, left):
    outside = max(HALO - plane, plane - (HALO + cx - 1), 0)
    return left - 2 * ((outside + 1) // 2)


def halo_planes(cx, late=False):
    planes = []
    for plane in range(2, cx + 2 * HALO - 2):
        if late and HALO <= plane < HALO + cx:
            continue
        planes.append((plane, reach(plane, cx, HALO)))
    return planes


def diag_planes(cx):
    return range(4, cx + 2 * HALO - 4)


def split_plane(plane, cx):
    if plane < HALO:
        return 0, plane
    if plane < HALO + cx:
        return 1, plane - HALO
    return 2, plane - HALO - cx


def tile_block(out_ref, at, block):
    out_ref[at : at + block.shape[1]] = jnp.swapaxes(block, 0, 1)


def first_tiles_kernel(groups, pieces, pot_ref, orb_ref, out_ref, pot_here, here, tiles, in_sems, out_sems):
    cx, cy, cz = pot_ref.shape
    pot_copy = pltpu.make_async_copy(pot_ref, pot_here, in_sems.at[groups * pieces])
    pot_copy.start()
    deep = cx // pieces
    parts = [(g, p) for g in range(groups) for p in range(pieces)]
    loads, stores = [], []
    for index, (g, p) in enumerate(parts):
        part = (pl.ds(GROUP * g, GROUP), pl.ds(deep * p, deep))
        loads.append(pltpu.make_async_copy(orb_ref.at[part], here.at[part], in_sems.at[index]))
        loads[-1].start()

    def store(index, start, size):
        rows = pl.ds(start, size)
        stores.append(pltpu.make_async_copy(tiles.at[rows], out_ref.at[rows], out_sems.at[index]))
        stores[-1].start()

    pot_copy.wait()
    tiles[groups * cx * cy :] = pot_here[...].reshape(cx * cy // 8, 8, cz)
    store(groups * pieces, groups * cx * cy, cx * cy // 8)
    for index, (g, p) in enumerate(parts):
        loads[index].wait()
        for x in range(deep * p, deep * (p + 1)):
            tile_block(tiles, g * cx * cy + x * cy, here[GROUP * g : GROUP * (g + 1), x])
        store(index, g * cx * cy + deep * p * cy, deep * cy)
    for copy in stores:
        copy.wait()


def first_tiles(orbitals, potential):
    _, cx, cy, cz = orbitals.shape
    groups, pieces = CHUNKS[0], 2
    tiles = (groups * cx * cy + cx * cy // 8, 8, cz)
    return pl.pallas_call(
        functools.partial(first_tiles_kernel, groups, pieces),
        out_shape=jax.ShapeDtypeStruct(tiles, jnp.float32),
        in_specs=[pl.BlockSpec(memory_space=pltpu.HBM)] * 2,
        out_specs=pl.BlockSpec(memory_space=pltpu.HBM),
        scratch_shapes=[
            pltpu.VMEM((cx, cy, cz), jnp.float32),
            pltpu.VMEM((groups * GROUP, cx, cy, cz), jnp.float32),
            pltpu.VMEM(tiles, jnp.float32),
            pltpu.SemaphoreType.DMA((groups * pieces + 1,)),
            pltpu.SemaphoreType.DMA((groups * pieces + 1,)),
        ],
        compiler_params=pltpu.CompilerParams(vmem_limit_bytes=PREP_VMEM),
        name="first_tiles",
    )(potential, orbitals)


def tiles_kernel(chunks, pot_ref, orb_ref, *out_refs):
    cx, cy, cz = pot_ref.shape
    group = 0
    for out_ref, groups in zip(out_refs, chunks):
        for g in range(groups):
            for x in range(cx):
                tile_block(out_ref, g * cx * cy + x * cy, orb_ref[GROUP * group : GROUP * (group + 1), x])
            group += 1
    out_refs[0][chunks[0] * cx * cy :] = pot_ref[...].reshape(cx * cy // 8, 8, cz)


def all_tiles(orbitals, potential):
    _, cx, cy, cz = orbitals.shape
    tiles = [groups * cx * cy for groups in CHUNKS]
    tiles[0] += cx * cy // 8
    return pl.pallas_call(
        functools.partial(tiles_kernel, CHUNKS),
        out_shape=[jax.ShapeDtypeStruct((t, 8, cz), jnp.float32) for t in tiles],
        in_specs=[pl.BlockSpec(memory_space=pltpu.VMEM)] * 2,
        out_specs=[pl.BlockSpec(memory_space=pltpu.VMEM)] * len(tiles),
        compiler_params=pltpu.CompilerParams(vmem_limit_bytes=16 * 2**20),
        name="all_tiles",
    )(potential, orbitals)


def sides_kernel(unit, chunk_groups, rider, cx, cy, *refs):
    low_ref, high_ref = refs[-2:]
    start, groups, first, late = unit
    at = 0
    for g in range(start, start + groups):
        for plane, rows in halo_planes(cx, late):
            which, x = split_plane(plane, cx)
            base = g * cx * cy + x * cy
            low_ref[at : at + rows] = refs[which][base : base + rows]
            high_ref[at : at + rows] = refs[which][base + cy - rows : base + cy]
            at += rows
    if first:
        per = cy // 8
        for plane in diag_planes(cx):
            which, x = split_plane(plane, cx)
            base = chunk_groups * cx * cy + x * per
            low_ref[at] = refs[which][base]
            high_ref[at] = refs[which][base + per - 1]
            at += 1
    if rider is not None:
        for g in range(rider[0], rider[0] + rider[1]):
            for x in range(cx):
                base = g * cx * cy + x * cy
                low_ref[at : at + HALO] = refs[3][base : base + HALO]
                high_ref[at : at + HALO] = refs[3][base + cy - HALO : base + cy]
                at += HALO


def unit_tiles(cx, unit):
    _, groups, first, late = unit
    return groups * sum(rows for _, rows in halo_planes(cx, late)) + (len(diag_planes(cx)) if first else 0)


def pack_sides(blocks, unit, chunk_groups, cx, cy, rider, rider_mid):
    tiles = unit_tiles(cx, unit) + (0 if rider is None else rider[1] * cx * HALO)
    shape = jax.ShapeDtypeStruct((tiles,) + blocks[0].shape[1:], jnp.float32)
    operands = blocks + (() if rider is None else (rider_mid,))
    return pl.pallas_call(
        functools.partial(sides_kernel, unit, chunk_groups, rider, cx, cy),
        out_shape=(shape, shape),
        in_specs=[pl.BlockSpec(memory_space=pltpu.VMEM)] * len(operands),
        out_specs=(pl.BlockSpec(memory_space=pltpu.VMEM),) * 2,
        compiler_params=pltpu.CompilerParams(vmem_limit_bytes=16 * 2**20),
        cost_estimate=pl.CostEstimate(flops=0, bytes_accessed=1_000_000, transcendentals=0),
        name="pack_sides",
    )(*operands)


def z_circulant(cz):
    row = lax.broadcasted_iota(jnp.int32, (cz, cz), 0)
    col = lax.broadcasted_iota(jnp.int32, (cz, cz), 1)
    gap = jnp.where(row >= col, row - col, row - col + cz)
    near = (gap == 1) | (gap == cz - 1)
    far = (gap == 2) | (gap == cz - 2)
    return jnp.where(near, -16.0, jnp.where(far, 1.0, 0.0)).astype(jnp.bfloat16)


def z_part(center, matrix):
    flat = center.reshape(-1, center.shape[-1])
    high = flat.astype(jnp.bfloat16)
    rest = flat - high.astype(jnp.float32)
    middle = rest.astype(jnp.bfloat16)
    low = (rest - middle.astype(jnp.float32)).astype(jnp.bfloat16)

    def times(part):
        return jnp.dot(part, matrix, preferred_element_type=jnp.float32)

    return (times(high) + (times(middle) + times(low))).reshape(center.shape)


def four_steps(cx, cy, chain, diag_ref, out_ref):
    total = cx + 2 * HALO
    matrix = z_circulant(out_ref.shape[-1])
    for step in range(DEG):
        source = chain[step]
        left = HALO - 2 * (step + 1)
        for plane in range(total):
            rows = reach(plane, cx, left)
            if rows < 0:
                continue
            first, count = HALO - rows, cy + 2 * rows
            here = slice(first, first + count)
            column = source[plane, first - 2 : first + count + 2]
            center = column[2:-2]
            near = (column[1:-3] + column[3:-1]) + (source[plane - 1, here] + source[plane + 1, here])
            far = (column[:-4] + column[4:]) + (source[plane - 2, here] + source[plane + 2, here])
            applied = diag_ref[plane, here][:, None, :] * center + FAR * ((z_part(center, matrix) + far) - 16.0 * near)
            fresh = 0.5 * applied if step == 0 else applied - chain[step - 1][plane, here]
            if step < DEG - 1:
                chain[step + 1][plane, here] = fresh
            else:
                out_ref[:, plane - HALO] = jnp.swapaxes(fresh, 0, 1)


def fill_blocks(cx, cy, base, sources, ext_ref):
    for x in range(cx):
        for which in range(3):
            ext_ref[which * cx + x, HALO : HALO + cy] = sources[which][pl.ds(base + x * cy, cy)]


def filter_kernel(unit, chunk_groups, own_at, cx, cy, lo_ref, mid_ref, hi_ref, yl_ref, yh_ref, *refs):
    start, groups, first, late = unit
    group = pl.program_id(0)
    sources = (lo_ref, mid_ref, hi_ref)
    planes = halo_planes(cx, late)
    side = sum(rows for _, rows in planes)
    if first:
        out_ref, diag_ref = refs[:2]

        @pl.when(group == 0)
        def _():
            per = cy // 8
            cz = out_ref.shape[-1]
            for x in range(cx):
                for which in range(3):
                    base = chunk_groups * cx * cy + x * per
                    block = sources[which][base : base + per].reshape(cy, cz)
                    diag_ref[which * cx + x, HALO : HALO + cy] = DIAG_SCALE * block + DIAG_SHIFT
            at = groups * side
            for plane in diag_planes(cx):
                diag_ref[plane, 0:HALO] = DIAG_SCALE * yl_ref[at] + DIAG_SHIFT
                diag_ref[plane, HALO + cy :] = DIAG_SCALE * yh_ref[at] + DIAG_SHIFT
                at += 1
    else:
        diag_ref, out_ref = refs[-6:-4]
    chain = refs[-4:]
    if late:
        for x in range(cx):
            base = own_at + group * cx * HALO + x * HALO
            chain[0][HALO + x, 0:HALO] = refs[0][pl.ds(base, HALO)]
            chain[0][HALO + x, HALO + cy :] = refs[1][pl.ds(base, HALO)]
    for x in range(cx):
        for which in range(3):
            tiles = sources[which][pl.ds((start + group) * cx * cy + x * cy, cy)]
            chain[0][which * cx + x, HALO : HALO + cy] = tiles
    at = 0
    for plane, rows in planes:
        chain[0][plane, HALO - rows : HALO] = yl_ref[pl.ds(group * side + at, rows)]
        chain[0][plane, HALO + cy : HALO + cy + rows] = yh_ref[pl.ds(group * side + at, rows)]
        at += rows
    four_steps(cx, cy, chain, diag_ref, out_ref)


def run_filter(blocks, sides, unit, chunk_groups, own, own_at, cx, cy, cz, diag):
    _, groups, first, late = unit
    ext = (cx + 2 * HALO, cy + 2 * HALO, GROUP, cz)
    out_shape = [jax.ShapeDtypeStruct((groups * GROUP, cx, cy, cz), jnp.float32)]
    out_specs = [pl.BlockSpec((GROUP, cx, cy, cz), lambda g: (g, 0, 0, 0))]
    operands = blocks + sides + (own if late else ())
    if first:
        wide = (cx + 2 * HALO, cy + 2 * HALO, cz)
        out_shape.append(jax.ShapeDtypeStruct(wide, jnp.float32))
        out_specs.append(pl.BlockSpec(wide, lambda g: (0, 0, 0)))
    else:
        operands = operands + (diag,)
    got = pl.pallas_call(
        functools.partial(filter_kernel, unit, chunk_groups, own_at, cx, cy),
        grid=(groups,),
        out_shape=out_shape,
        in_specs=[pl.BlockSpec(memory_space=pltpu.VMEM)] * len(operands),
        out_specs=out_specs,
        scratch_shapes=[pltpu.VMEM(ext, jnp.float32)] * 4,
        compiler_params=pltpu.CompilerParams(vmem_limit_bytes=32 * 2**20),
        cost_estimate=pl.CostEstimate(flops=0, bytes_accessed=groups * FILTER_COST, transcendentals=0),
        name="filter_orbitals",
    )(*operands)
    return got if first else (got[0], diag)


def gram_kernel(offset, scale, counts, *refs):
    chunks, earlier, out_ref, rows_ref = refs[: len(counts)], refs[len(counts) : -2], refs[-2], refs[-1]
    own = chunks[-1]
    count, cx, cy, cz = own.shape
    norb = rows_ref.shape[1]
    rows = []
    for ref, size in zip(chunks, counts):
        for at in range(size):
            rows.append((ref, at))
    rows_ref[...] = jnp.zeros_like(rows_ref)
    block = 4
    for a0 in range(0, count, block):
        a_list = list(range(a0, min(a0 + block, count)))
        last = offset + a_list[-1]
        for j0 in range(0, last + 1, block):
            j_list = list(range(j0, min(j0 + block, last + 1)))
            accs = [None] * (len(a_list) * len(j_list))
            for x in range(cx):
                left = [own[a, x] for a in a_list]
                right = [rows[j][0][rows[j][1], x] for j in j_list]
                at = 0
                for l in left:
                    for r in right:
                        prod = l * r
                        prod = prod[:8] + prod[8:]
                        accs[at] = prod if accs[at] is None else accs[at] + prod
                        at += 1
            at = 0
            for a in a_list:
                for j in j_list:
                    rows_ref[a, j : j + 1, :] = jnp.sum(accs[at], axis=0, keepdims=True)
                    at += 1
    sums = lax.dot_general(
        jnp.ones((8, cz), jnp.float32), rows_ref[...].reshape(count * norb, cz), (((1,), (1,)), ((), ())),
        precision=lax.Precision.HIGHEST, preferred_element_type=jnp.float32,
    )
    lane = lax.broadcasted_iota(jnp.int32, (8, 128), 1)
    row = lax.broadcasted_iota(jnp.int32, (8, 128), 0)
    per = 128 // norb
    packed = jnp.zeros((8, 128), jnp.float32)
    for a in range(count):
        here, slot = a // per, (offset + a) // 8
        value = pltpu.roll(sums[:, 128 * here : 128 * (here + 1)], (norb * (slot - a % per)) % 128, 1)
        mask = (row == (offset + a) % 8) & (lane >= norb * slot) & (lane < norb * (slot + 1))
        packed = packed + jnp.where(mask, value, 0.0)
    packed = packed * scale
    for ref in earlier:
        packed = packed + ref[...]
    out_ref[...] = packed


def run_gram(chunks, earlier, offset, norb, scale):
    count, cx, cy, cz = chunks[-1].shape
    counts = tuple(c.shape[0] for c in chunks)
    operands = tuple(chunks) + tuple(earlier)
    return pl.pallas_call(
        functools.partial(gram_kernel, offset, scale, counts),
        out_shape=jax.ShapeDtypeStruct((8, 128), jnp.float32),
        in_specs=[pl.BlockSpec(memory_space=pltpu.VMEM)] * len(operands),
        out_specs=pl.BlockSpec(memory_space=pltpu.VMEM),
        scratch_shapes=[pltpu.VMEM((count, norb, cz), jnp.float32)],
        compiler_params=pltpu.CompilerParams(vmem_limit_bytes=24 * 2**20),
        cost_estimate=pl.CostEstimate(flops=0, bytes_accessed=100, transcendentals=0),
        name="gram_rows",
    )(*operands)


def factor_table(gram, table_ref):
    norb = gram.shape[0]
    columns = [jnp.broadcast_to(gram[:, j : j + 1], (norb, 128)) for j in range(norb)]
    row = lax.broadcasted_iota(jnp.int32, (norb, 128), 0)
    for k in range(norb):
        scale = 1.0 / jnp.sqrt(columns[k][k : k + 1])
        column = columns[k] * scale
        table_ref[k] = jnp.where(row == k, scale, column)
        for j in range(k + 1, norb):
            top = 8 * (j // 8)
            fresh = columns[j][top:] - column[top:] * column[j : j + 1]
            columns[j] = fresh if top == 0 else jnp.concatenate([jnp.zeros((top, 128), jnp.float32), fresh], axis=0)


def solve_kernel(counts, recv_ref, *refs):
    norb = sum(counts)
    chunks, (out_ref, here_ref, table_ref, sems) = refs[: len(counts)], refs[len(counts) :]
    packed = jnp.sum(recv_ref[...], axis=0)
    rows = jnp.concatenate([packed] + [jnp.roll(packed, -norb * q, 1) for q in range(1, 4)], axis=0)
    factor_table(rows, table_ref)
    where = []
    for ref, count in zip(chunks, counts):
        for at in range(count):
            where.append((ref, at))
    block = 8
    cx = here_ref.shape[1]

    def copy_out(x):
        return pltpu.make_async_copy(here_ref.at[:, x], out_ref.at[:, x], sems.at[x])

    def layer(x, _):
        for i0 in range(0, norb, block):
            accs = [where[i0 + a][0][where[i0 + a][1], x] for a in range(block)]
            for j in range(i0):
                value = here_ref[j, x]
                for a in range(block):
                    accs[a] = accs[a] - table_ref[j, i0 + a : i0 + a + 1, :] * value
            for a in range(block):
                value = accs[a] * table_ref[i0 + a, i0 + a : i0 + a + 1, :]
                here_ref[i0 + a, x] = value
                for c in range(a + 1, block):
                    accs[c] = accs[c] - table_ref[i0 + a, i0 + c : i0 + c + 1, :] * value
        copy_out(x).start()
        return 0

    lax.fori_loop(0, cx, layer, 0)
    for x in range(cx):
        copy_out(x).wait()


def run_solve(received, chunks):
    counts = tuple(c.shape[0] for c in chunks)
    norb = sum(counts)
    _, cx, cy, cz = chunks[0].shape
    return pl.pallas_call(
        functools.partial(solve_kernel, counts),
        out_shape=jax.ShapeDtypeStruct((norb, cx, cy, cz), jnp.float32),
        in_specs=[pl.BlockSpec(memory_space=pltpu.VMEM)] * (1 + len(chunks)),
        out_specs=pl.BlockSpec(memory_space=pl.ANY),
        scratch_shapes=[
            pltpu.VMEM((norb, cx, cy, cz), jnp.float32),
            pltpu.VMEM((norb, norb, 128), jnp.float32),
            pltpu.SemaphoreType.DMA((cx,)),
        ],
        compiler_params=pltpu.CompilerParams(vmem_limit_bytes=24 * 2**20),
        name="orthonormalize",
    )(received, *chunks)


def body(orbitals, potential):
    norb, cx, cy, cz = orbitals.shape
    chips = axis_count(("gx", "gz"))
    scale = 1.0 / float(chips * CORES * cx * cy * cz)
    blocks = []
    first = first_tiles(orbitals, potential)
    for index, mid in enumerate(all_tiles(orbitals, potential)):
        lo, hi = both_ways(*((first, first) if index == 0 else (mid, mid)), "gx")
        blocks.append((lo, mid, hi))
    diag = None
    filtered, grams, all_sides, alone = [], [], [], {}
    for index, (chunk, start, groups) in enumerate(UNITS):
        unit = (start, groups, index == 0, index in RIDES or index in ALONE)
        if index in AFTER:
            lo, mid, hi = blocks[chunk]
            before = AFTER[index]
            tied = (lo, hi, filtered[before]) + ((grams[before],) if before == 0 else ())
            if index in ALONE:
                part = mid[start * cx * cy :][: cx * cy].reshape((cx, cy) + mid.shape[1:])
                rows = [p.reshape((cx * HALO,) + p.shape[2:]) for p in (part[:, :HALO], part[:, cy - HALO :])]
                tied = both_ways(*rows, GY) + tied
            tied = lax.optimization_barrier(tied)
            if index in ALONE:
                alone[index], tied = tied[:2], tied[2:]
            lo, hi, filtered[before], *rest = tied
            grams[before : before + len(rest)] = rest
            blocks[chunk] = lo, mid, hi
        rider, rider_mid = None, None
        for later, carrier in RIDES.items():
            if carrier == index:
                rider, rider_mid = UNITS[later][1:], blocks[UNITS[later][0]][1]
        low, high = pack_sides(blocks[chunk], unit, CHUNKS[chunk], cx, cy, rider, rider_mid)
        all_sides.append(both_ways(low, high, GY))
        own, own_at = None, 0
        if index in RIDES:
            carrier = RIDES[index]
            own = all_sides[carrier]
            own_at = unit_tiles(cx, UNITS[carrier][1:] + (carrier == 0, carrier in RIDES))
        if index in ALONE:
            own = alone[index]
        out, diag = run_filter(blocks[chunk], all_sides[index], unit, CHUNKS[chunk], own, own_at, cx, cy, cz, diag)
        offset = GROUP * sum(g for _, _, g in UNITS[:index])
        filtered.append(out)
        last = index + 1 == len(UNITS)
        grams.append(run_gram(filtered, grams if last else (), offset, norb, scale))
    local = grams[-1]
    other = lax.ppermute(local, "core", [(core, 1 - core) for core in range(CORES)])
    chip = jnp.broadcast_to((local + other)[None], (chips,) + local.shape)
    received = lax.all_to_all(chip, ("gx", "gz"), 0, 0, tiled=True)
    return run_solve(received, filtered)


def solution(mesh):
    count = mesh.shape["gx"], mesh.shape["gy"] // CORES, CORES
    split = jax.sharding.Mesh(mesh.devices.reshape(count), ("gx",) + GY)
    placed = (P(None, "gx", GY, None), P("gx", GY, None))
    return jax.shard_map(
        body, mesh=split, in_specs=placed, out_specs=P(None, "gx", GY, None), check_vma=False
    )
```

```python
import functools
import math

import jax
import jax.numpy as jnp
from jax import lax
from jax.experimental import pallas as pl
from jax.experimental.pallas import tpu as pltpu
from jax.sharding import PartitionSpec as P

DEG = 4
HALO = 2 * DEG
CENTER = 5.0
HALF_W = 4.0
NEAR = (2.0 / HALF_W) * -0.5 * (4.0 / 3.0)
FAR = (2.0 / HALF_W) * 0.5 / 12.0
DIAG_SCALE = 2.0 / HALF_W
DIAG_SHIFT = (2.0 / HALF_W) * (3 * 0.5 * 2.5 - CENTER)

GROUP = 8
PREP_VMEM = 59 * 2**20
CHUNKS = (1, 2, 1)
UNITS = ((0, 0, 1), (1, 0, 1), (1, 1, 1), (2, 0, 1))
AFTER = {1: 0, 3: 1}
RIDES = {}
ALONE = (1,)
FILTER_COST = 100
GY = ("gz", "core")
CORES = 2


def axis_count(axis):
    return math.prod(lax.axis_size(a) for a in ((axis,) if isinstance(axis, str) else axis))


def shift_perm(axis, step):
    count = axis_count(axis)
    return [(i, (i + step) % count) for i in range(count)]


def both_ways(low_part, high_part, axis):
    return (
        lax.ppermute(high_part, axis, shift_perm(axis, 1)),
        lax.ppermute(low_part, axis, shift_perm(axis, -1)),
    )


def reach(plane, cx, left):
    outside = max(HALO - plane, plane - (HALO + cx - 1), 0)
    return left - 2 * ((outside + 1) // 2)


def halo_planes(cx, late=False):
    planes = []
    for plane in range(2, cx + 2 * HALO - 2):
        if late and HALO <= plane < HALO + cx:
            continue
        planes.append((plane, reach(plane, cx, HALO)))
    return planes


def diag_planes(cx):
    return range(4, cx + 2 * HALO - 4)


def split_plane(plane, cx):
    if plane < HALO:
        return 0, plane
    if plane < HALO + cx:
        return 1, plane - HALO
    return 2, plane - HALO - cx


def tile_block(out_ref, at, block):
    out_ref[at : at + block.shape[1]] = jnp.swapaxes(block, 0, 1)


def first_tiles_kernel(groups, pieces, pot_ref, orb_ref, out_ref, pot_here, here, tiles, in_sems, out_sems):
    cx, cy, cz = pot_ref.shape
    pot_copy = pltpu.make_async_copy(pot_ref, pot_here, in_sems.at[groups * pieces])
    pot_copy.start()
    deep = cx // pieces
    parts = [(g, p) for g in range(groups) for p in range(pieces)]
    loads, stores = [], []
    for index, (g, p) in enumerate(parts):
        part = (pl.ds(GROUP * g, GROUP), pl.ds(deep * p, deep))
        loads.append(pltpu.make_async_copy(orb_ref.at[part], here.at[part], in_sems.at[index]))
        loads[-1].start()

    def store(index, start, size):
        rows = pl.ds(start, size)
        stores.append(pltpu.make_async_copy(tiles.at[rows], out_ref.at[rows], out_sems.at[index]))
        stores[-1].start()

    pot_copy.wait()
    tiles[groups * cx * cy :] = pot_here[...].reshape(cx * cy // 8, 8, cz)
    store(groups * pieces, groups * cx * cy, cx * cy // 8)
    for index, (g, p) in enumerate(parts):
        loads[index].wait()
        for x in range(deep * p, deep * (p + 1)):
            tile_block(tiles, g * cx * cy + x * cy, here[GROUP * g : GROUP * (g + 1), x])
        store(index, g * cx * cy + deep * p * cy, deep * cy)
    for copy in stores:
        copy.wait()


def first_tiles(orbitals, potential):
    _, cx, cy, cz = orbitals.shape
    groups, pieces = CHUNKS[0], 2
    tiles = (groups * cx * cy + cx * cy // 8, 8, cz)
    return pl.pallas_call(
        functools.partial(first_tiles_kernel, groups, pieces),
        out_shape=jax.ShapeDtypeStruct(tiles, jnp.float32),
        in_specs=[pl.BlockSpec(memory_space=pltpu.HBM)] * 2,
        out_specs=pl.BlockSpec(memory_space=pltpu.HBM),
        scratch_shapes=[
            pltpu.VMEM((cx, cy, cz), jnp.float32),
            pltpu.VMEM((groups * GROUP, cx, cy, cz), jnp.float32),
            pltpu.VMEM(tiles, jnp.float32),
            pltpu.SemaphoreType.DMA((groups * pieces + 1,)),
            pltpu.SemaphoreType.DMA((groups * pieces + 1,)),
        ],
        compiler_params=pltpu.CompilerParams(vmem_limit_bytes=PREP_VMEM),
        name="first_tiles",
    )(potential, orbitals)


def tiles_kernel(chunks, pot_ref, orb_ref, *out_refs):
    cx, cy, cz = pot_ref.shape
    group = 0
    for out_ref, groups in zip(out_refs, chunks):
        for g in range(groups):
            for x in range(cx):
                tile_block(out_ref, g * cx * cy + x * cy, orb_ref[GROUP * group : GROUP * (group + 1), x])
            group += 1
    out_refs[0][chunks[0] * cx * cy :] = pot_ref[...].reshape(cx * cy // 8, 8, cz)


def all_tiles(orbitals, potential):
    _, cx, cy, cz = orbitals.shape
    tiles = [groups * cx * cy for groups in CHUNKS]
    tiles[0] += cx * cy // 8
    return pl.pallas_call(
        functools.partial(tiles_kernel, CHUNKS),
        out_shape=[jax.ShapeDtypeStruct((t, 8, cz), jnp.float32) for t in tiles],
        in_specs=[pl.BlockSpec(memory_space=pltpu.VMEM)] * 2,
        out_specs=[pl.BlockSpec(memory_space=pltpu.VMEM)] * len(tiles),
        compiler_params=pltpu.CompilerParams(vmem_limit_bytes=16 * 2**20),
        name="all_tiles",
    )(potential, orbitals)


def sides_kernel(unit, chunk_groups, rider, cx, cy, *refs):
    low_ref, high_ref = refs[-2:]
    start, groups, first, late = unit
    at = 0
    for g in range(start, start + groups):
        for plane, rows in halo_planes(cx, late):
            which, x = split_plane(plane, cx)
            base = g * cx * cy + x * cy
            low_ref[at : at + rows] = refs[which][base : base + rows]
            high_ref[at : at + rows] = refs[which][base + cy - rows : base + cy]
            at += rows
    if first:
        per = cy // 8
        for plane in diag_planes(cx):
            which, x = split_plane(plane, cx)
            base = chunk_groups * cx * cy + x * per
            low_ref[at] = refs[which][base]
            high_ref[at] = refs[which][base + per - 1]
            at += 1
    if rider is not None:
        for g in range(rider[0], rider[0] + rider[1]):
            for x in range(cx):
                base = g * cx * cy + x * cy
                low_ref[at : at + HALO] = refs[3][base : base + HALO]
                high_ref[at : at + HALO] = refs[3][base + cy - HALO : base + cy]
                at += HALO


def unit_tiles(cx, unit):
    _, groups, first, late = unit
    return groups * sum(rows for _, rows in halo_planes(cx, late)) + (len(diag_planes(cx)) if first else 0)


def pack_sides(blocks, unit, chunk_groups, cx, cy, rider, rider_mid):
    tiles = unit_tiles(cx, unit) + (0 if rider is None else rider[1] * cx * HALO)
    shape = jax.ShapeDtypeStruct((tiles,) + blocks[0].shape[1:], jnp.float32)
    operands = blocks + (() if rider is None else (rider_mid,))
    return pl.pallas_call(
        functools.partial(sides_kernel, unit, chunk_groups, rider, cx, cy),
        out_shape=(shape, shape),
        in_specs=[pl.BlockSpec(memory_space=pltpu.VMEM)] * len(operands),
        out_specs=(pl.BlockSpec(memory_space=pltpu.VMEM),) * 2,
        compiler_params=pltpu.CompilerParams(vmem_limit_bytes=16 * 2**20),
        cost_estimate=pl.CostEstimate(flops=0, bytes_accessed=1_000_000, transcendentals=0),
        name="pack_sides",
    )(*operands)


def z_circulant(cz):
    row = lax.broadcasted_iota(jnp.int32, (cz, cz), 0)
    col = lax.broadcasted_iota(jnp.int32, (cz, cz), 1)
    gap = jnp.where(row >= col, row - col, row - col + cz)
    near = (gap == 1) | (gap == cz - 1)
    far = (gap == 2) | (gap == cz - 2)
    return jnp.where(near, -16.0, jnp.where(far, 1.0, 0.0)).astype(jnp.bfloat16)


def z_part(center, matrix):
    flat = center.reshape(-1, center.shape[-1])
    high = flat.astype(jnp.bfloat16)
    rest = flat - high.astype(jnp.float32)
    middle = rest.astype(jnp.bfloat16)
    low = (rest - middle.astype(jnp.float32)).astype(jnp.bfloat16)

    def times(part):
        return jnp.dot(part, matrix, preferred_element_type=jnp.float32)

    return (times(high) + (times(middle) + times(low))).reshape(center.shape)


def four_steps(cx, cy, start, steps, diag_ref, out_ref):
    total = cx + 2 * HALO
    matrix = z_circulant(out_ref.shape[-1])

    def rows_of(ref):
        return lambda plane, a, b: ref[plane, a:b]

    chain = [start] + [rows_of(ref) for ref in steps]
    for step in range(DEG):
        source = chain[step]
        left = HALO - 2 * (step + 1)
        for plane in range(total):
            rows = reach(plane, cx, left)
            if rows < 0:
                continue
            first, last = HALO - rows, HALO + cy + rows
            column = source(plane, first - 2, last + 2)
            center = column[2:-2]
            near = (column[1:-3] + column[3:-1]) + (source(plane - 1, first, last) + source(plane + 1, first, last))
            far = (column[:-4] + column[4:]) + (source(plane - 2, first, last) + source(plane + 2, first, last))
            diag = diag_ref[plane, first:last][:, None, :]
            applied = diag * center + FAR * ((z_part(center, matrix) + far) - 16.0 * near)
            fresh = 0.5 * applied if step == 0 else applied - chain[step - 1](plane, first, last)
            if step < DEG - 1:
                steps[step][plane, first:last] = fresh
            else:
                out_ref[:, plane - HALO] = jnp.swapaxes(fresh, 0, 1)


def filter_kernel(unit, chunk_groups, own_at, cx, cy, lo_ref, mid_ref, hi_ref, yl_ref, yh_ref, *refs):
    start, groups, first, late = unit
    sources = (lo_ref, mid_ref, hi_ref)
    planes = halo_planes(cx, late)
    sides = {}
    at = 0
    for plane, rows in planes:
        sides[plane] = (yl_ref, yh_ref, at, rows)
        at += rows
    if late:
        for x in range(cx):
            sides[HALO + x] = (refs[0], refs[1], own_at + x * HALO, HALO)
    if first:
        out_ref, diag_ref = refs[:2]
        per = cy // 8
        cz = out_ref.shape[-1]
        for x in range(cx):
            for which in range(3):
                base = chunk_groups * cx * cy + x * per
                block = sources[which][base : base + per].reshape(cy, cz)
                diag_ref[which * cx + x, HALO : HALO + cy] = DIAG_SCALE * block + DIAG_SHIFT
        for plane in diag_planes(cx):
            diag_ref[plane, 0:HALO] = DIAG_SCALE * yl_ref[at] + DIAG_SHIFT
            diag_ref[plane, HALO + cy :] = DIAG_SCALE * yh_ref[at] + DIAG_SHIFT
            at += 1
    else:
        diag_ref, out_ref = refs[-5:-3]

    def rows_of(plane, a, b):
        which, x = split_plane(plane, cx)
        base = (start * cx + x) * cy - HALO
        parts = [sources[which][base + max(a, HALO) : base + min(b, HALO + cy)]]
        if a < HALO:
            low, _, at, rows = sides[plane]
            parts.insert(0, low[at + a - (HALO - rows) : at + rows])
        if b > HALO + cy:
            _, high, at, _ = sides[plane]
            parts.append(high[at : at + b - HALO - cy])
        return parts[0] if len(parts) == 1 else jnp.concatenate(parts, axis=0)

    four_steps(cx, cy, rows_of, refs[-3:], diag_ref, out_ref)


def run_filter(blocks, sides, unit, chunk_groups, own, own_at, cx, cy, cz, diag):
    _, groups, first, late = unit
    assert groups == 1
    ext = (cx + 2 * HALO, cy + 2 * HALO, GROUP, cz)
    out_shape = [jax.ShapeDtypeStruct((GROUP, cx, cy, cz), jnp.float32)]
    operands = blocks + sides + (own if late else ())
    if first:
        out_shape.append(jax.ShapeDtypeStruct((cx + 2 * HALO, cy + 2 * HALO, cz), jnp.float32))
    else:
        operands = operands + (diag,)
    got = pl.pallas_call(
        functools.partial(filter_kernel, unit, chunk_groups, own_at, cx, cy),
        out_shape=out_shape,
        in_specs=[pl.BlockSpec(memory_space=pltpu.VMEM)] * len(operands),
        out_specs=[pl.BlockSpec(memory_space=pltpu.VMEM)] * len(out_shape),
        scratch_shapes=[pltpu.VMEM(ext, jnp.float32)] * 3,
        compiler_params=pltpu.CompilerParams(vmem_limit_bytes=32 * 2**20),
        cost_estimate=pl.CostEstimate(flops=0, bytes_accessed=FILTER_COST, transcendentals=0),
        name="filter_orbitals",
    )(*operands)
    return got if first else (got[0], diag)


def gram_kernel(offset, scale, counts, *refs):
    chunks, earlier, out_ref, rows_ref = refs[: len(counts)], refs[len(counts) : -2], refs[-2], refs[-1]
    own = chunks[-1]
    count, cx, cy, cz = own.shape
    norb = rows_ref.shape[1]
    rows = []
    for ref, size in zip(chunks, counts):
        for at in range(size):
            rows.append((ref, at))
    rows_ref[...] = jnp.zeros_like(rows_ref)
    block = 4
    for a0 in range(0, count, block):
        a_list = list(range(a0, min(a0 + block, count)))
        last = offset + a_list[-1]
        for j0 in range(0, last + 1, block):
            j_list = list(range(j0, min(j0 + block, last + 1)))
            accs = [None] * (len(a_list) * len(j_list))
            for x in range(cx):
                left = [own[a, x] for a in a_list]
                right = [rows[j][0][rows[j][1], x] for j in j_list]
                at = 0
                for l in left:
                    for r in right:
                        prod = l * r
                        prod = prod[:8] + prod[8:]
                        accs[at] = prod if accs[at] is None else accs[at] + prod
                        at += 1
            at = 0
            for a in a_list:
                for j in j_list:
                    rows_ref[a, j : j + 1, :] = jnp.sum(accs[at], axis=0, keepdims=True)
                    at += 1
    sums = lax.dot_general(
        jnp.ones((8, cz), jnp.float32), rows_ref[...].reshape(count * norb, cz), (((1,), (1,)), ((), ())),
        precision=lax.Precision.HIGHEST, preferred_element_type=jnp.float32,
    )
    lane = lax.broadcasted_iota(jnp.int32, (8, 128), 1)
    row = lax.broadcasted_iota(jnp.int32, (8, 128), 0)
    per = 128 // norb
    packed = jnp.zeros((8, 128), jnp.float32)
    for a in range(count):
        here, slot = a // per, (offset + a) // 8
        value = pltpu.roll(sums[:, 128 * here : 128 * (here + 1)], (norb * (slot - a % per)) % 128, 1)
        mask = (row == (offset + a) % 8) & (lane >= norb * slot) & (lane < norb * (slot + 1))
        packed = packed + jnp.where(mask, value, 0.0)
    packed = packed * scale
    for ref in earlier:
        packed = packed + ref[...]
    out_ref[...] = packed


def run_gram(chunks, earlier, offset, norb, scale):
    count, cx, cy, cz = chunks[-1].shape
    counts = tuple(c.shape[0] for c in chunks)
    operands = tuple(chunks) + tuple(earlier)
    return pl.pallas_call(
        functools.partial(gram_kernel, offset, scale, counts),
        out_shape=jax.ShapeDtypeStruct((8, 128), jnp.float32),
        in_specs=[pl.BlockSpec(memory_space=pltpu.VMEM)] * len(operands),
        out_specs=pl.BlockSpec(memory_space=pltpu.VMEM),
        scratch_shapes=[pltpu.VMEM((count, norb, cz), jnp.float32)],
        compiler_params=pltpu.CompilerParams(vmem_limit_bytes=24 * 2**20),
        cost_estimate=pl.CostEstimate(flops=0, bytes_accessed=100, transcendentals=0),
        name="gram_rows",
    )(*operands)


def factor_table(gram, table_ref):
    norb = gram.shape[0]
    columns = [jnp.broadcast_to(gram[:, j : j + 1], (norb, 128)) for j in range(norb)]
    row = lax.broadcasted_iota(jnp.int32, (norb, 128), 0)
    for k in range(norb):
        scale = 1.0 / jnp.sqrt(columns[k][k : k + 1])
        column = columns[k] * scale
        table_ref[k] = jnp.where(row == k, scale, column)
        for j in range(k + 1, norb):
            top = 8 * (j // 8)
            fresh = columns[j][top:] - column[top:] * column[j : j + 1]
            columns[j] = fresh if top == 0 else jnp.concatenate([jnp.zeros((top, 128), jnp.float32), fresh], axis=0)


def solve_kernel(counts, recv_ref, *refs):
    norb = sum(counts)
    chunks, (out_ref, here_ref, table_ref, sems) = refs[: len(counts)], refs[len(counts) :]
    packed = jnp.sum(recv_ref[...], axis=0)
    rows = jnp.concatenate([packed] + [jnp.roll(packed, -norb * q, 1) for q in range(1, 4)], axis=0)
    factor_table(rows, table_ref)
    where = []
    for ref, count in zip(chunks, counts):
        for at in range(count):
            where.append((ref, at))
    block = 8
    cx = here_ref.shape[1]

    def copy_out(x):
        return pltpu.make_async_copy(here_ref.at[:, x], out_ref.at[:, x], sems.at[x])

    def layer(x, _):
        for i0 in range(0, norb, block):
            accs = [where[i0 + a][0][where[i0 + a][1], x] for a in range(block)]
            for j in range(i0):
                value = here_ref[j, x]
                for a in range(block):
                    accs[a] = accs[a] - table_ref[j, i0 + a : i0 + a + 1, :] * value
            for a in range(block):
                value = accs[a] * table_ref[i0 + a, i0 + a : i0 + a + 1, :]
                here_ref[i0 + a, x] = value
                for c in range(a + 1, block):
                    accs[c] = accs[c] - table_ref[i0 + a, i0 + c : i0 + c + 1, :] * value
        copy_out(x).start()
        return 0

    lax.fori_loop(0, cx, layer, 0)
    for x in range(cx):
        copy_out(x).wait()


def run_solve(received, chunks):
    counts = tuple(c.shape[0] for c in chunks)
    norb = sum(counts)
    _, cx, cy, cz = chunks[0].shape
    return pl.pallas_call(
        functools.partial(solve_kernel, counts),
        out_shape=jax.ShapeDtypeStruct((norb, cx, cy, cz), jnp.float32),
        in_specs=[pl.BlockSpec(memory_space=pltpu.VMEM)] * (1 + len(chunks)),
        out_specs=pl.BlockSpec(memory_space=pl.ANY),
        scratch_shapes=[
            pltpu.VMEM((norb, cx, cy, cz), jnp.float32),
            pltpu.VMEM((norb, norb, 128), jnp.float32),
            pltpu.SemaphoreType.DMA((cx,)),
        ],
        compiler_params=pltpu.CompilerParams(vmem_limit_bytes=24 * 2**20),
        name="orthonormalize",
    )(received, *chunks)


def body(orbitals, potential):
    norb, cx, cy, cz = orbitals.shape
    chips = axis_count(("gx", "gz"))
    scale = 1.0 / float(chips * CORES * cx * cy * cz)
    blocks = []
    first = first_tiles(orbitals, potential)
    for index, mid in enumerate(all_tiles(orbitals, potential)):
        lo, hi = both_ways(*((first, first) if index == 0 else (mid, mid)), "gx")
        blocks.append((lo, mid, hi))
    diag = None
    filtered, grams, all_sides, alone = [], [], [], {}
    for index, (chunk, start, groups) in enumerate(UNITS):
        unit = (start, groups, index == 0, index in RIDES or index in ALONE)
        if index in AFTER:
            lo, mid, hi = blocks[chunk]
            before = AFTER[index]
            tied = (lo, hi, filtered[before]) + ((grams[before],) if before == 0 else ())
            if index in ALONE:
                part = mid[start * cx * cy :][: cx * cy].reshape((cx, cy) + mid.shape[1:])
                rows = [p.reshape((cx * HALO,) + p.shape[2:]) for p in (part[:, :HALO], part[:, cy - HALO :])]
                tied = both_ways(*rows, GY) + tied
            tied = lax.optimization_barrier(tied)
            if index in ALONE:
                alone[index], tied = tied[:2], tied[2:]
            lo, hi, filtered[before], *rest = tied
            grams[before : before + len(rest)] = rest
            blocks[chunk] = lo, mid, hi
        rider, rider_mid = None, None
        for later, carrier in RIDES.items():
            if carrier == index:
                rider, rider_mid = UNITS[later][1:], blocks[UNITS[later][0]][1]
        low, high = pack_sides(blocks[chunk], unit, CHUNKS[chunk], cx, cy, rider, rider_mid)
        all_sides.append(both_ways(low, high, GY))
        own, own_at = None, 0
        if index in RIDES:
            carrier = RIDES[index]
            own = all_sides[carrier]
            own_at = unit_tiles(cx, UNITS[carrier][1:] + (carrier == 0, carrier in RIDES))
        if index in ALONE:
            own = alone[index]
        out, diag = run_filter(blocks[chunk], all_sides[index], unit, CHUNKS[chunk], own, own_at, cx, cy, cz, diag)
        offset = GROUP * sum(g for _, _, g in UNITS[:index])
        filtered.append(out)
        last = index + 1 == len(UNITS)
        grams.append(run_gram(filtered, grams if last else (), offset, norb, scale))
    local = grams[-1]
    other = lax.ppermute(local, "core", [(core, 1 - core) for core in range(CORES)])
    chip = jnp.broadcast_to((local + other)[None], (chips,) + local.shape)
    received = lax.all_to_all(chip, ("gx", "gz"), 0, 0, tiled=True)
    return run_solve(received, filtered)


def solution(mesh):
    count = mesh.shape["gx"], mesh.shape["gy"] // CORES, CORES
    split = jax.sharding.Mesh(mesh.devices.reshape(count), ("gx",) + GY)
    placed = (P(None, "gx", GY, None), P("gx", GY, None))
    return jax.shard_map(
        body, mesh=split, in_specs=placed, out_specs=P(None, "gx", GY, None), check_vma=False
    )
```

```python
import functools
import math

import jax
import jax.numpy as jnp
from jax import lax
from jax.experimental import pallas as pl
from jax.experimental.pallas import tpu as pltpu
from jax.sharding import PartitionSpec as P

DEG = 4
HALO = 2 * DEG
CENTER = 5.0
HALF_W = 4.0
NEAR = (2.0 / HALF_W) * -0.5 * (4.0 / 3.0)
FAR = (2.0 / HALF_W) * 0.5 / 12.0
DIAG_SCALE = 2.0 / HALF_W
DIAG_SHIFT = (2.0 / HALF_W) * (3 * 0.5 * 2.5 - CENTER)

GROUP = 8
PREP_VMEM = 59 * 2**20
CHUNKS = (1, 2, 1)
UNITS = ((0, 0, 1), (1, 0, 1), (1, 1, 1), (2, 0, 1))
AFTER = {1: 0, 3: 1}
RIDES = {}
ALONE = (0, 1)
FILTER_COST = 100
GY = ("gz", "core")
CORES = 2


def axis_count(axis):
    return math.prod(lax.axis_size(a) for a in ((axis,) if isinstance(axis, str) else axis))


def shift_perm(axis, step):
    count = axis_count(axis)
    return [(i, (i + step) % count) for i in range(count)]


def both_ways(low_part, high_part, axis):
    return (
        lax.ppermute(high_part, axis, shift_perm(axis, 1)),
        lax.ppermute(low_part, axis, shift_perm(axis, -1)),
    )


def reach(plane, cx, left):
    outside = max(HALO - plane, plane - (HALO + cx - 1), 0)
    return left - 2 * ((outside + 1) // 2)


def halo_planes(cx, late=False):
    planes = []
    for plane in range(2, cx + 2 * HALO - 2):
        if late and HALO <= plane < HALO + cx:
            continue
        planes.append((plane, reach(plane, cx, HALO)))
    return planes


def diag_planes(cx):
    return range(4, cx + 2 * HALO - 4)


def split_plane(plane, cx):
    if plane < HALO:
        return 0, plane
    if plane < HALO + cx:
        return 1, plane - HALO
    return 2, plane - HALO - cx


def tile_block(out_ref, at, block):
    out_ref[at : at + block.shape[1]] = jnp.swapaxes(block, 0, 1)


def first_tiles_kernel(groups, pieces, pot_ref, orb_ref, out_ref, pot_here, here, tiles, in_sems, out_sems):
    cx, cy, cz = pot_ref.shape
    pot_copy = pltpu.make_async_copy(pot_ref, pot_here, in_sems.at[groups * pieces])
    pot_copy.start()
    deep = cx // pieces
    parts = [(g, p) for g in range(groups) for p in range(pieces)]
    loads, stores = [], []
    for index, (g, p) in enumerate(parts):
        part = (pl.ds(GROUP * g, GROUP), pl.ds(deep * p, deep))
        loads.append(pltpu.make_async_copy(orb_ref.at[part], here.at[part], in_sems.at[index]))
        loads[-1].start()

    def store(index, start, size):
        rows = pl.ds(start, size)
        stores.append(pltpu.make_async_copy(tiles.at[rows], out_ref.at[rows], out_sems.at[index]))
        stores[-1].start()

    pot_copy.wait()
    tiles[groups * cx * cy :] = pot_here[...].reshape(cx * cy // 8, 8, cz)
    store(groups * pieces, groups * cx * cy, cx * cy // 8)
    for index, (g, p) in enumerate(parts):
        loads[index].wait()
        for x in range(deep * p, deep * (p + 1)):
            tile_block(tiles, g * cx * cy + x * cy, here[GROUP * g : GROUP * (g + 1), x])
        store(index, g * cx * cy + deep * p * cy, deep * cy)
    for copy in stores:
        copy.wait()


def first_tiles(orbitals, potential):
    _, cx, cy, cz = orbitals.shape
    groups, pieces = CHUNKS[0], 2
    tiles = (groups * cx * cy + cx * cy // 8, 8, cz)
    return pl.pallas_call(
        functools.partial(first_tiles_kernel, groups, pieces),
        out_shape=jax.ShapeDtypeStruct(tiles, jnp.float32),
        in_specs=[pl.BlockSpec(memory_space=pltpu.HBM)] * 2,
        out_specs=pl.BlockSpec(memory_space=pltpu.HBM),
        scratch_shapes=[
            pltpu.VMEM((cx, cy, cz), jnp.float32),
            pltpu.VMEM((groups * GROUP, cx, cy, cz), jnp.float32),
            pltpu.VMEM(tiles, jnp.float32),
            pltpu.SemaphoreType.DMA((groups * pieces + 1,)),
            pltpu.SemaphoreType.DMA((groups * pieces + 1,)),
        ],
        compiler_params=pltpu.CompilerParams(vmem_limit_bytes=PREP_VMEM),
        name="first_tiles",
    )(potential, orbitals)


def tiles_kernel(chunks, pot_ref, orb_ref, *out_refs):
    cx, cy, cz = pot_ref.shape
    group = 0
    for out_ref, groups in zip(out_refs, chunks):
        for g in range(groups):
            for x in range(cx):
                tile_block(out_ref, g * cx * cy + x * cy, orb_ref[GROUP * group : GROUP * (group + 1), x])
            group += 1
    out_refs[0][chunks[0] * cx * cy :] = pot_ref[...].reshape(cx * cy // 8, 8, cz)


def all_tiles(orbitals, potential):
    _, cx, cy, cz = orbitals.shape
    tiles = [groups * cx * cy for groups in CHUNKS]
    tiles[0] += cx * cy // 8
    return pl.pallas_call(
        functools.partial(tiles_kernel, CHUNKS),
        out_shape=[jax.ShapeDtypeStruct((t, 8, cz), jnp.float32) for t in tiles],
        in_specs=[pl.BlockSpec(memory_space=pltpu.VMEM)] * 2,
        out_specs=[pl.BlockSpec(memory_space=pltpu.VMEM)] * len(tiles),
        compiler_params=pltpu.CompilerParams(vmem_limit_bytes=16 * 2**20),
        name="all_tiles",
    )(potential, orbitals)


def sides_kernel(unit, chunk_groups, rider, cx, cy, *refs):
    low_ref, high_ref = refs[-2:]
    start, groups, first, late = unit
    at = 0
    for g in range(start, start + groups):
        for plane, rows in halo_planes(cx, late):
            which, x = split_plane(plane, cx)
            base = g * cx * cy + x * cy
            low_ref[at : at + rows] = refs[which][base : base + rows]
            high_ref[at : at + rows] = refs[which][base + cy - rows : base + cy]
            at += rows
    if first:
        per = cy // 8
        for plane in diag_planes(cx):
            which, x = split_plane(plane, cx)
            base = chunk_groups * cx * cy + x * per
            low_ref[at] = refs[which][base]
            high_ref[at] = refs[which][base + per - 1]
            at += 1
    if rider is not None:
        for g in range(rider[0], rider[0] + rider[1]):
            for x in range(cx):
                base = g * cx * cy + x * cy
                low_ref[at : at + HALO] = refs[3][base : base + HALO]
                high_ref[at : at + HALO] = refs[3][base + cy - HALO : base + cy]
                at += HALO


def unit_tiles(cx, unit):
    _, groups, first, late = unit
    return groups * sum(rows for _, rows in halo_planes(cx, late)) + (len(diag_planes(cx)) if first else 0)


def pack_sides(blocks, unit, chunk_groups, cx, cy, rider, rider_mid):
    tiles = unit_tiles(cx, unit) + (0 if rider is None else rider[1] * cx * HALO)
    shape = jax.ShapeDtypeStruct((tiles,) + blocks[0].shape[1:], jnp.float32)
    operands = blocks + (() if rider is None else (rider_mid,))
    return pl.pallas_call(
        functools.partial(sides_kernel, unit, chunk_groups, rider, cx, cy),
        out_shape=(shape, shape),
        in_specs=[pl.BlockSpec(memory_space=pltpu.VMEM)] * len(operands),
        out_specs=(pl.BlockSpec(memory_space=pltpu.VMEM),) * 2,
        compiler_params=pltpu.CompilerParams(vmem_limit_bytes=16 * 2**20),
        cost_estimate=pl.CostEstimate(flops=0, bytes_accessed=1_000_000, transcendentals=0),
        name="pack_sides",
    )(*operands)


def z_circulant(cz):
    row = lax.broadcasted_iota(jnp.int32, (cz, cz), 0)
    col = lax.broadcasted_iota(jnp.int32, (cz, cz), 1)
    gap = jnp.where(row >= col, row - col, row - col + cz)
    near = (gap == 1) | (gap == cz - 1)
    far = (gap == 2) | (gap == cz - 2)
    return jnp.where(near, -16.0, jnp.where(far, 1.0, 0.0)).astype(jnp.bfloat16)


def z_part(center, matrix):
    flat = center.reshape(-1, center.shape[-1])
    high = flat.astype(jnp.bfloat16)
    rest = flat - high.astype(jnp.float32)
    middle = rest.astype(jnp.bfloat16)
    low = (rest - middle.astype(jnp.float32)).astype(jnp.bfloat16)

    def times(part):
        return jnp.dot(part, matrix, preferred_element_type=jnp.float32)

    return (times(high) + (times(middle) + times(low))).reshape(center.shape)


def four_steps(cx, cy, start, steps, diag_ref, out_ref):
    total = cx + 2 * HALO
    matrix = z_circulant(out_ref.shape[-1])

    def rows_of(ref):
        return lambda plane, a, b: ref[plane, a:b]

    chain = [start] + [rows_of(ref) for ref in steps]
    for step in range(DEG):
        source = chain[step]
        left = HALO - 2 * (step + 1)
        for plane in range(total):
            rows = reach(plane, cx, left)
            if rows < 0:
                continue
            first, last = HALO - rows, HALO + cy + rows
            column = source(plane, first - 2, last + 2)
            center = column[2:-2]
            near = (column[1:-3] + column[3:-1]) + (source(plane - 1, first, last) + source(plane + 1, first, last))
            far = (column[:-4] + column[4:]) + (source(plane - 2, first, last) + source(plane + 2, first, last))
            diag = diag_ref[plane, first:last][:, None, :]
            applied = diag * center + FAR * ((z_part(center, matrix) + far) - 16.0 * near)
            fresh = 0.5 * applied if step == 0 else applied - chain[step - 1](plane, first, last)
            if step < DEG - 1:
                steps[step][plane, first:last] = fresh
            else:
                out_ref[:, plane - HALO] = jnp.swapaxes(fresh, 0, 1)


def filter_kernel(unit, chunk_groups, own_at, cx, cy, lo_ref, mid_ref, hi_ref, yl_ref, yh_ref, *refs):
    start, groups, first, late = unit
    sources = (lo_ref, mid_ref, hi_ref)
    planes = halo_planes(cx, late)
    sides = {}
    at = 0
    for plane, rows in planes:
        sides[plane] = (yl_ref, yh_ref, at, rows)
        at += rows
    if late:
        for x in range(cx):
            sides[HALO + x] = (refs[0], refs[1], own_at + x * HALO, HALO)
    if first:
        out_ref, diag_ref = refs[-5:-3]
        per = cy // 8
        cz = out_ref.shape[-1]
        for x in range(cx):
            for which in range(3):
                base = chunk_groups * cx * cy + x * per
                block = sources[which][base : base + per].reshape(cy, cz)
                diag_ref[which * cx + x, HALO : HALO + cy] = DIAG_SCALE * block + DIAG_SHIFT
        for plane in diag_planes(cx):
            diag_ref[plane, 0:HALO] = DIAG_SCALE * yl_ref[at] + DIAG_SHIFT
            diag_ref[plane, HALO + cy :] = DIAG_SCALE * yh_ref[at] + DIAG_SHIFT
            at += 1
    else:
        diag_ref, out_ref = refs[-5:-3]

    def rows_of(plane, a, b):
        which, x = split_plane(plane, cx)
        base = (start * cx + x) * cy - HALO
        parts = [sources[which][base + max(a, HALO) : base + min(b, HALO + cy)]]
        if a < HALO:
            low, _, at, rows = sides[plane]
            parts.insert(0, low[at + a - (HALO - rows) : at + rows])
        if b > HALO + cy:
            _, high, at, _ = sides[plane]
            parts.append(high[at : at + b - HALO - cy])
        return parts[0] if len(parts) == 1 else jnp.concatenate(parts, axis=0)

    four_steps(cx, cy, rows_of, refs[-3:], diag_ref, out_ref)


def run_filter(blocks, sides, unit, chunk_groups, own, own_at, cx, cy, cz, diag):
    _, groups, first, late = unit
    assert groups == 1
    ext = (cx + 2 * HALO, cy + 2 * HALO, GROUP, cz)
    out_shape = [jax.ShapeDtypeStruct((GROUP, cx, cy, cz), jnp.float32)]
    operands = blocks + sides + (own if late else ())
    if first:
        out_shape.append(jax.ShapeDtypeStruct((cx + 2 * HALO, cy + 2 * HALO, cz), jnp.float32))
    else:
        operands = operands + (diag,)
    got = pl.pallas_call(
        functools.partial(filter_kernel, unit, chunk_groups, own_at, cx, cy),
        out_shape=out_shape,
        in_specs=[pl.BlockSpec(memory_space=pltpu.VMEM)] * len(operands),
        out_specs=[pl.BlockSpec(memory_space=pltpu.VMEM)] * len(out_shape),
        scratch_shapes=[pltpu.VMEM(ext, jnp.float32)] * 3,
        compiler_params=pltpu.CompilerParams(vmem_limit_bytes=32 * 2**20),
        cost_estimate=pl.CostEstimate(flops=0, bytes_accessed=FILTER_COST, transcendentals=0),
        name="filter_orbitals",
    )(*operands)
    return got if first else (got[0], diag)


def gram_kernel(offset, scale, counts, *refs):
    chunks, earlier, out_ref, rows_ref = refs[: len(counts)], refs[len(counts) : -2], refs[-2], refs[-1]
    own = chunks[-1]
    count, cx, cy, cz = own.shape
    norb = rows_ref.shape[1]
    rows = []
    for ref, size in zip(chunks, counts):
        for at in range(size):
            rows.append((ref, at))
    rows_ref[...] = jnp.zeros_like(rows_ref)
    block = 4
    for a0 in range(0, count, block):
        a_list = list(range(a0, min(a0 + block, count)))
        last = offset + a_list[-1]
        for j0 in range(0, last + 1, block):
            j_list = list(range(j0, min(j0 + block, last + 1)))
            accs = [None] * (len(a_list) * len(j_list))
            for x in range(cx):
                left = [own[a, x] for a in a_list]
                right = [rows[j][0][rows[j][1], x] for j in j_list]
                at = 0
                for l in left:
                    for r in right:
                        prod = l * r
                        prod = prod[:8] + prod[8:]
                        accs[at] = prod if accs[at] is None else accs[at] + prod
                        at += 1
            at = 0
            for a in a_list:
                for j in j_list:
                    rows_ref[a, j : j + 1, :] = jnp.sum(accs[at], axis=0, keepdims=True)
                    at += 1
    sums = lax.dot_general(
        jnp.ones((8, cz), jnp.float32), rows_ref[...].reshape(count * norb, cz), (((1,), (1,)), ((), ())),
        precision=lax.Precision.HIGHEST, preferred_element_type=jnp.float32,
    )
    lane = lax.broadcasted_iota(jnp.int32, (8, 128), 1)
    row = lax.broadcasted_iota(jnp.int32, (8, 128), 0)
    per = 128 // norb
    packed = jnp.zeros((8, 128), jnp.float32)
    for a in range(count):
        here, slot = a // per, (offset + a) // 8
        value = pltpu.roll(sums[:, 128 * here : 128 * (here + 1)], (norb * (slot - a % per)) % 128, 1)
        mask = (row == (offset + a) % 8) & (lane >= norb * slot) & (lane < norb * (slot + 1))
        packed = packed + jnp.where(mask, value, 0.0)
    packed = packed * scale
    for ref in earlier:
        packed = packed + ref[...]
    out_ref[...] = packed


def run_gram(chunks, earlier, offset, norb, scale):
    count, cx, cy, cz = chunks[-1].shape
    counts = tuple(c.shape[0] for c in chunks)
    operands = tuple(chunks) + tuple(earlier)
    return pl.pallas_call(
        functools.partial(gram_kernel, offset, scale, counts),
        out_shape=jax.ShapeDtypeStruct((8, 128), jnp.float32),
        in_specs=[pl.BlockSpec(memory_space=pltpu.VMEM)] * len(operands),
        out_specs=pl.BlockSpec(memory_space=pltpu.VMEM),
        scratch_shapes=[pltpu.VMEM((count, norb, cz), jnp.float32)],
        compiler_params=pltpu.CompilerParams(vmem_limit_bytes=24 * 2**20),
        cost_estimate=pl.CostEstimate(flops=0, bytes_accessed=100, transcendentals=0),
        name="gram_rows",
    )(*operands)


def factor_table(gram, table_ref):
    norb = gram.shape[0]
    columns = [jnp.broadcast_to(gram[:, j : j + 1], (norb, 128)) for j in range(norb)]
    row = lax.broadcasted_iota(jnp.int32, (norb, 128), 0)
    for k in range(norb):
        scale = 1.0 / jnp.sqrt(columns[k][k : k + 1])
        column = columns[k] * scale
        table_ref[k] = jnp.where(row == k, scale, column)
        for j in range(k + 1, norb):
            top = 8 * (j // 8)
            fresh = columns[j][top:] - column[top:] * column[j : j + 1]
            columns[j] = fresh if top == 0 else jnp.concatenate([jnp.zeros((top, 128), jnp.float32), fresh], axis=0)


def solve_kernel(counts, recv_ref, *refs):
    norb = sum(counts)
    chunks, (out_ref, here_ref, table_ref, sems) = refs[: len(counts)], refs[len(counts) :]
    packed = jnp.sum(recv_ref[...], axis=0)
    rows = jnp.concatenate([packed] + [jnp.roll(packed, -norb * q, 1) for q in range(1, 4)], axis=0)
    factor_table(rows, table_ref)
    where = []
    for ref, count in zip(chunks, counts):
        for at in range(count):
            where.append((ref, at))
    block = 8
    cx = here_ref.shape[1]

    def copy_out(x):
        return pltpu.make_async_copy(here_ref.at[:, x], out_ref.at[:, x], sems.at[x])

    def layer(x, _):
        for i0 in range(0, norb, block):
            accs = [where[i0 + a][0][where[i0 + a][1], x] for a in range(block)]
            for j in range(i0):
                value = here_ref[j, x]
                for a in range(block):
                    accs[a] = accs[a] - table_ref[j, i0 + a : i0 + a + 1, :] * value
            for a in range(block):
                value = accs[a] * table_ref[i0 + a, i0 + a : i0 + a + 1, :]
                here_ref[i0 + a, x] = value
                for c in range(a + 1, block):
                    accs[c] = accs[c] - table_ref[i0 + a, i0 + c : i0 + c + 1, :] * value
        copy_out(x).start()
        return 0

    lax.fori_loop(0, cx, layer, 0)
    for x in range(cx):
        copy_out(x).wait()


def run_solve(received, chunks):
    counts = tuple(c.shape[0] for c in chunks)
    norb = sum(counts)
    _, cx, cy, cz = chunks[0].shape
    return pl.pallas_call(
        functools.partial(solve_kernel, counts),
        out_shape=jax.ShapeDtypeStruct((norb, cx, cy, cz), jnp.float32),
        in_specs=[pl.BlockSpec(memory_space=pltpu.VMEM)] * (1 + len(chunks)),
        out_specs=pl.BlockSpec(memory_space=pl.ANY),
        scratch_shapes=[
            pltpu.VMEM((norb, cx, cy, cz), jnp.float32),
            pltpu.VMEM((norb, norb, 128), jnp.float32),
            pltpu.SemaphoreType.DMA((cx,)),
        ],
        compiler_params=pltpu.CompilerParams(vmem_limit_bytes=24 * 2**20),
        name="orthonormalize",
    )(received, *chunks)


def body(orbitals, potential):
    norb, cx, cy, cz = orbitals.shape
    chips = axis_count(("gx", "gz"))
    scale = 1.0 / float(chips * CORES * cx * cy * cz)
    blocks = []
    first = first_tiles(orbitals, potential)
    for index, mid in enumerate(all_tiles(orbitals, potential)):
        lo, hi = both_ways(*((first, first) if index == 0 else (mid, mid)), "gx")
        blocks.append((lo, mid, hi))
    diag = None
    filtered, grams, all_sides, alone = [], [], [], {}
    for index, (chunk, start, groups) in enumerate(UNITS):
        unit = (start, groups, index == 0, index in RIDES or index in ALONE)
        if index in AFTER or index in ALONE:
            lo, mid, hi = blocks[chunk]
            tied = (lo, hi)
            if index in ALONE:
                part = mid[start * cx * cy :][: cx * cy].reshape((cx, cy) + mid.shape[1:])
                rows = [p.reshape((cx * HALO,) + p.shape[2:]) for p in (part[:, :HALO], part[:, cy - HALO :])]
                tied += both_ways(*rows, GY)
            size = len(tied)
            before = AFTER.get(index)
            if before is not None:
                tied += (filtered[before],) + ((grams[before],) if before == 0 else ())
            tied = lax.optimization_barrier(tied)
            lo, hi = tied[:2]
            if index in ALONE:
                alone[index] = tied[2:4]
            if before is not None:
                filtered[before], *rest = tied[size:]
                grams[before : before + len(rest)] = rest
            blocks[chunk] = lo, mid, hi
        rider, rider_mid = None, None
        for later, carrier in RIDES.items():
            if carrier == index:
                rider, rider_mid = UNITS[later][1:], blocks[UNITS[later][0]][1]
        low, high = pack_sides(blocks[chunk], unit, CHUNKS[chunk], cx, cy, rider, rider_mid)
        all_sides.append(both_ways(low, high, GY))
        own, own_at = None, 0
        if index in RIDES:
            carrier = RIDES[index]
            own = all_sides[carrier]
            own_at = unit_tiles(cx, UNITS[carrier][1:] + (carrier == 0, carrier in RIDES))
        if index in ALONE:
            own = alone[index]
        out, diag = run_filter(blocks[chunk], all_sides[index], unit, CHUNKS[chunk], own, own_at, cx, cy, cz, diag)
        offset = GROUP * sum(g for _, _, g in UNITS[:index])
        filtered.append(out)
        last = index + 1 == len(UNITS)
        grams.append(run_gram(filtered, grams if last else (), offset, norb, scale))
    local = grams[-1]
    other = lax.ppermute(local, "core", [(core, 1 - core) for core in range(CORES)])
    chip = jnp.broadcast_to((local + other)[None], (chips,) + local.shape)
    received = lax.all_to_all(chip, ("gx", "gz"), 0, 0, tiled=True)
    return run_solve(received, filtered)


def solution(mesh):
    count = mesh.shape["gx"], mesh.shape["gy"] // CORES, CORES
    split = jax.sharding.Mesh(mesh.devices.reshape(count), ("gx",) + GY)
    placed = (P(None, "gx", GY, None), P("gx", GY, None))
    return jax.shard_map(
        body, mesh=split, in_specs=placed, out_specs=P(None, "gx", GY, None), check_vma=False
    )
```

```python
import functools
import math

import jax
import jax.numpy as jnp
from jax import lax
from jax.experimental import pallas as pl
from jax.experimental.pallas import tpu as pltpu
from jax.sharding import PartitionSpec as P

DEG = 4
HALO = 2 * DEG
CENTER = 5.0
HALF_W = 4.0
NEAR = (2.0 / HALF_W) * -0.5 * (4.0 / 3.0)
FAR = (2.0 / HALF_W) * 0.5 / 12.0
DIAG_SCALE = (2.0 / HALF_W) / FAR
DIAG_SHIFT = (2.0 / HALF_W) * (3 * 0.5 * 2.5 - CENTER) / FAR
BACK = (2.0 / FAR**2, 1.0 / FAR**2, 1.0 / FAR**2)

GROUP = 8
PREP_VMEM = 59 * 2**20
CHUNKS = (1, 2, 1)
UNITS = ((0, 0, 1), (1, 0, 1), (1, 1, 1), (2, 0, 1))
AFTER = {1: 0, 3: 1}
RIDES = {}
ALONE = (0, 1)
FILTER_COST = 100
GY = ("gz", "core")
CORES = 2


def axis_count(axis):
    return math.prod(lax.axis_size(a) for a in ((axis,) if isinstance(axis, str) else axis))


def shift_perm(axis, step):
    count = axis_count(axis)
    return [(i, (i + step) % count) for i in range(count)]


def both_ways(low_part, high_part, axis):
    return (
        lax.ppermute(high_part, axis, shift_perm(axis, 1)),
        lax.ppermute(low_part, axis, shift_perm(axis, -1)),
    )


def reach(plane, cx, left):
    outside = max(HALO - plane, plane - (HALO + cx - 1), 0)
    return left - 2 * ((outside + 1) // 2)


def halo_planes(cx, late=False):
    planes = []
    for plane in range(2, cx + 2 * HALO - 2):
        if late and HALO <= plane < HALO + cx:
            continue
        planes.append((plane, reach(plane, cx, HALO)))
    return planes


def diag_planes(cx):
    return range(4, cx + 2 * HALO - 4)


def split_plane(plane, cx):
    if plane < HALO:
        return 0, plane
    if plane < HALO + cx:
        return 1, plane - HALO
    return 2, plane - HALO - cx


def tile_block(out_ref, at, block):
    out_ref[at : at + block.shape[1]] = jnp.swapaxes(block, 0, 1)


def first_tiles_kernel(groups, pieces, pot_ref, orb_ref, out_ref, pot_here, here, tiles, in_sems, out_sems):
    cx, cy, cz = pot_ref.shape
    pot_copy = pltpu.make_async_copy(pot_ref, pot_here, in_sems.at[groups * pieces])
    pot_copy.start()
    deep = cx // pieces
    parts = [(g, p) for g in range(groups) for p in range(pieces)]
    loads, stores = [], []
    for index, (g, p) in enumerate(parts):
        part = (pl.ds(GROUP * g, GROUP), pl.ds(deep * p, deep))
        loads.append(pltpu.make_async_copy(orb_ref.at[part], here.at[part], in_sems.at[index]))
        loads[-1].start()

    def store(index, start, size):
        rows = pl.ds(start, size)
        stores.append(pltpu.make_async_copy(tiles.at[rows], out_ref.at[rows], out_sems.at[index]))
        stores[-1].start()

    pot_copy.wait()
    tiles[groups * cx * cy :] = pot_here[...].reshape(cx * cy // 8, 8, cz)
    store(groups * pieces, groups * cx * cy, cx * cy // 8)
    for index, (g, p) in enumerate(parts):
        loads[index].wait()
        for x in range(deep * p, deep * (p + 1)):
            tile_block(tiles, g * cx * cy + x * cy, here[GROUP * g : GROUP * (g + 1), x])
        store(index, g * cx * cy + deep * p * cy, deep * cy)
    for copy in stores:
        copy.wait()


def first_tiles(orbitals, potential):
    _, cx, cy, cz = orbitals.shape
    groups, pieces = CHUNKS[0], 2
    tiles = (groups * cx * cy + cx * cy // 8, 8, cz)
    return pl.pallas_call(
        functools.partial(first_tiles_kernel, groups, pieces),
        out_shape=jax.ShapeDtypeStruct(tiles, jnp.float32),
        in_specs=[pl.BlockSpec(memory_space=pltpu.HBM)] * 2,
        out_specs=pl.BlockSpec(memory_space=pltpu.HBM),
        scratch_shapes=[
            pltpu.VMEM((cx, cy, cz), jnp.float32),
            pltpu.VMEM((groups * GROUP, cx, cy, cz), jnp.float32),
            pltpu.VMEM(tiles, jnp.float32),
            pltpu.SemaphoreType.DMA((groups * pieces + 1,)),
            pltpu.SemaphoreType.DMA((groups * pieces + 1,)),
        ],
        compiler_params=pltpu.CompilerParams(vmem_limit_bytes=PREP_VMEM),
        name="first_tiles",
    )(potential, orbitals)


def tiles_kernel(chunks, pot_ref, orb_ref, *out_refs):
    cx, cy, cz = pot_ref.shape
    group = 0
    for out_ref, groups in zip(out_refs, chunks):
        for g in range(groups):
            for x in range(cx):
                tile_block(out_ref, g * cx * cy + x * cy, orb_ref[GROUP * group : GROUP * (group + 1), x])
            group += 1
    out_refs[0][chunks[0] * cx * cy :] = pot_ref[...].reshape(cx * cy // 8, 8, cz)


def all_tiles(orbitals, potential):
    _, cx, cy, cz = orbitals.shape
    tiles = [groups * cx * cy for groups in CHUNKS]
    tiles[0] += cx * cy // 8
    return pl.pallas_call(
        functools.partial(tiles_kernel, CHUNKS),
        out_shape=[jax.ShapeDtypeStruct((t, 8, cz), jnp.float32) for t in tiles],
        in_specs=[pl.BlockSpec(memory_space=pltpu.VMEM)] * 2,
        out_specs=[pl.BlockSpec(memory_space=pltpu.VMEM)] * len(tiles),
        compiler_params=pltpu.CompilerParams(vmem_limit_bytes=16 * 2**20),
        name="all_tiles",
    )(potential, orbitals)


def sides_kernel(unit, chunk_groups, rider, cx, cy, *refs):
    low_ref, high_ref = refs[-2:]
    start, groups, first, late = unit
    at = 0
    for g in range(start, start + groups):
        for plane, rows in halo_planes(cx, late):
            which, x = split_plane(plane, cx)
            base = g * cx * cy + x * cy
            low_ref[at : at + rows] = refs[which][base : base + rows]
            high_ref[at : at + rows] = refs[which][base + cy - rows : base + cy]
            at += rows
    if first:
        per = cy // 8
        for plane in diag_planes(cx):
            which, x = split_plane(plane, cx)
            base = chunk_groups * cx * cy + x * per
            low_ref[at] = refs[which][base]
            high_ref[at] = refs[which][base + per - 1]
            at += 1
    if rider is not None:
        for g in range(rider[0], rider[0] + rider[1]):
            for x in range(cx):
                base = g * cx * cy + x * cy
                low_ref[at : at + HALO] = refs[3][base : base + HALO]
                high_ref[at : at + HALO] = refs[3][base + cy - HALO : base + cy]
                at += HALO


def unit_tiles(cx, unit):
    _, groups, first, late = unit
    return groups * sum(rows for _, rows in halo_planes(cx, late)) + (len(diag_planes(cx)) if first else 0)


def pack_sides(blocks, unit, chunk_groups, cx, cy, rider, rider_mid):
    tiles = unit_tiles(cx, unit) + (0 if rider is None else rider[1] * cx * HALO)
    shape = jax.ShapeDtypeStruct((tiles,) + blocks[0].shape[1:], jnp.float32)
    operands = blocks + (() if rider is None else (rider_mid,))
    return pl.pallas_call(
        functools.partial(sides_kernel, unit, chunk_groups, rider, cx, cy),
        out_shape=(shape, shape),
        in_specs=[pl.BlockSpec(memory_space=pltpu.VMEM)] * len(operands),
        out_specs=(pl.BlockSpec(memory_space=pltpu.VMEM),) * 2,
        compiler_params=pltpu.CompilerParams(vmem_limit_bytes=16 * 2**20),
        cost_estimate=pl.CostEstimate(flops=0, bytes_accessed=1_000_000, transcendentals=0),
        name="pack_sides",
    )(*operands)


def z_circulant(cz):
    row = lax.broadcasted_iota(jnp.int32, (cz, cz), 0)
    col = lax.broadcasted_iota(jnp.int32, (cz, cz), 1)
    gap = jnp.where(row >= col, row - col, row - col + cz)
    near = (gap == 1) | (gap == cz - 1)
    far = (gap == 2) | (gap == cz - 2)
    return jnp.where(near, -16.0, jnp.where(far, 1.0, 0.0)).astype(jnp.bfloat16)


def z_part(center, matrix):
    flat = center.reshape(-1, center.shape[-1])
    high = flat.astype(jnp.bfloat16)
    rest = flat - high.astype(jnp.float32)
    middle = rest.astype(jnp.bfloat16)
    low = (rest - middle.astype(jnp.float32)).astype(jnp.bfloat16)

    def times(part):
        return jnp.dot(part, matrix, preferred_element_type=jnp.float32)

    return (times(high) + (times(middle) + times(low))).reshape(center.shape)


def four_steps(cx, cy, start, steps, diag_ref, out_ref):
    total = cx + 2 * HALO
    matrix = z_circulant(out_ref.shape[-1])

    def rows_of(ref):
        return lambda plane, a, b: ref[plane, a:b]

    chain = [start] + [rows_of(ref) for ref in steps]
    for step in range(DEG):
        source = chain[step]
        left = HALO - 2 * (step + 1)
        for plane in range(total):
            rows = reach(plane, cx, left)
            if rows < 0:
                continue
            first, last = HALO - rows, HALO + cy + rows
            column = source(plane, first - 2, last + 2)
            center = column[2:-2]
            near = (column[1:-3] + column[3:-1]) + (source(plane - 1, first, last) + source(plane + 1, first, last))
            far = (column[:-4] + column[4:]) + (source(plane - 2, first, last) + source(plane + 2, first, last))
            diag = diag_ref[plane, first:last][:, None, :]
            fresh = diag * center + ((z_part(center, matrix) + far) - 16.0 * near)
            if step > 0:
                fresh = fresh - BACK[step - 1] * chain[step - 1](plane, first, last)
            if step < DEG - 1:
                steps[step][plane, first:last] = fresh
            else:
                out_ref[:, plane - HALO] = jnp.swapaxes((0.5 * FAR**DEG) * fresh, 0, 1)


def filter_kernel(unit, chunk_groups, own_at, cx, cy, lo_ref, mid_ref, hi_ref, yl_ref, yh_ref, *refs):
    start, groups, first, late = unit
    sources = (lo_ref, mid_ref, hi_ref)
    planes = halo_planes(cx, late)
    sides = {}
    at = 0
    for plane, rows in planes:
        sides[plane] = (yl_ref, yh_ref, at, rows)
        at += rows
    if late:
        for x in range(cx):
            sides[HALO + x] = (refs[0], refs[1], own_at + x * HALO, HALO)
    if first:
        out_ref, diag_ref = refs[-5:-3]
        per = cy // 8
        cz = out_ref.shape[-1]
        for x in range(cx):
            for which in range(3):
                base = chunk_groups * cx * cy + x * per
                block = sources[which][base : base + per].reshape(cy, cz)
                diag_ref[which * cx + x, HALO : HALO + cy] = DIAG_SCALE * block + DIAG_SHIFT
        for plane in diag_planes(cx):
            diag_ref[plane, 0:HALO] = DIAG_SCALE * yl_ref[at] + DIAG_SHIFT
            diag_ref[plane, HALO + cy :] = DIAG_SCALE * yh_ref[at] + DIAG_SHIFT
            at += 1
    else:
        diag_ref, out_ref = refs[-5:-3]

    def rows_of(plane, a, b):
        which, x = split_plane(plane, cx)
        base = (start * cx + x) * cy - HALO
        parts = [sources[which][base + max(a, HALO) : base + min(b, HALO + cy)]]
        if a < HALO:
            low, _, at, rows = sides[plane]
            parts.insert(0, low[at + a - (HALO - rows) : at + rows])
        if b > HALO + cy:
            _, high, at, _ = sides[plane]
            parts.append(high[at : at + b - HALO - cy])
        return parts[0] if len(parts) == 1 else jnp.concatenate(parts, axis=0)

    four_steps(cx, cy, rows_of, refs[-3:], diag_ref, out_ref)


def run_filter(blocks, sides, unit, chunk_groups, own, own_at, cx, cy, cz, diag):
    _, groups, first, late = unit
    assert groups == 1
    ext = (cx + 2 * HALO, cy + 2 * HALO, GROUP, cz)
    out_shape = [jax.ShapeDtypeStruct((GROUP, cx, cy, cz), jnp.float32)]
    operands = blocks + sides + (own if late else ())
    if first:
        out_shape.append(jax.ShapeDtypeStruct((cx + 2 * HALO, cy + 2 * HALO, cz), jnp.float32))
    else:
        operands = operands + (diag,)
    got = pl.pallas_call(
        functools.partial(filter_kernel, unit, chunk_groups, own_at, cx, cy),
        out_shape=out_shape,
        in_specs=[pl.BlockSpec(memory_space=pltpu.VMEM)] * len(operands),
        out_specs=[pl.BlockSpec(memory_space=pltpu.VMEM)] * len(out_shape),
        scratch_shapes=[pltpu.VMEM(ext, jnp.float32)] * 3,
        compiler_params=pltpu.CompilerParams(vmem_limit_bytes=32 * 2**20),
        cost_estimate=pl.CostEstimate(flops=0, bytes_accessed=FILTER_COST, transcendentals=0),
        name="filter_orbitals",
    )(*operands)
    return got if first else (got[0], diag)


def gram_kernel(offset, scale, counts, *refs):
    chunks, earlier, out_ref, rows_ref = refs[: len(counts)], refs[len(counts) : -2], refs[-2], refs[-1]
    own = chunks[-1]
    count, cx, cy, cz = own.shape
    norb = rows_ref.shape[1]
    rows = []
    for ref, size in zip(chunks, counts):
        for at in range(size):
            rows.append((ref, at))
    rows_ref[...] = jnp.zeros_like(rows_ref)
    block = 4
    for a0 in range(0, count, block):
        a_list = list(range(a0, min(a0 + block, count)))
        last = offset + a_list[-1]
        for j0 in range(0, last + 1, block):
            j_list = list(range(j0, min(j0 + block, last + 1)))
            accs = [None] * (len(a_list) * len(j_list))
            for x in range(cx):
                left = [own[a, x] for a in a_list]
                right = [rows[j][0][rows[j][1], x] for j in j_list]
                at = 0
                for l in left:
                    for r in right:
                        prod = l * r
                        prod = prod[:8] + prod[8:]
                        accs[at] = prod if accs[at] is None else accs[at] + prod
                        at += 1
            at = 0
            for a in a_list:
                for j in j_list:
                    rows_ref[a, j : j + 1, :] = jnp.sum(accs[at], axis=0, keepdims=True)
                    at += 1
    sums = lax.dot_general(
        jnp.ones((8, cz), jnp.float32), rows_ref[...].reshape(count * norb, cz), (((1,), (1,)), ((), ())),
        precision=lax.Precision.HIGHEST, preferred_element_type=jnp.float32,
    )
    lane = lax.broadcasted_iota(jnp.int32, (8, 128), 1)
    row = lax.broadcasted_iota(jnp.int32, (8, 128), 0)
    per = 128 // norb
    packed = jnp.zeros((8, 128), jnp.float32)
    for a in range(count):
        here, slot = a // per, (offset + a) // 8
        value = pltpu.roll(sums[:, 128 * here : 128 * (here + 1)], (norb * (slot - a % per)) % 128, 1)
        mask = (row == (offset + a) % 8) & (lane >= norb * slot) & (lane < norb * (slot + 1))
        packed = packed + jnp.where(mask, value, 0.0)
    packed = packed * scale
    for ref in earlier:
        packed = packed + ref[...]
    out_ref[...] = packed


def run_gram(chunks, earlier, offset, norb, scale):
    count, cx, cy, cz = chunks[-1].shape
    counts = tuple(c.shape[0] for c in chunks)
    operands = tuple(chunks) + tuple(earlier)
    return pl.pallas_call(
        functools.partial(gram_kernel, offset, scale, counts),
        out_shape=jax.ShapeDtypeStruct((8, 128), jnp.float32),
        in_specs=[pl.BlockSpec(memory_space=pltpu.VMEM)] * len(operands),
        out_specs=pl.BlockSpec(memory_space=pltpu.VMEM),
        scratch_shapes=[pltpu.VMEM((count, norb, cz), jnp.float32)],
        compiler_params=pltpu.CompilerParams(vmem_limit_bytes=24 * 2**20),
        cost_estimate=pl.CostEstimate(flops=0, bytes_accessed=100, transcendentals=0),
        name="gram_rows",
    )(*operands)


def factor_table(gram, table_ref):
    norb = gram.shape[0]
    columns = [jnp.broadcast_to(gram[:, j : j + 1], (norb, 128)) for j in range(norb)]
    row = lax.broadcasted_iota(jnp.int32, (norb, 128), 0)
    for k in range(norb):
        scale = 1.0 / jnp.sqrt(columns[k][k : k + 1])
        column = columns[k] * scale
        table_ref[k] = jnp.where(row == k, scale, column)
        for j in range(k + 1, norb):
            top = 8 * (j // 8)
            fresh = columns[j][top:] - column[top:] * column[j : j + 1]
            columns[j] = fresh if top == 0 else jnp.concatenate([jnp.zeros((top, 128), jnp.float32), fresh], axis=0)


def solve_kernel(counts, recv_ref, *refs):
    norb = sum(counts)
    chunks, (out_ref, here_ref, table_ref, sems) = refs[: len(counts)], refs[len(counts) :]
    packed = jnp.sum(recv_ref[...], axis=0)
    rows = jnp.concatenate([packed] + [jnp.roll(packed, -norb * q, 1) for q in range(1, 4)], axis=0)
    factor_table(rows, table_ref)
    where = []
    for ref, count in zip(chunks, counts):
        for at in range(count):
            where.append((ref, at))
    block = 8
    cx = here_ref.shape[1]

    def copy_out(x):
        return pltpu.make_async_copy(here_ref.at[:, x], out_ref.at[:, x], sems.at[x])

    def layer(x, _):
        for i0 in range(0, norb, block):
            accs = [where[i0 + a][0][where[i0 + a][1], x] for a in range(block)]
            for j in range(i0):
                value = here_ref[j, x]
                for a in range(block):
                    accs[a] = accs[a] - table_ref[j, i0 + a : i0 + a + 1, :] * value
            for a in range(block):
                value = accs[a] * table_ref[i0 + a, i0 + a : i0 + a + 1, :]
                here_ref[i0 + a, x] = value
                for c in range(a + 1, block):
                    accs[c] = accs[c] - table_ref[i0 + a, i0 + c : i0 + c + 1, :] * value
        copy_out(x).start()
        return 0

    lax.fori_loop(0, cx, layer, 0)
    for x in range(cx):
        copy_out(x).wait()


def run_solve(received, chunks):
    counts = tuple(c.shape[0] for c in chunks)
    norb = sum(counts)
    _, cx, cy, cz = chunks[0].shape
    return pl.pallas_call(
        functools.partial(solve_kernel, counts),
        out_shape=jax.ShapeDtypeStruct((norb, cx, cy, cz), jnp.float32),
        in_specs=[pl.BlockSpec(memory_space=pltpu.VMEM)] * (1 + len(chunks)),
        out_specs=pl.BlockSpec(memory_space=pl.ANY),
        scratch_shapes=[
            pltpu.VMEM((norb, cx, cy, cz), jnp.float32),
            pltpu.VMEM((norb, norb, 128), jnp.float32),
            pltpu.SemaphoreType.DMA((cx,)),
        ],
        compiler_params=pltpu.CompilerParams(vmem_limit_bytes=24 * 2**20),
        name="orthonormalize",
    )(received, *chunks)


def body(orbitals, potential):
    norb, cx, cy, cz = orbitals.shape
    chips = axis_count(("gx", "gz"))
    scale = 1.0 / float(chips * CORES * cx * cy * cz)
    blocks = []
    first = first_tiles(orbitals, potential)
    for index, mid in enumerate(all_tiles(orbitals, potential)):
        lo, hi = both_ways(*((first, first) if index == 0 else (mid, mid)), "gx")
        blocks.append((lo, mid, hi))
    diag = None
    filtered, grams, all_sides, alone = [], [], [], {}
    for index, (chunk, start, groups) in enumerate(UNITS):
        unit = (start, groups, index == 0, index in RIDES or index in ALONE)
        if index in AFTER or index in ALONE:
            lo, mid, hi = blocks[chunk]
            tied = (lo, hi)
            if index in ALONE:
                part = mid[start * cx * cy :][: cx * cy].reshape((cx, cy) + mid.shape[1:])
                rows = [p.reshape((cx * HALO,) + p.shape[2:]) for p in (part[:, :HALO], part[:, cy - HALO :])]
                tied += both_ways(*rows, GY)
            size = len(tied)
            before = AFTER.get(index)
            if before is not None:
                tied += (filtered[before],) + ((grams[before],) if before == 0 else ())
            tied = lax.optimization_barrier(tied)
            lo, hi = tied[:2]
            if index in ALONE:
                alone[index] = tied[2:4]
            if before is not None:
                filtered[before], *rest = tied[size:]
                grams[before : before + len(rest)] = rest
            blocks[chunk] = lo, mid, hi
        rider, rider_mid = None, None
        for later, carrier in RIDES.items():
            if carrier == index:
                rider, rider_mid = UNITS[later][1:], blocks[UNITS[later][0]][1]
        low, high = pack_sides(blocks[chunk], unit, CHUNKS[chunk], cx, cy, rider, rider_mid)
        all_sides.append(both_ways(low, high, GY))
        own, own_at = None, 0
        if index in RIDES:
            carrier = RIDES[index]
            own = all_sides[carrier]
            own_at = unit_tiles(cx, UNITS[carrier][1:] + (carrier == 0, carrier in RIDES))
        if index in ALONE:
            own = alone[index]
        out, diag = run_filter(blocks[chunk], all_sides[index], unit, CHUNKS[chunk], own, own_at, cx, cy, cz, diag)
        offset = GROUP * sum(g for _, _, g in UNITS[:index])
        filtered.append(out)
        last = index + 1 == len(UNITS)
        grams.append(run_gram(filtered, grams if last else (), offset, norb, scale))
    local = grams[-1]
    other = lax.ppermute(local, "core", [(core, 1 - core) for core in range(CORES)])
    chip = jnp.broadcast_to((local + other)[None], (chips,) + local.shape)
    received = lax.all_to_all(chip, ("gx", "gz"), 0, 0, tiled=True)
    return run_solve(received, filtered)


def solution(mesh):
    count = mesh.shape["gx"], mesh.shape["gy"] // CORES, CORES
    split = jax.sharding.Mesh(mesh.devices.reshape(count), ("gx",) + GY)
    placed = (P(None, "gx", GY, None), P("gx", GY, None))
    return jax.shard_map(
        body, mesh=split, in_specs=placed, out_specs=P(None, "gx", GY, None), check_vma=False
    )
```

```python
import functools
import math

import jax
import jax.numpy as jnp
from jax import lax
from jax.experimental import pallas as pl
from jax.experimental.pallas import tpu as pltpu
from jax.sharding import PartitionSpec as P

DEG = 4
HALO = 2 * DEG
CENTER = 5.0
HALF_W = 4.0
NEAR = (2.0 / HALF_W) * -0.5 * (4.0 / 3.0)
FAR = (2.0 / HALF_W) * 0.5 / 12.0
DIAG_SCALE = (2.0 / HALF_W) / FAR
DIAG_SHIFT = (2.0 / HALF_W) * (3 * 0.5 * 2.5 - CENTER) / FAR
BACK = (2.0 / FAR**2, 1.0 / FAR**2, 1.0 / FAR**2)

GROUP = 8
PREP_VMEM = 59 * 2**20
CHUNKS = (1, 2, 1)
UNITS = ((0, 0, 1), (1, 0, 1), (1, 1, 1), (2, 0, 1))
AFTER = {1: 0, 3: 1}
RIDES = {}
ALONE = (0, 1)
FILTER_COST = 100
GY = ("gz", "core")
CORES = 2


def axis_count(axis):
    return math.prod(lax.axis_size(a) for a in ((axis,) if isinstance(axis, str) else axis))


def shift_perm(axis, step):
    count = axis_count(axis)
    return [(i, (i + step) % count) for i in range(count)]


def both_ways(low_part, high_part, axis):
    return (
        lax.ppermute(high_part, axis, shift_perm(axis, 1)),
        lax.ppermute(low_part, axis, shift_perm(axis, -1)),
    )


def reach(plane, cx, left):
    outside = max(HALO - plane, plane - (HALO + cx - 1), 0)
    return left - 2 * ((outside + 1) // 2)


def halo_planes(cx, late=False):
    planes = []
    for plane in range(2, cx + 2 * HALO - 2):
        if late and HALO <= plane < HALO + cx:
            continue
        planes.append((plane, reach(plane, cx, HALO)))
    return planes


def diag_planes(cx):
    return range(4, cx + 2 * HALO - 4)


def split_plane(plane, cx):
    if plane < HALO:
        return 0, plane
    if plane < HALO + cx:
        return 1, plane - HALO
    return 2, plane - HALO - cx


def tile_block(out_ref, at, block):
    out_ref[at : at + block.shape[1]] = jnp.swapaxes(block, 0, 1)


def first_tiles_kernel(groups, pieces, pot_ref, orb_ref, out_ref, pot_here, here, tiles, in_sems, out_sems):
    cx, cy, cz = pot_ref.shape
    pot_copy = pltpu.make_async_copy(pot_ref, pot_here, in_sems.at[groups * pieces])
    pot_copy.start()
    deep = cx // pieces
    parts = [(g, p) for g in range(groups) for p in range(pieces)]
    loads, stores = [], []
    for index, (g, p) in enumerate(parts):
        part = (pl.ds(GROUP * g, GROUP), pl.ds(deep * p, deep))
        loads.append(pltpu.make_async_copy(orb_ref.at[part], here.at[part], in_sems.at[index]))
        loads[-1].start()

    def store(index, start, size):
        rows = pl.ds(start, size)
        stores.append(pltpu.make_async_copy(tiles.at[rows], out_ref.at[rows], out_sems.at[index]))
        stores[-1].start()

    pot_copy.wait()
    tiles[groups * cx * cy :] = pot_here[...].reshape(cx * cy // 8, 8, cz)
    store(groups * pieces, groups * cx * cy, cx * cy // 8)
    for index, (g, p) in enumerate(parts):
        loads[index].wait()
        for x in range(deep * p, deep * (p + 1)):
            tile_block(tiles, g * cx * cy + x * cy, here[GROUP * g : GROUP * (g + 1), x])
        store(index, g * cx * cy + deep * p * cy, deep * cy)
    for copy in stores:
        copy.wait()


def first_tiles(orbitals, potential):
    _, cx, cy, cz = orbitals.shape
    groups, pieces = CHUNKS[0], 2
    tiles = (groups * cx * cy + cx * cy // 8, 8, cz)
    return pl.pallas_call(
        functools.partial(first_tiles_kernel, groups, pieces),
        out_shape=jax.ShapeDtypeStruct(tiles, jnp.float32),
        in_specs=[pl.BlockSpec(memory_space=pltpu.HBM)] * 2,
        out_specs=pl.BlockSpec(memory_space=pltpu.HBM),
        scratch_shapes=[
            pltpu.VMEM((cx, cy, cz), jnp.float32),
            pltpu.VMEM((groups * GROUP, cx, cy, cz), jnp.float32),
            pltpu.VMEM(tiles, jnp.float32),
            pltpu.SemaphoreType.DMA((groups * pieces + 1,)),
            pltpu.SemaphoreType.DMA((groups * pieces + 1,)),
        ],
        compiler_params=pltpu.CompilerParams(vmem_limit_bytes=PREP_VMEM),
        name="first_tiles",
    )(potential, orbitals)


def tiles_kernel(chunks, pot_ref, orb_ref, *out_refs):
    cx, cy, cz = pot_ref.shape
    group = 0
    for out_ref, groups in zip(out_refs, chunks):
        for g in range(groups):
            for x in range(cx):
                tile_block(out_ref, g * cx * cy + x * cy, orb_ref[GROUP * group : GROUP * (group + 1), x])
            group += 1
    out_refs[0][chunks[0] * cx * cy :] = pot_ref[...].reshape(cx * cy // 8, 8, cz)


def all_tiles(orbitals, potential):
    _, cx, cy, cz = orbitals.shape
    tiles = [groups * cx * cy for groups in CHUNKS]
    tiles[0] += cx * cy // 8
    return pl.pallas_call(
        functools.partial(tiles_kernel, CHUNKS),
        out_shape=[jax.ShapeDtypeStruct((t, 8, cz), jnp.float32) for t in tiles],
        in_specs=[pl.BlockSpec(memory_space=pltpu.VMEM)] * 2,
        out_specs=[pl.BlockSpec(memory_space=pltpu.VMEM)] * len(tiles),
        compiler_params=pltpu.CompilerParams(vmem_limit_bytes=16 * 2**20),
        name="all_tiles",
    )(potential, orbitals)


def sides_kernel(unit, chunk_groups, rider, cx, cy, *refs):
    low_ref, high_ref = refs[-2:]
    start, groups, first, late = unit
    at = 0
    for g in range(start, start + groups):
        for plane, rows in halo_planes(cx, late):
            which, x = split_plane(plane, cx)
            base = g * cx * cy + x * cy
            low_ref[at : at + rows] = refs[which][base : base + rows]
            high_ref[at : at + rows] = refs[which][base + cy - rows : base + cy]
            at += rows
    if first:
        per = cy // 8
        for plane in diag_planes(cx):
            which, x = split_plane(plane, cx)
            base = chunk_groups * cx * cy + x * per
            low_ref[at] = refs[which][base]
            high_ref[at] = refs[which][base + per - 1]
            at += 1
    if rider is not None:
        for g in range(rider[0], rider[0] + rider[1]):
            for x in range(cx):
                base = g * cx * cy + x * cy
                low_ref[at : at + HALO] = refs[3][base : base + HALO]
                high_ref[at : at + HALO] = refs[3][base + cy - HALO : base + cy]
                at += HALO


def unit_tiles(cx, unit):
    _, groups, first, late = unit
    return groups * sum(rows for _, rows in halo_planes(cx, late)) + (len(diag_planes(cx)) if first else 0)


def pack_sides(blocks, unit, chunk_groups, cx, cy, rider, rider_mid):
    tiles = unit_tiles(cx, unit) + (0 if rider is None else rider[1] * cx * HALO)
    shape = jax.ShapeDtypeStruct((tiles,) + blocks[0].shape[1:], jnp.float32)
    operands = blocks + (() if rider is None else (rider_mid,))
    return pl.pallas_call(
        functools.partial(sides_kernel, unit, chunk_groups, rider, cx, cy),
        out_shape=(shape, shape),
        in_specs=[pl.BlockSpec(memory_space=pltpu.VMEM)] * len(operands),
        out_specs=(pl.BlockSpec(memory_space=pltpu.VMEM),) * 2,
        compiler_params=pltpu.CompilerParams(vmem_limit_bytes=16 * 2**20),
        cost_estimate=pl.CostEstimate(flops=0, bytes_accessed=1_000_000, transcendentals=0),
        name="pack_sides",
    )(*operands)


def z_circulant(cz):
    row = lax.broadcasted_iota(jnp.int32, (cz, cz), 0)
    col = lax.broadcasted_iota(jnp.int32, (cz, cz), 1)
    gap = jnp.where(row >= col, row - col, row - col + cz)
    near = (gap == 1) | (gap == cz - 1)
    far = (gap == 2) | (gap == cz - 2)
    return jnp.where(near, -16.0, jnp.where(far, 1.0, 0.0)).astype(jnp.bfloat16)


def z_part(center, matrix):
    flat = center.reshape(-1, center.shape[-1])
    high = flat.astype(jnp.bfloat16)
    rest = flat - high.astype(jnp.float32)
    middle = rest.astype(jnp.bfloat16)
    low = (rest - middle.astype(jnp.float32)).astype(jnp.bfloat16)

    both = jnp.concatenate([high, middle], axis=1)
    twice = jnp.concatenate([matrix, matrix], axis=0)
    upper = jnp.dot(both, twice, preferred_element_type=jnp.float32)
    return (upper + jnp.dot(low, matrix, preferred_element_type=jnp.float32)).reshape(center.shape)


def four_steps(cx, cy, start, steps, diag_ref, out_ref):
    total = cx + 2 * HALO
    matrix = z_circulant(out_ref.shape[-1])

    def rows_of(ref):
        return lambda plane, a, b: ref[plane, a:b]

    chain = [start] + [rows_of(ref) for ref in steps]
    for step in range(DEG):
        source = chain[step]
        left = HALO - 2 * (step + 1)
        for plane in range(total):
            rows = reach(plane, cx, left)
            if rows < 0:
                continue
            first, last = HALO - rows, HALO + cy + rows
            column = source(plane, first - 2, last + 2)
            center = column[2:-2]
            near = (column[1:-3] + column[3:-1]) + (source(plane - 1, first, last) + source(plane + 1, first, last))
            far = (column[:-4] + column[4:]) + (source(plane - 2, first, last) + source(plane + 2, first, last))
            diag = diag_ref[plane, first:last][:, None, :]
            fresh = diag * center + ((z_part(center, matrix) + far) - 16.0 * near)
            if step > 0:
                fresh = fresh - BACK[step - 1] * chain[step - 1](plane, first, last)
            if step < DEG - 1:
                steps[step][plane, first:last] = fresh
            else:
                out_ref[:, plane - HALO] = jnp.swapaxes((0.5 * FAR**DEG) * fresh, 0, 1)


def filter_kernel(unit, chunk_groups, own_at, cx, cy, lo_ref, mid_ref, hi_ref, yl_ref, yh_ref, *refs):
    start, groups, first, late = unit
    sources = (lo_ref, mid_ref, hi_ref)
    planes = halo_planes(cx, late)
    sides = {}
    at = 0
    for plane, rows in planes:
        sides[plane] = (yl_ref, yh_ref, at, rows)
        at += rows
    if late:
        for x in range(cx):
            sides[HALO + x] = (refs[0], refs[1], own_at + x * HALO, HALO)
    if first:
        out_ref, diag_ref = refs[-5:-3]
        per = cy // 8
        cz = out_ref.shape[-1]
        for x in range(cx):
            for which in range(3):
                base = chunk_groups * cx * cy + x * per
                block = sources[which][base : base + per].reshape(cy, cz)
                diag_ref[which * cx + x, HALO : HALO + cy] = DIAG_SCALE * block + DIAG_SHIFT
        for plane in diag_planes(cx):
            diag_ref[plane, 0:HALO] = DIAG_SCALE * yl_ref[at] + DIAG_SHIFT
            diag_ref[plane, HALO + cy :] = DIAG_SCALE * yh_ref[at] + DIAG_SHIFT
            at += 1
    else:
        diag_ref, out_ref = refs[-5:-3]

    def rows_of(plane, a, b):
        which, x = split_plane(plane, cx)
        base = (start * cx + x) * cy - HALO
        parts = [sources[which][base + max(a, HALO) : base + min(b, HALO + cy)]]
        if a < HALO:
            low, _, at, rows = sides[plane]
            parts.insert(0, low[at + a - (HALO - rows) : at + rows])
        if b > HALO + cy:
            _, high, at, _ = sides[plane]
            parts.append(high[at : at + b - HALO - cy])
        return parts[0] if len(parts) == 1 else jnp.concatenate(parts, axis=0)

    four_steps(cx, cy, rows_of, refs[-3:], diag_ref, out_ref)


def run_filter(blocks, sides, unit, chunk_groups, own, own_at, cx, cy, cz, diag):
    _, groups, first, late = unit
    assert groups == 1
    ext = (cx + 2 * HALO, cy + 2 * HALO, GROUP, cz)
    out_shape = [jax.ShapeDtypeStruct((GROUP, cx, cy, cz), jnp.float32)]
    operands = blocks + sides + (own if late else ())
    if first:
        out_shape.append(jax.ShapeDtypeStruct((cx + 2 * HALO, cy + 2 * HALO, cz), jnp.float32))
    else:
        operands = operands + (diag,)
    got = pl.pallas_call(
        functools.partial(filter_kernel, unit, chunk_groups, own_at, cx, cy),
        out_shape=out_shape,
        in_specs=[pl.BlockSpec(memory_space=pltpu.VMEM)] * len(operands),
        out_specs=[pl.BlockSpec(memory_space=pltpu.VMEM)] * len(out_shape),
        scratch_shapes=[pltpu.VMEM(ext, jnp.float32)] * 3,
        compiler_params=pltpu.CompilerParams(vmem_limit_bytes=32 * 2**20),
        cost_estimate=pl.CostEstimate(flops=0, bytes_accessed=FILTER_COST, transcendentals=0),
        name="filter_orbitals",
    )(*operands)
    return got if first else (got[0], diag)


def gram_kernel(offset, scale, counts, *refs):
    chunks, earlier, out_ref, rows_ref = refs[: len(counts)], refs[len(counts) : -2], refs[-2], refs[-1]
    own = chunks[-1]
    count, cx, cy, cz = own.shape
    norb = rows_ref.shape[1]
    rows = []
    for ref, size in zip(chunks, counts):
        for at in range(size):
            rows.append((ref, at))
    rows_ref[...] = jnp.zeros_like(rows_ref)
    block = 4
    for a0 in range(0, count, block):
        a_list = list(range(a0, min(a0 + block, count)))
        last = offset + a_list[-1]
        for j0 in range(0, last + 1, block):
            j_list = list(range(j0, min(j0 + block, last + 1)))
            accs = [None] * (len(a_list) * len(j_list))
            for x in range(cx):
                left = [own[a, x] for a in a_list]
                right = [rows[j][0][rows[j][1], x] for j in j_list]
                at = 0
                for l in left:
                    for r in right:
                        prod = l * r
                        prod = prod[:8] + prod[8:]
                        accs[at] = prod if accs[at] is None else accs[at] + prod
                        at += 1
            at = 0
            for a in a_list:
                for j in j_list:
                    rows_ref[a, j : j + 1, :] = jnp.sum(accs[at], axis=0, keepdims=True)
                    at += 1
    sums = lax.dot_general(
        jnp.ones((8, cz), jnp.float32), rows_ref[...].reshape(count * norb, cz), (((1,), (1,)), ((), ())),
        precision=lax.Precision.HIGHEST, preferred_element_type=jnp.float32,
    )
    lane = lax.broadcasted_iota(jnp.int32, (8, 128), 1)
    row = lax.broadcasted_iota(jnp.int32, (8, 128), 0)
    per = 128 // norb
    packed = jnp.zeros((8, 128), jnp.float32)
    for a in range(count):
        here, slot = a // per, (offset + a) // 8
        value = pltpu.roll(sums[:, 128 * here : 128 * (here + 1)], (norb * (slot - a % per)) % 128, 1)
        mask = (row == (offset + a) % 8) & (lane >= norb * slot) & (lane < norb * (slot + 1))
        packed = packed + jnp.where(mask, value, 0.0)
    packed = packed * scale
    for ref in earlier:
        packed = packed + ref[...]
    out_ref[...] = packed


def run_gram(chunks, earlier, offset, norb, scale):
    count, cx, cy, cz = chunks[-1].shape
    counts = tuple(c.shape[0] for c in chunks)
    operands = tuple(chunks) + tuple(earlier)
    return pl.pallas_call(
        functools.partial(gram_kernel, offset, scale, counts),
        out_shape=jax.ShapeDtypeStruct((8, 128), jnp.float32),
        in_specs=[pl.BlockSpec(memory_space=pltpu.VMEM)] * len(operands),
        out_specs=pl.BlockSpec(memory_space=pltpu.VMEM),
        scratch_shapes=[pltpu.VMEM((count, norb, cz), jnp.float32)],
        compiler_params=pltpu.CompilerParams(vmem_limit_bytes=24 * 2**20),
        cost_estimate=pl.CostEstimate(flops=0, bytes_accessed=100, transcendentals=0),
        name="gram_rows",
    )(*operands)


def factor_table(gram, table_ref):
    norb = gram.shape[0]
    columns = [jnp.broadcast_to(gram[:, j : j + 1], (norb, 128)) for j in range(norb)]
    row = lax.broadcasted_iota(jnp.int32, (norb, 128), 0)
    for k in range(norb):
        scale = 1.0 / jnp.sqrt(columns[k][k : k + 1])
        column = columns[k] * scale
        table_ref[k] = jnp.where(row == k, scale, column)
        for j in range(k + 1, norb):
            top = 8 * (j // 8)
            fresh = columns[j][top:] - column[top:] * column[j : j + 1]
            columns[j] = fresh if top == 0 else jnp.concatenate([jnp.zeros((top, 128), jnp.float32), fresh], axis=0)


def solve_kernel(counts, recv_ref, *refs):
    norb = sum(counts)
    chunks, (out_ref, here_ref, table_ref, sems) = refs[: len(counts)], refs[len(counts) :]
    packed = jnp.sum(recv_ref[...], axis=0)
    rows = jnp.concatenate([packed] + [jnp.roll(packed, -norb * q, 1) for q in range(1, 4)], axis=0)
    factor_table(rows, table_ref)
    where = []
    for ref, count in zip(chunks, counts):
        for at in range(count):
            where.append((ref, at))
    block = 8
    cx = here_ref.shape[1]

    def copy_out(x):
        return pltpu.make_async_copy(here_ref.at[:, x], out_ref.at[:, x], sems.at[x])

    def layer(x, _):
        for i0 in range(0, norb, block):
            accs = [where[i0 + a][0][where[i0 + a][1], x] for a in range(block)]
            for j in range(i0):
                value = here_ref[j, x]
                for a in range(block):
                    accs[a] = accs[a] - table_ref[j, i0 + a : i0 + a + 1, :] * value
            for a in range(block):
                value = accs[a] * table_ref[i0 + a, i0 + a : i0 + a + 1, :]
                here_ref[i0 + a, x] = value
                for c in range(a + 1, block):
                    accs[c] = accs[c] - table_ref[i0 + a, i0 + c : i0 + c + 1, :] * value
        copy_out(x).start()
        return 0

    lax.fori_loop(0, cx, layer, 0)
    for x in range(cx):
        copy_out(x).wait()


def run_solve(received, chunks):
    counts = tuple(c.shape[0] for c in chunks)
    norb = sum(counts)
    _, cx, cy, cz = chunks[0].shape
    return pl.pallas_call(
        functools.partial(solve_kernel, counts),
        out_shape=jax.ShapeDtypeStruct((norb, cx, cy, cz), jnp.float32),
        in_specs=[pl.BlockSpec(memory_space=pltpu.VMEM)] * (1 + len(chunks)),
        out_specs=pl.BlockSpec(memory_space=pl.ANY),
        scratch_shapes=[
            pltpu.VMEM((norb, cx, cy, cz), jnp.float32),
            pltpu.VMEM((norb, norb, 128), jnp.float32),
            pltpu.SemaphoreType.DMA((cx,)),
        ],
        compiler_params=pltpu.CompilerParams(vmem_limit_bytes=24 * 2**20),
        name="orthonormalize",
    )(received, *chunks)


def body(orbitals, potential):
    norb, cx, cy, cz = orbitals.shape
    chips = axis_count(("gx", "gz"))
    scale = 1.0 / float(chips * CORES * cx * cy * cz)
    blocks = []
    first = first_tiles(orbitals, potential)
    for index, mid in enumerate(all_tiles(orbitals, potential)):
        lo, hi = both_ways(*((first, first) if index == 0 else (mid, mid)), "gx")
        blocks.append((lo, mid, hi))
    diag = None
    filtered, grams, all_sides, alone = [], [], [], {}
    for index, (chunk, start, groups) in enumerate(UNITS):
        unit = (start, groups, index == 0, index in RIDES or index in ALONE)
        if index in AFTER or index in ALONE:
            lo, mid, hi = blocks[chunk]
            tied = (lo, hi)
            if index in ALONE:
                part = mid[start * cx * cy :][: cx * cy].reshape((cx, cy) + mid.shape[1:])
                rows = [p.reshape((cx * HALO,) + p.shape[2:]) for p in (part[:, :HALO], part[:, cy - HALO :])]
                tied += both_ways(*rows, GY)
            size = len(tied)
            before = AFTER.get(index)
            if before is not None:
                tied += (filtered[before],) + ((grams[before],) if before == 0 else ())
            tied = lax.optimization_barrier(tied)
            lo, hi = tied[:2]
            if index in ALONE:
                alone[index] = tied[2:4]
            if before is not None:
                filtered[before], *rest = tied[size:]
                grams[before : before + len(rest)] = rest
            blocks[chunk] = lo, mid, hi
        rider, rider_mid = None, None
        for later, carrier in RIDES.items():
            if carrier == index:
                rider, rider_mid = UNITS[later][1:], blocks[UNITS[later][0]][1]
        low, high = pack_sides(blocks[chunk], unit, CHUNKS[chunk], cx, cy, rider, rider_mid)
        all_sides.append(both_ways(low, high, GY))
        own, own_at = None, 0
        if index in RIDES:
            carrier = RIDES[index]
            own = all_sides[carrier]
            own_at = unit_tiles(cx, UNITS[carrier][1:] + (carrier == 0, carrier in RIDES))
        if index in ALONE:
            own = alone[index]
        out, diag = run_filter(blocks[chunk], all_sides[index], unit, CHUNKS[chunk], own, own_at, cx, cy, cz, diag)
        offset = GROUP * sum(g for _, _, g in UNITS[:index])
        filtered.append(out)
        last = index + 1 == len(UNITS)
        grams.append(run_gram(filtered, grams if last else (), offset, norb, scale))
    local = grams[-1]
    other = lax.ppermute(local, "core", [(core, 1 - core) for core in range(CORES)])
    chip = jnp.broadcast_to((local + other)[None], (chips,) + local.shape)
    received = lax.all_to_all(chip, ("gx", "gz"), 0, 0, tiled=True)
    return run_solve(received, filtered)


def solution(mesh):
    count = mesh.shape["gx"], mesh.shape["gy"] // CORES, CORES
    split = jax.sharding.Mesh(mesh.devices.reshape(count), ("gx",) + GY)
    placed = (P(None, "gx", GY, None), P("gx", GY, None))
    return jax.shard_map(
        body, mesh=split, in_specs=placed, out_specs=P(None, "gx", GY, None), check_vma=False
    )
```
